128 devices in a mesh: dp: 16 (over x_hi, y, core), head: 8 (over z, x_lo).
Axes of the slice: x: 4 (x_hi: 2, x_lo: 2; x = x_hi * 2 + x_lo), y: 4, z: 4, core: 2. Of those that a mesh axis runs over, the one named last changes fastest.
Arguments:
- inputs: bfloat16 [16, 1024, 512], P('dp', 'head'), may hold values from -6 to 6
- cotangent: bfloat16 [16, 1024, 512], P('dp', 'head'), may hold values from -6 to 6
- qkv_weight: float32 [3, 512, 512], P(None, None, 'head'), may hold values from -0.25 to 0.25
- qkv_first: float32 [3, 512, 512], P(None, None, 'head'), may hold values from -16 to 16
- qkv_second: float32 [3, 512, 512], P(None, None, 'head'), may hold values from 0.65536 to 2.62144
- out_weight: float32 [512, 512], P('head'), may hold values from -0.75 to 0.75
- out_first: float32 [512, 512], P('head'), may hold values from -6 to 6
- out_second: float32 [512, 512], P('head'), may hold values from 0.2359296 to 0.9437184
- up_weight: float32 [512, 2048], P(None, 'head'), may hold values from -0.25 to 0.25
- up_first: float32 [512, 2048], P(None, 'head'), may hold values from -6 to 6
- up_second: float32 [512, 2048], P(None, 'head'), may hold values from 0.36864 to 1.47456
- down_weight: float32 [2048, 512], P('head'), may hold values from -0.125 to 0.125
- down_first: float32 [2048, 512], P('head'), may hold values from -24 to 24
- down_second: float32 [2048, 512], P('head'), may hold values from 1.47456 to 5.89824
- gate_weight: float32 [2, 512, 512], replicated, may hold values from -0.25 to 0.25
- gate_first: float32 [2, 512, 512], replicated, may hold values from -32 to 32
- gate_second: float32 [2, 512, 512], replicated, may hold values from 2.00704 to 8.02816
- norm_gains: float32 [2, 512], replicated, may hold values from 0.5 to 1.5
- gains_first: float32 [2, 512], replicated, may hold values from -40 to 40
- gains_second: float32 [2, 512], replicated, may hold values from 4.096 to 16.384
- biases: float32 [4, 512], replicated, may hold values from -4 to 4
- biases_first: float32 [4, 512], replicated, may hold values from -40 to 40
- biases_second: float32 [4, 512], replicated, may hold values from 4.096 to 16.384
Outputs:
- mixed: float32 [16, 1024, 512], P('dp', 'head')
- input_grad: float32 [16, 1024, 512], P('dp', 'head')
- new_qkv: float32 [3, 512, 512], P(None, None, 'head')
- new_qkv_first: float32 [3, 512, 512], P(None, None, 'head')
- new_qkv_second: float32 [3, 512, 512], P(None, None, 'head')
- new_out: float32 [512, 512], P('head')
- new_out_first: float32 [512, 512], P('head')
- new_out_second: float32 [512, 512], P('head')
- new_up: float32 [512, 2048], P(None, 'head')
- new_up_first: float32 [512, 2048], P(None, 'head')
- new_up_second: float32 [512, 2048], P(None, 'head')
- new_down: float32 [2048, 512], P('head')
- new_down_first: float32 [2048, 512], P('head')
- new_down_second: float32 [2048, 512], P('head')
- new_gate: float32 [2, 512, 512], replicated
- new_gate_first: float32 [2, 512, 512], replicated
- new_gate_second: float32 [2, 512, 512], replicated
- new_gains: float32 [2, 512], replicated
- new_gains_first: float32 [2, 512], replicated
- new_gains_second: float32 [2, 512], replicated
- new_biases: float32 [4, 512], replicated
- new_biases_first: float32 [4, 512], replicated
- new_biases_second: float32 [4, 512], replicated
The draws below stay inside these ranges and needn't reach their ends.
All inputs are finite; a program needn't handle non-finite values.
Results may differ from the reference program's by a relative error of at most 0.034.
Values may be sent and summed in bfloat16 or wider, within the bound.
A program may use at most 128 MiB of HBM per device.

```python
import math
import jax
import jax.numpy as jnp
from jax import lax

D = 512
HEADS = 8
HDIM = 64
FF = 2048
LEN = 1024
STEP = 10
SEQS = 16


def shard_levels(stream_key, shape, shards, low, high):
    factor_of, own = 1.0, jax.random.fold_in(stream_key, 6)
    for axis_at, parts in shards:
        draws = jnp.exp(jax.random.uniform(jax.random.fold_in(own, axis_at), (parts,), jnp.float32, low / len(shards), high / len(shards)))
        factor_of = factor_of * jnp.repeat(draws, shape[axis_at] // parts).reshape([-1 if axis == axis_at else 1 for axis in range(len(shape))])
    return factor_of


def gaussian(rng, dims, scale, bound, split=(), kind=jnp.bfloat16):
    drawn = scale * jax.random.normal(rng, dims, jnp.float32)
    if split:
        drawn = drawn * shard_levels(rng, dims, split, -0.22, 0.18)
    return jnp.clip(drawn, -bound, bound).astype(kind)


def setup_inputs(seed: int = 0) -> dict:
    streams_of = jax.random.split(jax.random.key(seed), 24)
    return {
        "inputs": gaussian(streams_of[0], (SEQS, LEN, D), 1.0, 6.0, ((0, 16), (1, 8))),
        "cotangent": gaussian(streams_of[1], (SEQS, LEN, D), 1.0, 6.0, ((0, 16), (1, 8))),
        "qkv_weight": gaussian(streams_of[2], (3, D, D), D ** -0.5, 0.25, ((2, 8),), jnp.float32),
        "qkv_first": gaussian(streams_of[3], (3, D, D), (0.111 * 0.2 * (SEQS * LEN) ** 0.5), 16.0, ((2, 8),), jnp.float32),
        "qkv_second": jnp.clip(jnp.exp(math.log(2.62144) - 1.3862944 * jax.random.uniform(streams_of[4], (3, D, D), jnp.float32) ** shard_levels(streams_of[4], (3, D, D), ((2, 8),), -0.2, 0.2)), 0.65536, 2.62144),
        "out_weight": gaussian(streams_of[5], (D, D), (D // 8) ** -0.5, 0.75, ((0, 8),), jnp.float32),
        "out_first": gaussian(streams_of[6], (D, D), (0.111 * 0.12 * (SEQS * LEN) ** 0.5), 6.0, ((0, 8),), jnp.float32),
        "out_second": jnp.clip(jnp.exp(math.log(0.9437184) - 1.3862944 * jax.random.uniform(streams_of[7], (D, D), jnp.float32) ** shard_levels(streams_of[7], (D, D), ((0, 8),), -0.2, 0.2)), 0.2359296, 0.9437184),
        "up_weight": gaussian(streams_of[8], (D, FF), D ** -0.5, 0.25, ((1, 8),), jnp.float32),
        "up_first": gaussian(streams_of[9], (D, FF), (0.111 * 0.15 * (SEQS * LEN) ** 0.5), 6.0, ((1, 8),), jnp.float32),
        "up_second": jnp.clip(jnp.exp(math.log(1.47456) - 1.3862944 * jax.random.uniform(streams_of[10], (D, FF), jnp.float32) ** shard_levels(streams_of[10], (D, FF), ((1, 8),), -0.2, 0.2)), 0.36864, 1.47456),
        "down_weight": gaussian(streams_of[11], (FF, D), FF ** -0.5, 0.125, ((0, 8),), jnp.float32),
        "down_first": gaussian(streams_of[12], (FF, D), (0.111 * 0.3 * (SEQS * LEN) ** 0.5), 24.0, ((0, 8),), jnp.float32),
        "down_second": jnp.clip(jnp.exp(math.log(5.89824) - 1.3862944 * jax.random.uniform(streams_of[13], (FF, D), jnp.float32) ** shard_levels(streams_of[13], (FF, D), ((0, 8),), -0.2, 0.2)), 1.47456, 5.89824),
        "gate_weight": gaussian(streams_of[14], (2, D, D), D ** -0.5, 0.25, (), jnp.float32),
        "gate_first": gaussian(streams_of[15], (2, D, D), (0.111 * 0.35 * (SEQS * LEN) ** 0.5), 32.0, (), jnp.float32),
        "gate_second": jnp.clip(jnp.exp(jax.random.uniform(streams_of[16], (2, D, D), jnp.float32, math.log(2.00704), math.log(8.02816))), 2.00704, 8.02816),
        "norm_gains": jnp.clip(1.0 + 0.1 * jax.random.normal(streams_of[17], (2, D), jnp.float32), 0.5, 1.5),
        "gains_first": gaussian(streams_of[18], (2, D), (0.111 * 0.5 * (SEQS * LEN) ** 0.5), 40.0, (), jnp.float32),
        "gains_second": jnp.clip(jnp.exp(jax.random.uniform(streams_of[19], (2, D), jnp.float32, math.log(4.096), math.log(16.384))), 4.096, 16.384),
        "biases": gaussian(streams_of[20], (4, D), 0.3, 4.0, (), jnp.float32),
        "biases_first": gaussian(streams_of[21], (4, D), (0.111 * 0.5 * (SEQS * LEN) ** 0.5), 40.0, (), jnp.float32),
        "biases_second": jnp.clip(jnp.exp(jax.random.uniform(streams_of[22], (4, D), jnp.float32, math.log(4.096), math.log(16.384))), 4.096, 16.384),
    }


@jax.custom_vjp
def low(v):
    return lax.optimization_barrier(v.astype(jnp.bfloat16)).astype(jnp.float32)

@jax.custom_vjp
def low_back(v):
    return v

def low_keep(v):
    return (low(v), None)

def low_pass(kept, grad):
    return (grad,)

def back_keep(v):
    return (v, None)

def back_low(kept, grad):
    return (low(grad),)
low.defvjp(low_keep, low_pass)
low_back.defvjp(back_keep, back_low)
HIGH = lax.Precision.HIGHEST
NORM_EPS = 1e-05
BETA_ONE = 0.9
BETA_TWO = 0.999
ADAM_EPS = 1e-08
DECAY = 0.01
RATES = (0.04, 0.1, 0.04, 0.02, 0.04, 0.4, 0.3)

def rounded_both(value):
    return low_back(low(value))

def norm_layer(value, gain, shift):
    center = value - lax.optimization_barrier(jnp.mean(value, axis=-1, keepdims=True))
    spread = lax.optimization_barrier(jnp.mean(center * center, axis=-1, keepdims=True))
    return center * lax.rsqrt(spread + NORM_EPS) * gain + shift

def attend_sequence(query, keys, values):
    length = query.shape[0]
    block = min(512, length)
    scale = 1.0 / math.sqrt(HDIM)
    columns = jnp.arange(length).astype(jnp.int32)

    def block_rows(start):
        rows_query = lax.dynamic_slice_in_dim(query, start, block, 0)
        scores = jnp.einsum('qhe,khe->hqk', rows_query, keys, precision=HIGH) * scale
        scores = low_back(scores)
        positions = start + jnp.arange(block).astype(jnp.int32)
        keep = columns[None, :] <= positions[:, None]
        scores = jnp.where(keep[None], scores, -1e+30)
        weights = low(jax.nn.softmax(scores, axis=-1))
        return jnp.einsum('hqk,khe->qhe', weights, values, precision=HIGH)
    starts = (jnp.arange(length // block) * block).astype(jnp.int32)
    pieces = lax.map(jax.checkpoint(block_rows), starts)
    return pieces.reshape(length, HEADS, HDIM)

def layer(xf, qkv, outw, upw, downw, gatew, gains, biases):
    group, length, width = xf.shape
    h1 = low(norm_layer(xf, gains[0], biases[0]))
    proj = rounded_both(jnp.einsum('bld,jde->jble', h1, low(qkv), precision=HIGH))
    query = proj[0].reshape(group, length, HEADS, HDIM)
    keys = proj[1].reshape(group, length, HEADS, HDIM)
    values = proj[2].reshape(group, length, HEADS, HDIM)
    heads_out = jax.vmap(attend_sequence)(query, keys, values)
    heads_out = rounded_both(heads_out.reshape(group, length, width))
    attn = low_back(jnp.einsum('bld,de->ble', heads_out, low(outw), precision=HIGH))
    gate_one = jax.nn.sigmoid(low_back(jnp.einsum('bld,de->ble', h1, low(gatew[0]), precision=HIGH) + biases[2]))
    mid = gate_one * attn + (1.0 - gate_one) * xf
    h2 = low(norm_layer(mid, gains[1], biases[1]))
    hidden = low_back(jnp.einsum('bld,df->blf', h2, low(upw), precision=HIGH))
    active = low(jax.nn.gelu(hidden))
    ffn = low_back(jnp.einsum('blf,fd->bld', active, low(downw), precision=HIGH))
    gate_two = jax.nn.sigmoid(low_back(jnp.einsum('bld,de->ble', h2, low(gatew[1]), precision=HIGH) + biases[3]))
    return gate_two * ffn + (1.0 - gate_two) * mid

def adamw(weight, first, second, grad, rate):
    first = BETA_ONE * first + (1.0 - BETA_ONE) * grad
    second = BETA_TWO * second + (1.0 - BETA_TWO) * grad * grad
    first_hat = first / (1.0 - BETA_ONE ** STEP)
    second_hat = second / (1.0 - BETA_TWO ** STEP)
    weight = weight - rate * (first_hat / (jnp.sqrt(second_hat) + ADAM_EPS) + DECAY * weight)
    return (weight, first, second)

def reference(inputs, cotangent, qkv_weight, qkv_first, qkv_second, out_weight, out_first, out_second, up_weight, up_first, up_second, down_weight, down_first, down_second, gate_weight, gate_first, gate_second, norm_gains, gains_first, gains_second, biases, biases_first, biases_second):
    group = 4 if SEQS % 4 == 0 else 1
    xs = inputs.astype(jnp.float32).reshape(SEQS // group, group, LEN, D)
    cs = cotangent.astype(jnp.float32).reshape(SEQS // group, group, LEN, D)
    params = (qkv_weight, out_weight, up_weight, down_weight, gate_weight, norm_gains, biases)

    def scan_step(total, pair):
        xg, cg = pair
        result, pull = jax.vjp(layer, xg, *params)
        grads = pull(cg)
        total = jax.tree.map(jnp.add, total, tuple(grads[1:]))
        return (total, (result, grads[0]))
    zero = tuple((jnp.zeros_like(p) for p in params))
    total, (results, input_grads) = lax.scan(scan_step, zero, (xs, cs))
    mixed = results.reshape(SEQS, LEN, D)
    input_grad = input_grads.reshape(SEQS, LEN, D)
    firsts = (qkv_first, out_first, up_first, down_first, gate_first, gains_first, biases_first)
    seconds = (qkv_second, out_second, up_second, down_second, gate_second, gains_second, biases_second)
    updated = [adamw(params[i], firsts[i], seconds[i], total[i], RATES[i]) for i in range(7)]
    return (mixed, input_grad, updated[0][0], updated[0][1], updated[0][2], updated[1][0], updated[1][1], updated[1][2], updated[2][0], updated[2][1], updated[2][2], updated[3][0], updated[3][1], updated[3][2], updated[4][0], updated[4][1], updated[4][2], updated[5][0], updated[5][1], updated[5][2], updated[6][0], updated[6][1], updated[6][2])
```

```python
import jax
import jax.numpy as jnp
from jax import lax
from jax.experimental import pallas as pl
from jax.experimental.pallas import tpu as pltpu
from jax.sharding import PartitionSpec as P

F32 = jnp.float32
BF16 = jnp.bfloat16
STEP = 10
NORM_EPS = 1e-05
BETA_ONE = 0.9
BETA_TWO = 0.999
ADAM_EPS = 1e-08
DECAY = 0.01
RATES = (0.04, 0.1, 0.04, 0.02, 0.04, 0.4, 0.3)
D = 512
ROWS = 128
LEN = 1024
QB = 256
NN = ((1,), (0,))
NT = ((1,), (1,))
TN = ((0,), (0,))


def dot(a, b, dims=NN):
    return lax.dot_general(a, b, (dims, ((), ())), preferred_element_type=F32)


def aligned(value, by):
    return pl.multiple_of(value, by)


class Links:
    def __init__(self, send_sems, recv_sems):
        self.send_sems, self.recv_sems, self.used, self.sent = send_sems, recv_sems, 0, []

    def start(self, src, dst, device):
        copy = pltpu.make_async_remote_copy(
            src_ref=src,
            dst_ref=dst,
            send_sem=self.send_sems.at[self.used],
            recv_sem=self.recv_sems.at[self.used],
            device_id=device,
            device_id_type=pl.DeviceIdType.MESH,
        )
        self.used += 1
        copy.start()
        self.sent.append(copy)
        return copy

    def drain(self):
        for copy in self.sent:
            copy.wait_send()


N_SEMS = 240


def layer_kernel(
    x_ref,
    dy_ref,
    qkv_ref,
    out_ref,
    up_ref,
    down_ref,
    gate_ref,
    gains_ref,
    biases_ref,
    mixed_ref,
    ingrad_ref,
    o_qkv_ref,
    o_out_ref,
    o_up_ref,
    o_down_ref,
    o_gate_ref,
    o_vec_ref,
    x_all,
    h1_all,
    w_all,
    out_all,
    up_all,
    down_all,
    gate_low,
    proj_t,
    k_nat,
    v_nat,
    s_buf,
    p_buf,
    ds_buf,
    o_t,
    o_low,
    lse,
    heads_t,
    g1_buf,
    attn_buf,
    x1_buf,
    xhat_buf,
    rstd_buf,
    h1_pair,
    h2_pair,
    g2_buf,
    act_buf,
    dgelu_buf,
    ffn_own,
    ffn_send,
    ffn_recv,
    dffn_pair,
    dz2_full,
    dz1_full,
    dattn_full,
    dz2_half,
    dz1_half,
    dattn_half,
    dhid_buf,
    dh2_own,
    dh2_send,
    dh2_recv,
    dh2_gate,
    dheads_t,
    do_t,
    vec,
    vec_a,
    vec_b,
    dq_t,
    dk_t,
    dv_t,
    dproj_low,
    dproj_all,
    gq_send,
    gq_recv,
    gq_all,
    su1,
    ru1,
    su2,
    ru2,
    su3,
    ru3,
    sd1,
    rd1,
    sd2,
    rd2,
    sd3,
    rd3,
    sg1,
    rg1,
    sg2,
    rg2,
    sg3,
    rg3,
    gout_all,
    gup_all,
    gdown_all,
    ggate_all,
    send_sems,
    recv_sems,
):
    dp, head = lax.axis_index("dp"), lax.axis_index("head")
    x_hi, y, core = dp // 8, (dp // 2) % 4, dp % 2
    z, x_lo = head // 2, head % 2
    xx = x_hi * 2 + x_lo
    sub = x_hi * 4 + y
    sibling = (x_hi * 8 + y * 2 + (1 - core), head)
    links = Links(send_sems, recv_sems)

    def head_peer(o):
        return (head + o) % 8

    def head_from(o):
        return (head + 8 - o) % 8

    def dp_peer(o):
        return (dp + o) % 16

    def dp_from(o):
        return (dp + 16 - o) % 16

    def ring(axis, o):
        nx = (xx + o) % 4 if axis == "x" else xx
        ny = (y + o) % 4 if axis == "y" else y
        nz = (z + o) % 4 if axis == "z" else z
        return ((nx // 2) * 8 + ny * 2 + core, nz * 2 + nx % 2)

    barrier = pltpu.get_barrier_semaphore()
    greeted = [(dp, head_peer(o)) for o in range(1, 8)]
    greeted += [(dp_peer(o), head) for o in range(1, 16)]
    greeted += [((1 - x_hi) * 8 + y * 2 + core, z * 2 + 1 - x_lo)]
    for device in greeted:
        pl.semaphore_signal(
            barrier, inc=1, device_id=device, device_id_type=pl.DeviceIdType.MESH
        )

    own = pl.ds(aligned(head * ROWS, ROWS), ROWS)
    own_core = pl.ds(aligned(core * ROWS, ROWS), ROWS)
    sib_core = pl.ds(aligned((1 - core) * ROWS, ROWS), ROWS)

    x_all[own, :] = x_ref[...]
    own_w = pl.ds(aligned(head * 192, 64), 192)
    for j in range(3):
        w_all[pl.ds(aligned(head * 192 + j * 64, 64), 64), :] = qkv_ref[j].T.astype(BF16)
    own_out = pl.ds(aligned(head * 64, 64), 64)
    out_all[own_out, :] = out_ref[...].astype(BF16)
    up_all[:, own] = up_ref[:, own_core].astype(BF16)
    down_all[own, :] = down_ref[own_core, :].astype(BF16)

    pl.semaphore_wait(barrier, len(greeted))

    x_copies = [
        links.start(x_ref, x_all.at[own, :], (dp, head_peer(o))) for o in range(1, 8)
    ]

    gate_low[...] = gate_ref[...].astype(BF16)
    gain_one, shift_one = gains_ref[0:1, :], biases_ref[0:1, :]
    gain_two, shift_two = gains_ref[1:2, :], biases_ref[1:2, :]

    def project(block):
        for s in range(4):
            rows = pl.ds(aligned(block * ROWS + 32 * s, 32), 32)
            v = x_all[rows, :].astype(F32)
            center = v - jnp.mean(v, axis=-1, keepdims=True)
            spread = jnp.mean(center * center, axis=-1, keepdims=True)
            h = center * lax.rsqrt(spread + NORM_EPS) * gain_one + shift_one
            h1_all[rows, :] = h.astype(BF16)
        rows = pl.ds(aligned(block * ROWS, ROWS), ROWS)
        pt = dot(w_all[own_w, :], h1_all[rows, :], NT)
        proj_t[0:64, rows] = (pt[0:64].astype(BF16).astype(F32) * 0.125).astype(BF16)
        proj_t[64:192, rows] = pt[64:192].astype(BF16)
        k_nat[rows, :] = pt[64:128].T.astype(BF16)
        v_nat[rows, :] = pt[128:192].T.astype(BF16)

    project(head)
    for o in range(1, 8):
        x_copies[o - 1].wait_recv()
        project(head_from(o))

    weight_copies = []
    for o in range(1, 8):
        to = (dp, head_peer(o))
        weight_copies.append(links.start(out_all.at[own_out, :], out_all.at[own_out, :], to))
    for o in range(1, 8):
        to = (dp, head_peer(o))
        weight_copies.append(links.start(up_all.at[:, own], up_all.at[:, own], to))
    for o in range(1, 8):
        to = (dp, head_peer(o))
        weight_copies.append(links.start(down_all.at[own, :], down_all.at[own, :], to))
    for o in range(1, 8):
        to = (dp, head_peer(o))
        weight_copies.append(links.start(w_all.at[own_w, :], w_all.at[own_w, :], to))

    h1_pair[own_core, :] = h1_all[own, :]
    h1_copy = links.start(h1_pair.at[own_core, :], h1_pair.at[own_core, :], sibling)

    for j in range(LEN // QB):
        cols = slice(QB * j, QB * (j + 1))
        queries = proj_t[0:64, cols]
        ceiling = jnp.full((1, QB), -1e30, F32)
        tiles = QB * (j + 1) // ROWS
        for t in range(tiles):
            s = dot(k_nat[ROWS * t : ROWS * (t + 1), :], queries)
            if ROWS * t >= QB * j:
                keys_at = lax.broadcasted_iota(jnp.int32, (ROWS, QB), 0) + ROWS * t
                queries_at = lax.broadcasted_iota(jnp.int32, (ROWS, QB), 1) + QB * j
                s = jnp.where(keys_at <= queries_at, s, -1e30)
            s_buf[ROWS * t : ROWS * (t + 1), :] = s
            ceiling = jnp.maximum(ceiling, jnp.max(s, axis=0, keepdims=True))
        mass = jnp.zeros((1, QB), F32)
        for t in range(tiles):
            e = jnp.exp(s_buf[ROWS * t : ROWS * (t + 1), :] - ceiling)
            mass = mass + jnp.sum(e, axis=0, keepdims=True)
            p_buf[ROWS * t : ROWS * (t + 1), :] = e.astype(BF16)
        total = dot(proj_t[128:192, 0 : QB * (j + 1)], p_buf[0 : QB * (j + 1), :])
        total = total / mass
        o_t[:, cols] = total
        o_low[:, cols] = total.astype(BF16)
        lse[:, cols] = ceiling + jnp.log(mass)

    own_heads = pl.ds(aligned(head * 64, 64), 64)
    heads_copies = []
    for o in range(1, 8):
        peer = head_peer(o)
        block = o_low.at[:, pl.ds(aligned(peer * ROWS, ROWS), ROWS)]
        heads_copies.append(links.start(block, heads_t.at[own_heads, own_core], (dp, peer)))
    heads_t[own_heads, own_core] = o_low[:, own]

    h1_own = h1_all[own, :]
    g1_buf[...] = dot(h1_own, gate_low[0]) + biases_ref[2:3, :]
    for c in heads_copies:
        c.wait_recv()
    headst_copy = links.start(heads_t.at[:, own_core], heads_t.at[:, own_core], sibling)
    for c in weight_copies[0:7]:
        c.wait_recv()
    attn_buf[...] = dot(heads_t[:, own_core], out_all[...], TN)
    for s in range(4):
        rows = slice(32 * s, 32 * s + 32)
        g1 = jax.nn.sigmoid(g1_buf[rows, :])
        g1_buf[rows, :] = g1
        x = x_ref[rows, :].astype(F32)
        x1 = g1 * attn_buf[rows, :] + (1.0 - g1) * x
        x1_buf[rows, :] = x1
        center = x1 - jnp.mean(x1, axis=-1, keepdims=True)
        spread = jnp.mean(center * center, axis=-1, keepdims=True)
        rstd = lax.rsqrt(spread + NORM_EPS)
        xhat = center * rstd
        xhat_buf[rows, :] = xhat
        rstd_buf[rows, :] = jnp.broadcast_to(rstd, (32, 128))
        h2 = xhat * gain_two + shift_two
        h2_pair[pl.ds(aligned(core * ROWS + 32 * s, 32), 32), :] = h2.astype(BF16)
    h2_copy = links.start(h2_pair.at[own_core, :], h2_pair.at[own_core, :], sibling)
    g2_buf[...] = dot(h2_pair[own_core, :], gate_low[1]) + biases_ref[3:4, :]
    for c in weight_copies[7:14]:
        c.wait_recv()
    h2_copy.wait_recv()
    for n in range(4):
        cols = slice(256 * n, 256 * n + 256)
        u = dot(h2_pair[...], up_all[:, cols])
        c0 = 0.7978845608028654
        inner = jnp.tanh(c0 * (u + 0.044715 * u * u * u))
        act_buf[:, cols] = (0.5 * u * (1.0 + inner)).astype(BF16)
        dgelu_buf[:, cols] = 0.5 * (1.0 + inner) + 0.5 * u * (1.0 - inner * inner) * c0 * (
            1.0 + 3.0 * 0.044715 * u * u
        )
    for c in weight_copies[14:21]:
        c.wait_recv()
    ffn_send[...] = dot(act_buf[sib_core, :], down_all[...]).astype(BF16)
    ffn_copy = links.start(ffn_send, ffn_recv, sibling)
    ffn_own[...] = dot(act_buf[own_core, :], down_all[...])
    ffn_copy.wait_recv()
    bias_two = jnp.zeros((1, D), F32)
    for s in range(4):
        rows = slice(32 * s, 32 * s + 32)
        ffn = ffn_own[rows, :] + ffn_recv[rows, :].astype(F32)
        g2 = jax.nn.sigmoid(g2_buf[rows, :])
        g2_buf[rows, :] = g2
        x1 = x1_buf[rows, :]
        dy = dy_ref[rows, :].astype(F32)
        mixed_ref[rows, :] = g2 * ffn + (1.0 - g2) * x1
        dffn_pair[pl.ds(aligned(core * ROWS + 32 * s, 32), 32), :] = (g2 * dy).astype(BF16)
        dz = (dy * (ffn - x1) * g2 * (1.0 - g2)).astype(BF16)
        dz2_full[rows, :] = dz
        bias_two = bias_two + jnp.sum(dz.astype(F32), axis=0, keepdims=True)
    dffn_copy = links.start(dffn_pair.at[own_core, :], dffn_pair.at[own_core, :], sibling)
    half = pl.ds(aligned(core * 256, 256), 256)
    sib_half = pl.ds(aligned((1 - core) * 256, 256), 256)
    dz2_half[own_core, :] = dz2_full[:, half]
    dz2_copy = links.start(dz2_full.at[:, sib_half], dz2_half.at[own_core, :], sibling)
    dh2_gate[...] = dot(dz2_full[...], gate_low[1], NT)
    dffn_copy.wait_recv()
    for n in range(4):
        cols = slice(256 * n, 256 * n + 256)
        da = dot(dffn_pair[...], down_all[cols, :], NT)
        dhid_buf[:, cols] = (da * dgelu_buf[:, cols]).astype(BF16)
    dh2_send[...] = dot(dhid_buf[sib_core, :], up_all[...], NT).astype(BF16)
    dh2_copy = links.start(dh2_send, dh2_recv, sibling)
    dh2_own[...] = dot(dhid_buf[own_core, :], up_all[...], NT)
    dh2_copy.wait_recv()
    gain_sum = jnp.zeros((1, D), F32)
    shift_sum = jnp.zeros((1, D), F32)
    bias_one = jnp.zeros((1, D), F32)
    for s in range(4):
        rows = slice(32 * s, 32 * s + 32)
        dh2 = dh2_own[rows, :] + dh2_recv[rows, :].astype(F32) + dh2_gate[rows, :]
        xhat = xhat_buf[rows, :]
        gain_sum = gain_sum + jnp.sum(dh2 * xhat, axis=0, keepdims=True)
        shift_sum = shift_sum + jnp.sum(dh2, axis=0, keepdims=True)
        dxhat = dh2 * gain_two
        mean_a = jnp.mean(dxhat, axis=-1, keepdims=True)
        mean_b = jnp.mean(dxhat * xhat, axis=-1, keepdims=True)
        rstd = rstd_buf[rows, 0:1]
        dx1 = (1.0 - g2_buf[rows, :]) * dy_ref[rows, :].astype(F32) + rstd * (
            dxhat - mean_a - xhat * mean_b
        )
        g1 = g1_buf[rows, :]
        dattn_full[rows, :] = (g1 * dx1).astype(BF16)
        x = x_ref[rows, :].astype(F32)
        dz = (dx1 * (attn_buf[rows, :] - x) * g1 * (1.0 - g1)).astype(BF16)
        dz1_full[rows, :] = dz
        bias_one = bias_one + jnp.sum(dz.astype(F32), axis=0, keepdims=True)
        ingrad_ref[rows, :] = (1.0 - g1) * dx1
    vec[1:2, :] = gain_sum
    vec[3:4, :] = shift_sum
    vec[4:5, :] = bias_one
    vec[5:6, :] = bias_two
    vec[6:8, :] = jnp.zeros((2, D), F32)

    dheads_t[...] = dot(out_all[...], dattn_full[...], NT).astype(BF16)
    dheads_copies = []
    for o in range(1, 8):
        peer = head_peer(o)
        block = dheads_t.at[pl.ds(aligned(peer * 64, 64), 64), :]
        dheads_copies.append(links.start(block, do_t.at[:, own], (dp, peer)))
    do_t[:, own] = dheads_t[own_heads, :]
    dz1_half[own_core, :] = dz1_full[:, half]
    dz1_copy = links.start(dz1_full.at[:, sib_half], dz1_half.at[own_core, :], sibling)
    dattn_half[own_core, :] = dattn_full[:, half]
    dattn_copy = links.start(dattn_full.at[:, sib_half], dattn_half.at[own_core, :], sibling)

    for h in range(8):
        cols = slice(128 * h, 128 * h + 128)
        gu = dot(h2_pair[...], dhid_buf[:, cols], TN).astype(BF16)
        gd = dot(act_buf[:, cols], dffn_pair[...], TN).astype(BF16)
        for g in range(8):
            ch_x, ch_y, ch_z = (g // 4) * 2 + h % 2, g % 4, h // 2
            su1[ch_z * 16 + ch_y * 4 + ch_x] = gu[64 * g : 64 * g + 64, :]
            sd1[ch_y * 16 + ch_x * 4 + ch_z] = gd[16 * g : 16 * g + 16, :]

    def stage(axis, at, src, dst, size):
        copies = []
        for o in range(1, 4):
            t = (at + o) % 4
            copies.append(
                links.start(
                    src.at[pl.ds(t * size, size)],
                    dst.at[pl.ds((o - 1) * size, size)],
                    ring(axis, o),
                )
            )
        return copies

    def gather(copies, at, src, got, size, store):
        for c in copies:
            c.wait_recv()

        def add(i, carry):
            total = src[at * size + i].astype(F32)
            for o in range(3):
                total = total + got[o * size + i].astype(F32)
            store(i, total)
            return carry

        lax.fori_loop(0, size, add, 0)

    up_copies = stage("z", z, su1, ru1, 16)
    down_copies = stage("y", y, sd1, rd1, 16)

    for c in (h1_copy, headst_copy, dz2_copy, dz1_copy, dattn_copy):
        c.wait_recv()
    gates = (
        dot(h1_pair[...], dz1_half[...], TN).astype(BF16),
        dot(h2_pair[...], dz2_half[...], TN).astype(BF16),
    )
    go = dot(heads_t[...], dattn_half[...]).astype(BF16)
    for h in range(8):
        for g in range(8):
            ch = ((g // 4) * 2 + h % 2) * 16 + (h // 2) * 4 + g % 4
            q = 16 * (8 * h + g)
            sg1[ch, :, 0:256] = gates[q // 512][q % 512 : q % 512 + 16, :]
            r = 64 * h + 16 * (g % 4)
            sg1[ch, :, 256:384] = go[r : r + 16, 128 * (g // 4) : 128 * (g // 4) + 128]
    gate_copies = stage("x", xx, sg1, rg1, 16)

    for c in dheads_copies:
        c.wait_recv()
    dk_t[...] = jnp.zeros_like(dk_t)
    dv_t[...] = jnp.zeros_like(dv_t)
    for j in range(LEN // QB):
        cols = slice(QB * j, QB * (j + 1))
        upto = QB * (j + 1)
        queries = proj_t[0:64, cols]
        grads = do_t[:, cols]
        delta = jnp.sum(o_t[:, cols] * grads.astype(F32), axis=0, keepdims=True)
        row_lse = lse[:, cols]
        for t in range(upto // ROWS):
            keys = slice(ROWS * t, ROWS * (t + 1))
            p = jnp.exp(dot(k_nat[keys, :], queries) - row_lse)
            if ROWS * t >= QB * j:
                keys_at = lax.broadcasted_iota(jnp.int32, (ROWS, QB), 0) + ROWS * t
                queries_at = lax.broadcasted_iota(jnp.int32, (ROWS, QB), 1) + QB * j
                p = jnp.where(keys_at <= queries_at, p, 0.0)
            d = dot(v_nat[keys, :], grads)
            p_buf[keys, :] = p.astype(BF16)
            ds_buf[keys, :] = (p * (d - delta)).astype(BF16)
        dq_t[:, cols] = dot(proj_t[64:128, 0:upto], ds_buf[0:upto, :]) * 0.125
        dk_t[:, 0:upto] += dot(queries, ds_buf[0:upto, :], NT)
        dv_t[:, 0:upto] += dot(grads, p_buf[0:upto, :], NT)
    dproj_low[0:64, :] = dq_t[...].astype(BF16)
    dproj_low[64:128, :] = dk_t[...].astype(BF16)
    dproj_low[128:192, :] = dv_t[...].astype(BF16)

    dproj_copies = []
    for o in range(1, 8):
        peer = head_peer(o)
        block = dproj_low.at[:, pl.ds(aligned(peer * ROWS, ROWS), ROWS)]
        dproj_copies.append(links.start(block, dproj_all.at[own_w, :], (dp, peer)))
    dproj_all[own_w, :] = dproj_low[:, own]

    gq = dot(dproj_low[...], h1_all[...]).astype(BF16)
    for i in range(16):
        r, c = 48 * (i // 4), 128 * (i % 4)
        gq_send[i] = gq[r : r + 48, c : c + 128]
    gq_copies = []
    for o in range(1, 16):
        peer = dp_peer(o)
        gq_copies.append(links.start(gq_send.at[peer], gq_recv.at[o - 1], (peer, head)))

    def to_bf16(ref):
        def store(i, total):
            ref[i] = total.astype(BF16)

        return store

    gather(up_copies, z, su1, ru1, 16, to_bf16(su2))
    up_copies = stage("y", y, su2, ru2, 4)
    gather(down_copies, y, sd1, rd1, 16, to_bf16(sd2))
    down_copies = stage("x", xx, sd2, rd2, 4)
    gather(gate_copies, xx, sg1, rg1, 16, to_bf16(sg2))
    gate_copies = stage("z", z, sg2, rg2, 4)

    for c in dproj_copies:
        c.wait_recv()
    for c in weight_copies[21:28]:
        c.wait_recv()
    dh2_own[...] = dot(dproj_all[...], w_all[...], TN) + dot(dz1_full[...], gate_low[0], NT)
    gain_sum = jnp.zeros((1, D), F32)
    shift_sum = jnp.zeros((1, D), F32)
    for s in range(4):
        rows = slice(32 * s, 32 * s + 32)
        v = x_ref[rows, :].astype(F32)
        center = v - jnp.mean(v, axis=-1, keepdims=True)
        spread = jnp.mean(center * center, axis=-1, keepdims=True)
        rstd = lax.rsqrt(spread + NORM_EPS)
        xhat = center * rstd
        dh = dh2_own[rows, :]
        gain_sum = gain_sum + jnp.sum(dh * xhat, axis=0, keepdims=True)
        shift_sum = shift_sum + jnp.sum(dh, axis=0, keepdims=True)
        dxhat = dh * gain_one
        mean_a = jnp.mean(dxhat, axis=-1, keepdims=True)
        mean_b = jnp.mean(dxhat * xhat, axis=-1, keepdims=True)
        ingrad_ref[rows, :] += rstd * (dxhat - mean_a - xhat * mean_b)
    vec[0:1, :] = gain_sum
    vec[2:3, :] = shift_sum
    vec_copies = [
        links.start(vec, vec_a.at[o - 1], (dp, head_peer(o))) for o in range(1, 8)
    ]

    for c in gq_copies:
        c.wait_recv()
    total = gq_send[dp].astype(F32)
    for o in range(15):
        total = total + gq_recv[o].astype(F32)
    gq_rows = pl.ds(aligned((dp // 4) * 48, 48), 48)
    gq_cols = pl.ds(aligned((dp % 4) * 128, 128), 128)
    gq_all[gq_rows, gq_cols] = total.astype(BF16)
    gq_copies = []
    for o in range(1, 16):
        block = gq_all.at[gq_rows, gq_cols]
        gq_copies.append(links.start(block, block, (dp_peer(o), head)))

    gather(up_copies, y, su2, ru2, 4, to_bf16(su3))
    up_copies = stage("x", xx, su3, ru3, 1)
    gather(down_copies, xx, sd2, rd2, 4, to_bf16(sd3))
    down_copies = stage("z", z, sd3, rd3, 1)
    gather(gate_copies, z, sg2, rg2, 4, to_bf16(sg3))
    gate_copies = stage("y", y, sg3, rg3, 1)

    for c in vec_copies:
        c.wait_recv()
    total = vec[...]
    for o in range(7):
        total = total + vec_a[o]
    vec_b[15] = total
    vec_copies = [
        links.start(vec_b.at[15], vec_b.at[o - 1], (dp_peer(o), head)) for o in range(1, 16)
    ]

    up_rows = pl.ds(aligned(sub * 64, 64), 64)
    down_rows = pl.ds(aligned(core * 128 + sub * 16, 16), 16)
    out_rows = pl.ds(aligned(y * 16, 16), 16)
    out_cols = pl.ds(aligned(core * 256 + x_hi * 128, 128), 128)
    gate_rows = pl.ds(aligned(head * 128 + sub * 16, 16), 16)

    def store_up(i, total):
        gup_all[up_rows, own_core] = total.astype(BF16)

    def store_down(i, total):
        gdown_all[down_rows, :] = total.astype(BF16)

    def store_gate(i, total):
        ggate_all[gate_rows, half] = total[:, 0:256].astype(BF16)
        gout_all[out_rows, out_cols] = total[:, 256:384].astype(BF16)

    last_copies, gate_gather = [], []
    gather(gate_copies, y, sg3, rg3, 1, store_gate)
    for o in range(1, 16):
        to = (dp_peer(o), head)
        block = ggate_all.at[gate_rows, half]
        gate_gather.append(links.start(block, block, to))
    for o in range(1, 16):
        to = (dp_peer(o), head)
        block = gout_all.at[out_rows, out_cols]
        last_copies.append(links.start(block, block, to))
    gather(up_copies, xx, su3, ru3, 1, store_up)
    for o in range(1, 16):
        to = (dp_peer(o), head)
        block = gup_all.at[up_rows, own_core]
        last_copies.append(links.start(block, block, to))
    gather(down_copies, z, sd3, rd3, 1, store_down)
    for o in range(1, 16):
        to = (dp_peer(o), head)
        block = gdown_all.at[down_rows, :]
        last_copies.append(links.start(block, block, to))
    for c in gate_gather:
        c.wait_recv()
    block = ggate_all.at[own, :]
    for o in range(1, 8):
        last_copies.append(links.start(block, block, (dp, head_peer(o))))

    for c in vec_copies:
        c.wait_recv()
    total = vec_b[15]
    for o in range(15):
        total = total + vec_b[o]
    o_vec_ref[...] = total
    for c in gq_copies + last_copies:
        c.wait_recv()
    o_qkv_ref[...] = gq_all[...]
    o_out_ref[...] = gout_all[...]
    o_up_ref[...] = gup_all[...]
    o_down_ref[...] = gdown_all[...]
    o_gate_ref[...] = ggate_all[...]
    links.drain()


VMEM = pl.BlockSpec(memory_space=pltpu.VMEM)


def run_layer(*args):
    shapes = [
        ((ROWS, D), F32),
        ((ROWS, D), F32),
        ((192, D), BF16),
        ((64, D), BF16),
        ((D, 256), BF16),
        ((256, D), BF16),
        ((LEN, D), BF16),
        ((8, D), F32),
    ]
    scratch = [
        ((LEN, D), BF16),
        ((LEN, D), BF16),
        ((1536, D), BF16),
        ((D, D), BF16),
        ((D, 1024), BF16),
        ((1024, D), BF16),
        ((2, D, D), BF16),
        ((192, LEN), BF16),
        ((LEN, 64), BF16),
        ((LEN, 64), BF16),
        ((LEN, QB), F32),
        ((LEN, QB), BF16),
        ((LEN, QB), BF16),
        ((64, LEN), F32),
        ((64, LEN), BF16),
        ((1, LEN), F32),
        ((D, 256), BF16),
        ((ROWS, D), F32),
        ((ROWS, D), F32),
        ((ROWS, D), F32),
        ((ROWS, D), F32),
        ((ROWS, 128), F32),
        ((256, D), BF16),
        ((256, D), BF16),
        ((ROWS, D), F32),
        ((256, 1024), BF16),
        ((256, 1024), F32),
        ((ROWS, D), F32),
        ((ROWS, D), BF16),
        ((ROWS, D), BF16),
        ((256, D), BF16),
        ((ROWS, D), BF16),
        ((ROWS, D), BF16),
        ((ROWS, D), BF16),
        ((256, 256), BF16),
        ((256, 256), BF16),
        ((256, 256), BF16),
        ((256, 1024), BF16),
        ((ROWS, D), F32),
        ((ROWS, D), BF16),
        ((ROWS, D), BF16),
        ((ROWS, D), F32),
        ((D, ROWS), BF16),
        ((64, LEN), BF16),
        ((8, D), F32),
        ((7, 8, D), F32),
        ((16, 8, D), F32),
        ((64, LEN), F32),
        ((64, LEN), F32),
        ((64, LEN), F32),
        ((192, LEN), BF16),
        ((1536, ROWS), BF16),
        ((16, 48, 128), BF16),
        ((15, 48, 128), BF16),
        ((192, D), BF16),
    ]
    for rows, cols in ((64, 128), (16, 512), (16, 384)):
        for count in (64, 48, 16, 12, 4, 3):
            scratch.append(((count, rows, cols), BF16))
    scratch += [
        ((64, D), BF16),
        ((D, 256), BF16),
        ((256, D), BF16),
        ((LEN, D), BF16),
    ]
    return pl.pallas_call(
        layer_kernel,
        out_shape=[jax.ShapeDtypeStruct(s, t) for s, t in shapes],
        in_specs=[VMEM] * 9,
        out_specs=[VMEM] * len(shapes),
        scratch_shapes=[pltpu.VMEM(s, t) for s, t in scratch]
        + [pltpu.SemaphoreType.DMA((N_SEMS,)), pltpu.SemaphoreType.DMA((N_SEMS,))],
        compiler_params=pltpu.CompilerParams(
            collective_id=0, has_side_effects=True, vmem_limit_bytes=60 * 1024 * 1024
        ),
        name="layer",
    )(*args)


def adamw(weight, first, second, grad, rate):
    first = BETA_ONE * first + (1.0 - BETA_ONE) * grad
    second = BETA_TWO * second + (1.0 - BETA_TWO) * grad * grad
    first_hat = first / (1.0 - BETA_ONE**STEP)
    second_hat = second / (1.0 - BETA_TWO**STEP)
    weight = weight - rate * (first_hat / (jnp.sqrt(second_hat) + ADAM_EPS) + DECAY * weight)
    return (weight, first, second)


def adamw_kernel(*refs):
    states, grads, outs = refs[0:21], refs[21:27], refs[27:48]
    for i in range(7):
        w, m, v = (r[...] for r in states[3 * i : 3 * i + 3])
        if i == 0:
            g = jnp.stack([grads[0][64 * j : 64 * j + 64, :].astype(F32).T for j in range(3)])
        elif i == 5:
            g = grads[5][0:2, :]
        elif i == 6:
            g = grads[5][2:6, :]
        else:
            g = grads[i][...].astype(F32)
        for ref, value in zip(outs[3 * i : 3 * i + 3], adamw(w, m, v, g, RATES[i])):
            ref[...] = value


GRID = 4


def run_adamw(states, grads):
    blocks = [
        ((3, D // GRID, 64), lambda i: (0, i, 0)),
        ((64 // GRID, D), lambda i: (i, 0)),
        ((D // GRID, 256), lambda i: (i, 0)),
        ((256 // GRID, D), lambda i: (i, 0)),
        ((LEN // GRID, D), lambda i: (i, 0)),
        ((2, D), lambda i: (0, 0)),
        ((4, D), lambda i: (0, 0)),
    ]
    state_specs = [pl.BlockSpec(*b) for b in blocks for _ in range(3)]
    grad_specs = [
        pl.BlockSpec((192, D // GRID), lambda i: (0, i)),
        *(pl.BlockSpec(*b) for b in blocks[1:5]),
        pl.BlockSpec((8, D), lambda i: (0, 0)),
    ]
    return pl.pallas_call(
        adamw_kernel,
        grid=(GRID,),
        out_shape=[jax.ShapeDtypeStruct(s.shape, F32) for s in states],
        in_specs=state_specs + grad_specs,
        out_specs=state_specs,
        compiler_params=pltpu.CompilerParams(vmem_limit_bytes=56 * 1024 * 1024),
        name="adamw",
    )(*states, *grads)


def local(inputs, cotangent, *state):
    rows = inputs.shape[1]
    weights = [state[3 * i] for i in range(7)]
    results = run_layer(
        inputs.reshape(rows, D),
        cotangent.reshape(rows, D),
        *weights,
    )
    mixed, ingrad, gq, gout, gup, gdown, ggate, gvec = results
    flat = list(state)
    for i in (12, 13, 14):
        flat[i] = flat[i].reshape(2 * D, D)
    new = list(run_adamw(flat, (gq, gout, gup, gdown, ggate, gvec)))
    for i in (12, 13, 14):
        new[i] = new[i].reshape(2, D, D)
    return (mixed.reshape(1, rows, D), ingrad.reshape(1, rows, D), *new)


def solution(mesh):
    batch = P("dp", "head", None)
    qkv = P(None, None, "head")
    first = P("head", None)
    second = P(None, "head")
    state = (qkv,) * 3 + (first,) * 3 + (second,) * 3 + (first,) * 3 + (P(),) * 9
    return jax.shard_map(
        local,
        mesh=mesh,
        in_specs=(batch, batch, *state),
        out_specs=(batch, batch, *state),
        check_vma=False,
    )
```

```python
import jax
import jax.numpy as jnp
from jax import lax
from jax.experimental import pallas as pl
from jax.experimental.pallas import tpu as pltpu
from jax.sharding import PartitionSpec as P

F32 = jnp.float32
BF16 = jnp.bfloat16
STEP = 10
NORM_EPS = 1e-05
BETA_ONE = 0.9
BETA_TWO = 0.999
ADAM_EPS = 1e-08
DECAY = 0.01
RATES = (0.04, 0.1, 0.04, 0.02, 0.04, 0.4, 0.3)
D = 512
ROWS = 128
LEN = 1024
QB = 256
NN = ((1,), (0,))
NT = ((1,), (1,))
TN = ((0,), (0,))


def dot(a, b, dims=NN):
    return lax.dot_general(a, b, (dims, ((), ())), preferred_element_type=F32)


def aligned(value, by):
    return pl.multiple_of(value, by)


class Group:
    def __init__(self, links, total, receives=1, each=None):
        self.send_sem, self.total = links.semaphore(), total
        self.each = total if each is None else each
        self.recv_sems = [links.semaphore() for _ in range(receives)]
        links.groups.append(self)

    def send(self, src, dst, device, k=0):
        pltpu.make_async_remote_copy(
            src_ref=src,
            dst_ref=dst,
            send_sem=self.send_sem,
            recv_sem=self.recv_sems[k],
            device_id=device,
            device_id_type=pl.DeviceIdType.MESH,
        ).start()

    def wait(self, k=0):
        pltpu.make_async_copy(self.each, self.each, self.recv_sems[k]).wait()


class Links:
    def __init__(self, sems):
        self.sems, self.used, self.groups = sems, 0, []

    def semaphore(self):
        self.used += 1
        return self.sems.at[self.used - 1]

    def drain(self):
        for g in self.groups:
            pltpu.make_async_copy(g.total, g.total, g.send_sem).wait()


N_SEMS = 128
N_LOCAL = 32


def layer_kernel(
    x_hbm,
    dy_hbm,
    gains_hbm,
    biases_hbm,
    qkv_hbm,
    out_hbm,
    up_hbm,
    down_hbm,
    gate_hbm,
    *rest,
):
    states = [r for i, w in enumerate((qkv_hbm, out_hbm, up_hbm, down_hbm, gate_hbm)) for r in (w, *rest[2 * i : 2 * i + 2])]
    kept = rest[18:33]
    layer_body(x_hbm, dy_hbm, gains_hbm, biases_hbm, qkv_hbm, out_hbm, up_hbm, down_hbm, gate_hbm, *rest[10:18], states, kept, *rest[33:])


def layer_body(
    x_hbm,
    dy_hbm,
    gains_hbm,
    biases_hbm,
    qkv_hbm,
    out_hbm,
    up_hbm,
    down_hbm,
    gate_hbm,
    mixed_ref,
    ingrad_ref,
    o_qkv_ref,
    o_out_ref,
    o_up_ref,
    o_down_ref,
    o_gate_ref,
    o_vec_ref,
    states,
    kept,
    x_ref,
    dy_ref,
    gains_ref,
    biases_ref,
    qkv_ref,
    out_ref,
    up_ref,
    down_ref,
    gate_ref,
    x_all,
    h1_all,
    w_all,
    out_all,
    up_all,
    down_all,
    gate_low,
    proj_t,
    k_nat,
    v_nat,
    s_buf,
    p_buf,
    ds_buf,
    o_t,
    o_low,
    lse,
    heads_t,
    g1_buf,
    attn_buf,
    x1_buf,
    xhat_buf,
    rstd_buf,
    h1_pair,
    h2_pair,
    g2_buf,
    act_buf,
    dgelu_buf,
    ffn_own,
    ffn_send,
    ffn_recv,
    dffn_pair,
    dz2_full,
    dz1_full,
    dattn_full,
    dz2_half,
    late_half,
    dhid_buf,
    dh2_own,
    dh2_send,
    dh2_recv,
    dh2_gate,
    dheads_t,
    do_t,
    vec,
    vec_s,
    vec_a,
    vec_b,
    dq_t,
    dk_t,
    dv_t,
    dproj_low,
    dproj_all,
    gq_low,
    gq_sib,
    gq_send,
    gq_recv,
    gq_all,
    gates_low,
    gates_recv,
    gates_sum,
    gout_low,
    gout_recv,
    gout_sum,
    gout_all,
    gup_all,
    gdown_all,
    ggate_all,
    su1,
    ru1,
    su2,
    ru2,
    su3,
    ru3,
    sd1,
    rd1,
    sd2,
    rd2,
    sd3,
    rd3,
    sems,
    local_sems,
):
    loads = [
        pltpu.make_async_copy(src, dst, local_sems.at[i])
        for i, (src, dst) in enumerate(
            (
                (x_hbm, x_ref),
                (qkv_hbm, qkv_ref),
                (out_hbm, out_ref),
                (up_hbm, up_ref),
                (down_hbm, down_ref),
                (gains_hbm, gains_ref),
                (biases_hbm, biases_ref),
                (gate_hbm, gate_ref),
                (dy_hbm, dy_ref),
            )
        )
    ]
    for load in loads:
        load.start()
    keeps = [
        pltpu.make_async_copy(src, dst, local_sems.at[14 + i])
        for i, (src, dst) in enumerate(zip(states, kept))
    ]

    dp, head = lax.axis_index("dp"), lax.axis_index("head")
    x_hi, y, core = dp // 8, (dp // 2) % 4, dp % 2
    z, x_lo = head // 2, head % 2
    xx = x_hi * 2 + x_lo
    sub = x_hi * 4 + y
    links = Links(sems)

    def head_peer(o):
        return (head + o) % 8

    def in_head(o):
        return (dp, (head + o) % 8)

    def head_from(o):
        return (head + 8 - o) % 8

    def sub_peer(o):
        return (sub + o) % 8

    def in_sub(o):
        return (((sub + o) % 8) * 2 + core, head)

    def ring(axis, o):
        nx = (xx + o) % 4 if axis == "x" else xx
        ny = (y + o) % 4 if axis == "y" else y
        nz = (z + o) % 4 if axis == "z" else z
        return ((nx // 2) * 8 + ny * 2 + core, nz * 2 + nx % 2)

    sibling = (sub * 2 + (1 - core), head)

    barrier = pltpu.get_barrier_semaphore()
    greeted = [in_head(o) for o in range(1, 8)] + [in_sub(o) for o in range(1, 8)]
    greeted += [sibling, ((1 - x_hi) * 8 + y * 2 + core, z * 2 + 1 - x_lo)]
    for device in greeted:
        pl.semaphore_signal(
            barrier, inc=1, device_id=device, device_id_type=pl.DeviceIdType.MESH
        )

    own = pl.ds(aligned(head * ROWS, ROWS), ROWS)
    own_core = pl.ds(aligned(core * ROWS, ROWS), ROWS)
    sib_core = pl.ds(aligned((1 - core) * ROWS, ROWS), ROWS)
    half = pl.ds(aligned(core * 256, 256), 256)
    sib_half = pl.ds(aligned((1 - core) * 256, 256), 256)
    own_heads = pl.ds(aligned(head * 64, 64), 64)
    own_w = pl.ds(aligned(head * 192, 64), 192)
    sub_rows = pl.ds(aligned(sub * 128, 128), 128)

    for load in loads[0:5]:
        load.wait()
    x_all[own, :] = x_ref[...]
    w_all[own_w, :] = qkv_ref[...].astype(BF16)
    out_all[own_heads, :] = out_ref[...].astype(BF16)
    up_all[:, own] = up_ref[:, own_core].astype(BF16)
    down_all[own, :] = down_ref[own_core, :].astype(BF16)

    def out_at(s):
        return [out_all.at[pl.ds(aligned(s * 64 + a, 32), n), :] for a, n in ((0, 64), (0, 32), (32, 32))]

    def up_at(s):
        cols = pl.ds(aligned(s * 128, 128), 128)
        return [up_all.at[a : a + n, cols] for a, n in ((0, 512), (0, 256), (256, 256))]

    def down_at(s):
        return [down_all.at[pl.ds(aligned(s * 128 + a, 64), n), :] for a, n in ((0, 128), (0, 64), (64, 64))]

    def w_at(s):
        return [w_all.at[pl.ds(aligned(s * 192 + a, 96), n), :] for a, n in ((0, 192), (0, 96), (96, 96))]

    class Spread:
        def __init__(self, at, three, four):
            self.at, self.one = at, at(head)[0]
            self.ring_z = Group(links, three, 3, self.one)
            self.over_x = Group(links, four)

        def begin(self):
            for o in range(1, 4):
                self.ring_z.send(self.one, self.one, ring("z", o), o - 1)
            self.forward(head)

        def forward(self, s):
            _, first, second = self.at(s)
            self.over_x.send(first, first, ring("x", 1))
            self.over_x.send(second, second, ring("x", 3))

        def pass_on(self):
            for o in range(1, 4):
                self.ring_z.wait(o - 1)
                self.forward(((z + 4 - o) % 4) * 2 + x_lo)

    x_group = Group(links, x_all.at[0 : 7 * ROWS, :], 7, x_ref)
    spread_out = Spread(out_at, out_all.at[0:192, :], out_all.at[0:256, :])
    spread_up = Spread(up_at, up_all.at[:, 0:384], up_all.at[:, 0:512])
    spread_down = Spread(down_at, down_all.at[0:384, :], down_all.at[0:512, :])
    spread_w = Spread(w_at, w_all.at[0:576, :], w_all.at[0:768, :])

    pl.semaphore_wait(barrier, len(greeted))
    for o in range(1, 8):
        x_group.send(x_ref, x_all.at[own, :], in_head(o), o - 1)
    for keep in keeps:
        keep.start()
    spread_out.begin()
    spread_up.begin()
    spread_down.begin()

    for load in loads[5:9]:
        load.wait()
    for i in range(2):
        gate_low[i] = gate_ref[D * i : D * i + D, :].astype(BF16)
    gain_one, shift_one = gains_ref[0:1, :], biases_ref[0:1, :]
    gain_two, shift_two = gains_ref[1:2, :], biases_ref[1:2, :]

    def project(block):
        for s in range(4):
            rows = pl.ds(aligned(block * ROWS + 32 * s, 32), 32)
            v = x_all[rows, :].astype(F32)
            center = v - jnp.mean(v, axis=-1, keepdims=True)
            spread = jnp.mean(center * center, axis=-1, keepdims=True)
            h = center * lax.rsqrt(spread + NORM_EPS) * gain_one + shift_one
            h1_all[rows, :] = h.astype(BF16)
        rows = pl.ds(aligned(block * ROWS, ROWS), ROWS)
        pt = dot(w_all[own_w, :], h1_all[rows, :], NT)
        proj_t[0:64, rows] = (pt[0:64].astype(BF16).astype(F32) * 0.125).astype(BF16)
        proj_t[64:192, rows] = pt[64:192].astype(BF16)
        k_nat[rows, :] = pt[64:128].T.astype(BF16)
        v_nat[rows, :] = pt[128:192].T.astype(BF16)

    project(head)
    for o in range(1, 8):
        x_group.wait(o - 1)
        project(head_from(o))
    h1_pair[own_core, :] = h1_all[own, :]
    h1_group = Group(links, h1_pair.at[0:ROWS, :])
    h1_group.send(h1_pair.at[own_core, :], h1_pair.at[own_core, :], sibling)
    spread_out.pass_on()

    for j in range(LEN // QB):
        cols = slice(QB * j, QB * (j + 1))
        queries = proj_t[0:64, cols]
        ceiling = jnp.full((1, QB), -1e30, F32)
        tiles = QB * (j + 1) // ROWS
        for t in range(tiles):
            s = dot(k_nat[ROWS * t : ROWS * (t + 1), :], queries)
            if ROWS * t >= QB * j:
                keys_at = lax.broadcasted_iota(jnp.int32, (ROWS, QB), 0) + ROWS * t
                queries_at = lax.broadcasted_iota(jnp.int32, (ROWS, QB), 1) + QB * j
                s = jnp.where(keys_at <= queries_at, s, -1e30)
            s_buf[ROWS * t : ROWS * (t + 1), :] = s
            ceiling = jnp.maximum(ceiling, jnp.max(s, axis=0, keepdims=True))
        mass = jnp.zeros((1, QB), F32)
        for t in range(tiles):
            e = jnp.exp(s_buf[ROWS * t : ROWS * (t + 1), :] - ceiling)
            mass = mass + jnp.sum(e, axis=0, keepdims=True)
            p_buf[ROWS * t : ROWS * (t + 1), :] = e.astype(BF16)
        total = dot(proj_t[128:192, 0 : QB * (j + 1)], p_buf[0 : QB * (j + 1), :])
        total = total / mass
        o_t[:, cols] = total
        o_low[:, cols] = total.astype(BF16)
        lse[:, cols] = ceiling + jnp.log(mass)
    heads_group = Group(links, heads_t.at[0:448, 0:ROWS])
    for o in range(1, 8):
        block = o_low.at[:, pl.ds(aligned(head_peer(o) * ROWS, ROWS), ROWS)]
        heads_group.send(block, heads_t.at[own_heads, own_core], in_head(o))
    heads_t[own_heads, own_core] = o_low[:, own]

    g1_buf[...] = dot(h1_all[own, :], gate_low[0]) + biases_ref[2:3, :]
    spread_up.pass_on()
    heads_group.wait()
    headst_group = Group(links, heads_t.at[:, 0:ROWS])
    headst_group.send(heads_t.at[:, own_core], heads_t.at[:, own_core], sibling)
    spread_out.over_x.wait()
    attn_buf[...] = dot(heads_t[:, own_core], out_all[...], TN)
    for s in range(4):
        rows = slice(32 * s, 32 * s + 32)
        g1 = jax.nn.sigmoid(g1_buf[rows, :])
        g1_buf[rows, :] = g1
        x = x_ref[rows, :].astype(F32)
        x1 = g1 * attn_buf[rows, :] + (1.0 - g1) * x
        x1_buf[rows, :] = x1
        center = x1 - jnp.mean(x1, axis=-1, keepdims=True)
        spread = jnp.mean(center * center, axis=-1, keepdims=True)
        rstd = lax.rsqrt(spread + NORM_EPS)
        xhat = center * rstd
        xhat_buf[rows, :] = xhat
        rstd_buf[rows, :] = jnp.broadcast_to(rstd, (32, 128))
        h2 = xhat * gain_two + shift_two
        h2_pair[pl.ds(aligned(core * ROWS + 32 * s, 32), 32), :] = h2.astype(BF16)
    h2_group = Group(links, h2_pair.at[0:ROWS, :])
    h2_group.send(h2_pair.at[own_core, :], h2_pair.at[own_core, :], sibling)
    spread_down.pass_on()
    spread_w.begin()
    g2_buf[...] = dot(h2_pair[own_core, :], gate_low[1]) + biases_ref[3:4, :]
    spread_up.over_x.wait()
    h2_group.wait()
    for n in range(4):
        cols = slice(256 * n, 256 * n + 256)
        u = dot(h2_pair[...], up_all[:, cols])
        c0 = 0.7978845608028654
        inner = jnp.tanh(c0 * (u + 0.044715 * u * u * u))
        act_buf[:, cols] = (0.5 * u * (1.0 + inner)).astype(BF16)
        dgelu_buf[:, cols] = 0.5 * (1.0 + inner) + 0.5 * u * (1.0 - inner * inner) * c0 * (
            1.0 + 3.0 * 0.044715 * u * u
        )
    spread_down.over_x.wait()
    ffn_send[...] = dot(act_buf[sib_core, :], down_all[...]).astype(BF16)
    ffn_group = Group(links, ffn_recv)
    ffn_group.send(ffn_send, ffn_recv, sibling)
    ffn_own[...] = dot(act_buf[own_core, :], down_all[...])
    ffn_group.wait()
    bias_two = jnp.zeros((1, D), F32)
    for s in range(4):
        rows = slice(32 * s, 32 * s + 32)
        ffn = ffn_own[rows, :] + ffn_recv[rows, :].astype(F32)
        g2 = jax.nn.sigmoid(g2_buf[rows, :])
        g2_buf[rows, :] = g2
        x1 = x1_buf[rows, :]
        dy = dy_ref[rows, :].astype(F32)
        mixed_ref[rows, :] = g2 * ffn + (1.0 - g2) * x1
        dffn_pair[pl.ds(aligned(core * ROWS + 32 * s, 32), 32), :] = (g2 * dy).astype(BF16)
        dz = (dy * (ffn - x1) * g2 * (1.0 - g2)).astype(BF16)
        dz2_full[rows, :] = dz
        bias_two = bias_two + jnp.sum(dz.astype(F32), axis=0, keepdims=True)
    dffn_group = Group(links, dffn_pair.at[0:ROWS, :])
    dffn_group.send(dffn_pair.at[own_core, :], dffn_pair.at[own_core, :], sibling)
    dz2_group = Group(links, dz2_half.at[0:ROWS, :])
    dz2_group.send(dz2_full.at[:, sib_half], dz2_half.at[own_core, :], sibling)
    dz2_half[own_core, :] = dz2_full[:, half]
    dh2_gate[...] = dot(dz2_full[...], gate_low[1], NT)
    dffn_group.wait()

    def stage(axis, at, src, dst, size):
        group = Group(links, dst)
        for o in range(1, 4):
            t = (at + o) % 4
            group.send(
                src.at[pl.ds(t * size, size)],
                dst.at[pl.ds((o - 1) * size, size)],
                ring(axis, o),
            )
        return group

    def add_up(group, at, src, got, size, store):
        group.wait()

        def add(i, carry):
            total = src[at * size + i].astype(F32)
            for o in range(3):
                total = total + got[o * size + i].astype(F32)
            store(i, total)
            return carry

        lax.fori_loop(0, size, add, 0)

    def to_bf16(ref):
        def store(i, total):
            ref[i] = total.astype(BF16)

        return store

    for h in range(8):
        gd = dot(act_buf[:, 128 * h : 128 * h + 128], dffn_pair[...], TN).astype(BF16)
        for g in range(8):
            ch_x, ch_y, ch_z = (g // 4) * 2 + h % 2, g % 4, h // 2
            sd1[ch_y * 16 + ch_x * 4 + ch_z] = gd[16 * g : 16 * g + 16, :]
    down_group = stage("y", y, sd1, rd1, 16)
    for n in range(4):
        cols = slice(256 * n, 256 * n + 256)
        da = dot(dffn_pair[...], down_all[cols, :], NT)
        dhid_buf[:, cols] = (da * dgelu_buf[:, cols]).astype(BF16)
    dh2_send[...] = dot(dhid_buf[sib_core, :], up_all[...], NT).astype(BF16)
    dh2_group = Group(links, dh2_recv)
    dh2_group.send(dh2_send, dh2_recv, sibling)
    for h in range(8):
        gu = dot(h2_pair[...], dhid_buf[:, 128 * h : 128 * h + 128], TN).astype(BF16)
        for g in range(8):
            ch_x, ch_y, ch_z = (g // 4) * 2 + h % 2, g % 4, h // 2
            su1[ch_z * 16 + ch_y * 4 + ch_x] = gu[64 * g : 64 * g + 64, :]
    up_group = stage("z", z, su1, ru1, 16)
    dh2_own[...] = dot(dhid_buf[own_core, :], up_all[...], NT)
    dh2_group.wait()
    gain_sum = jnp.zeros((1, D), F32)
    shift_sum = jnp.zeros((1, D), F32)
    bias_one = jnp.zeros((1, D), F32)
    for s in range(4):
        rows = slice(32 * s, 32 * s + 32)
        dh2 = dh2_own[rows, :] + dh2_recv[rows, :].astype(F32) + dh2_gate[rows, :]
        xhat = xhat_buf[rows, :]
        gain_sum = gain_sum + jnp.sum(dh2 * xhat, axis=0, keepdims=True)
        shift_sum = shift_sum + jnp.sum(dh2, axis=0, keepdims=True)
        dxhat = dh2 * gain_two
        mean_a = jnp.mean(dxhat, axis=-1, keepdims=True)
        mean_b = jnp.mean(dxhat * xhat, axis=-1, keepdims=True)
        rstd = rstd_buf[rows, 0:1]
        dx1 = (1.0 - g2_buf[rows, :]) * dy_ref[rows, :].astype(F32) + rstd * (
            dxhat - mean_a - xhat * mean_b
        )
        g1 = g1_buf[rows, :]
        dattn_full[rows, :] = (g1 * dx1).astype(BF16)
        x = x_ref[rows, :].astype(F32)
        dz = (dx1 * (attn_buf[rows, :] - x) * g1 * (1.0 - g1)).astype(BF16)
        dz1_full[rows, :] = dz
        bias_one = bias_one + jnp.sum(dz.astype(F32), axis=0, keepdims=True)
        ingrad_ref[rows, :] = (1.0 - g1) * dx1
    vec[1:2, :] = gain_sum
    vec[3:4, :] = shift_sum
    vec[4:5, :] = bias_one
    vec[5:6, :] = bias_two
    vec[6:8, :] = jnp.zeros((2, D), F32)

    late_group = Group(links, late_half.at[0])
    late_group.send(dz1_full.at[:, sib_half], late_half.at[0, own_core, :], sibling)
    late_group.send(dattn_full.at[:, sib_half], late_half.at[1, own_core, :], sibling)
    dheads_t[...] = dot(out_all[...], dattn_full[...], NT).astype(BF16)
    dheads_group = Group(links, do_t.at[:, 0 : 7 * ROWS])
    for o in range(1, 8):
        block = dheads_t.at[pl.ds(aligned(head_peer(o) * 64, 64), 64), :]
        dheads_group.send(block, do_t.at[:, own], in_head(o))
    do_t[:, own] = dheads_t[own_heads, :]
    late_half[0, own_core, :] = dz1_full[:, half]
    late_half[1, own_core, :] = dattn_full[:, half]

    h1_group.wait()
    dz2_group.wait()
    headst_group.wait()
    late_group.wait()
    gates_low[0:512, :] = dot(h1_pair[...], late_half[0], TN).astype(BF16)
    gates_low[512:1024, :] = dot(h2_pair[...], dz2_half[...], TN).astype(BF16)
    gates_group = Group(links, gates_recv.at[0, 0:7])
    for o in range(1, 8):
        block = gates_low.at[pl.ds(aligned(sub_peer(o) * 128, 128), 128), :]
        gates_group.send(block, gates_recv.at[0, sub], in_sub(o))
    gates_recv[0, sub] = gates_low[sub_rows, :]
    gout_low[...] = dot(heads_t[...], late_half[1]).astype(BF16)
    gout_group = Group(links, gout_recv.at[0, 0:7])
    for o in range(1, 8):
        block = gout_low.at[pl.ds(aligned(head_peer(o) * 64, 64), 64), :]
        gout_group.send(block, gout_recv.at[0, head], in_head(o))
    gout_recv[0, head] = gout_low[own_heads, :]
    spread_w.pass_on()

    def add_eight(ref):
        total = ref[0].astype(F32)
        for o in range(1, 8):
            total = total + ref[o].astype(F32)
        return total

    dheads_group.wait()
    dk_t[...] = jnp.zeros_like(dk_t)
    dv_t[...] = jnp.zeros_like(dv_t)
    for j in range(LEN // QB):
        cols = slice(QB * j, QB * (j + 1))
        upto = QB * (j + 1)
        queries = proj_t[0:64, cols]
        grads = do_t[:, cols]
        delta = jnp.sum(o_t[:, cols] * grads.astype(F32), axis=0, keepdims=True)
        row_lse = lse[:, cols]
        for t in range(upto // ROWS):
            keys = slice(ROWS * t, ROWS * (t + 1))
            p = jnp.exp(dot(k_nat[keys, :], queries) - row_lse)
            if ROWS * t >= QB * j:
                keys_at = lax.broadcasted_iota(jnp.int32, (ROWS, QB), 0) + ROWS * t
                queries_at = lax.broadcasted_iota(jnp.int32, (ROWS, QB), 1) + QB * j
                p = jnp.where(keys_at <= queries_at, p, 0.0)
            d = dot(v_nat[keys, :], grads)
            p_buf[keys, :] = p.astype(BF16)
            ds_buf[keys, :] = (p * (d - delta)).astype(BF16)
        dq_t[:, cols] = dot(proj_t[64:128, 0:upto], ds_buf[0:upto, :]) * 0.125
        dk_t[:, 0:upto] += dot(queries, ds_buf[0:upto, :], NT)
        dv_t[:, 0:upto] += dot(grads, p_buf[0:upto, :], NT)
    dproj_low[0:64, :] = dq_t[...].astype(BF16)
    dproj_low[64:128, :] = dk_t[...].astype(BF16)
    dproj_low[128:192, :] = dv_t[...].astype(BF16)
    dproj_group = Group(links, dproj_all.at[0 : 7 * 192, :])
    for o in range(1, 8):
        block = dproj_low.at[:, pl.ds(aligned(head_peer(o) * ROWS, ROWS), ROWS)]
        dproj_group.send(block, dproj_all.at[own_w, :], in_head(o))
    dproj_all[own_w, :] = dproj_low[:, own]

    gq_low[...] = dot(dproj_low[...], h1_all[...]).astype(BF16)
    gq_pair = Group(links, gq_sib)
    gq_pair.send(gq_low.at[:, sib_half], gq_sib, sibling)

    gout_group.wait()
    gout_sum[...] = add_eight(gout_recv.at[0]).astype(BF16)
    gout_group = Group(links, gout_recv.at[1, 0:7])
    for o in range(1, 8):
        gout_group.send(gout_sum, gout_recv.at[1, sub], in_sub(o))
    gout_recv[1, sub] = gout_sum[...]
    gates_group.wait()
    gates_sum[...] = add_eight(gates_recv.at[0]).astype(BF16)
    gates_group = Group(links, gates_recv.at[1, 0:7])
    for o in range(1, 8):
        gates_group.send(gates_sum, gates_recv.at[1, head], in_head(o))
    gates_recv[1, head] = gates_sum[...]

    gq_pair.wait()
    total = gq_low[:, half].astype(F32) + gq_sib[...].astype(F32)
    for i in range(8):
        r, c = 48 * (i // 2), 128 * (i % 2)
        gq_send[i] = total[r : r + 48, c : c + 128].astype(BF16)
    gq_group = Group(links, gq_recv.at[0:7])
    for o in range(1, 8):
        gq_group.send(gq_send.at[sub_peer(o)], gq_recv.at[sub], in_sub(o))
    gq_recv[sub] = gq_send[sub]

    add_up(down_group, y, sd1, rd1, 16, to_bf16(sd2))
    down_group = stage("x", xx, sd2, rd2, 4)
    add_up(up_group, z, su1, ru1, 16, to_bf16(su2))
    up_group = stage("y", y, su2, ru2, 4)

    spread_w.over_x.wait()
    dproj_group.wait()
    dh2_own[...] = dot(dproj_all[...], w_all[...], TN) + dot(dz1_full[...], gate_low[0], NT)
    gain_sum = jnp.zeros((1, D), F32)
    shift_sum = jnp.zeros((1, D), F32)
    for s in range(4):
        rows = slice(32 * s, 32 * s + 32)
        v = x_ref[rows, :].astype(F32)
        center = v - jnp.mean(v, axis=-1, keepdims=True)
        spread = jnp.mean(center * center, axis=-1, keepdims=True)
        rstd = lax.rsqrt(spread + NORM_EPS)
        xhat = center * rstd
        dh = dh2_own[rows, :]
        gain_sum = gain_sum + jnp.sum(dh * xhat, axis=0, keepdims=True)
        shift_sum = shift_sum + jnp.sum(dh, axis=0, keepdims=True)
        dxhat = dh * gain_one
        mean_a = jnp.mean(dxhat, axis=-1, keepdims=True)
        mean_b = jnp.mean(dxhat * xhat, axis=-1, keepdims=True)
        ingrad_ref[rows, :] += rstd * (dxhat - mean_a - xhat * mean_b)
    vec[0:1, :] = gain_sum
    vec[2:3, :] = shift_sum
    vec_group = Group(links, vec_s)
    vec_group.send(vec, vec_s, sibling)

    gq_group.wait()
    gq_rows = pl.ds(aligned((sub // 2) * 48, 48), 48)
    gq_cols = pl.ds(aligned(core * 256 + (sub % 2) * 128, 128), 128)
    gq_all[gq_rows, gq_cols] = add_eight(gq_recv).astype(BF16)
    gq_group = Group(links, gq_recv.at[0:7])
    for o in range(1, 8):
        block = gq_all.at[gq_rows, gq_cols]
        gq_group.send(block, block, in_sub(o))

    vec_group.wait()
    vec_a[sub] = vec[...] + vec_s[...]
    vec_group = Group(links, vec_a.at[0:7])
    for o in range(1, 8):
        vec_group.send(vec_a.at[sub], vec_a.at[sub], in_sub(o))

    gout_group.wait()
    gout_all[:, half] = add_eight(gout_recv.at[1]).astype(BF16)
    gout_pair = Group(links, gout_sum)
    gout_pair.send(gout_all.at[:, half], gout_all.at[:, half], sibling)
    gates_group.wait()
    ggate_all[sub_rows, half] = add_eight(gates_recv.at[1]).astype(BF16)
    gates_group = Group(links, gates_recv.at[0, 0:7])
    for o in range(1, 8):
        block = ggate_all.at[sub_rows, half]
        gates_group.send(block, block, in_sub(o))

    add_up(down_group, xx, sd2, rd2, 4, to_bf16(sd3))
    down_group = stage("z", z, sd3, rd3, 1)
    add_up(up_group, y, su2, ru2, 4, to_bf16(su3))
    up_group = stage("x", xx, su3, ru3, 1)

    vec_group.wait()
    vec_b[head] = add_eight(vec_a)
    vec_group = Group(links, vec_b.at[0:7])
    for o in range(1, 8):
        vec_group.send(vec_b.at[head], vec_b.at[head], in_head(o))
    gq_group.wait()
    gq_pair = Group(links, gq_sib)
    gq_pair.send(gq_all.at[:, half], gq_all.at[:, half], sibling)

    up_rows = pl.ds(aligned(sub * 64, 64), 64)
    down_rows = pl.ds(aligned(core * 128 + sub * 16, 16), 16)

    def store_up(i, total):
        gup_all[up_rows, own_core] = total.astype(BF16)

    def store_down(i, total):
        gdown_all[down_rows, :] = total.astype(BF16)

    add_up(down_group, z, sd3, rd3, 1, store_down)
    down_group = Group(links, gdown_all.at[0:112, :])
    for o in range(1, 8):
        block = gdown_all.at[down_rows, :]
        down_group.send(block, block, in_sub(o))
    add_up(up_group, xx, su3, ru3, 1, store_up)
    up_group = Group(links, gup_all.at[0:448, 0:128])
    for o in range(1, 8):
        block = gup_all.at[up_rows, own_core]
        up_group.send(block, block, in_sub(o))

    gates_group.wait()
    gates_pair = Group(links, gates_low)
    gates_pair.send(ggate_all.at[:, half], ggate_all.at[:, half], sibling)
    down_group.wait()
    down_pair = Group(links, gdown_all.at[0:128, :])
    down_pair.send(gdown_all.at[own_core, :], gdown_all.at[own_core, :], sibling)
    up_group.wait()
    up_pair = Group(links, gup_all.at[:, 0:128])
    up_pair.send(gup_all.at[:, own_core], gup_all.at[:, own_core], sibling)
    vec_group.wait()
    o_vec_ref[...] = add_eight(vec_b)

    stores = []
    for i, (group, src, dst) in enumerate(
        (
            (gq_pair, gq_all, o_qkv_ref),
            (gout_pair, gout_all, o_out_ref),
            (gates_pair, ggate_all, o_gate_ref),
            (down_pair, gdown_all, o_down_ref),
            (up_pair, gup_all, o_up_ref),
        )
    ):
        group.wait()
        stores.append(pltpu.make_async_copy(src, dst, local_sems.at[9 + i]))
        stores[-1].start()
    links.drain()
    for store in stores + keeps:
        store.wait()


VMEM = pl.BlockSpec(memory_space=pltpu.VMEM)
ANY = pl.BlockSpec(memory_space=pl.ANY)
HBM = pl.BlockSpec(memory_space=pltpu.HBM)


def run_layer(*args):
    shapes = [
        ((ROWS, D), F32),
        ((ROWS, D), F32),
        ((192, D), BF16),
        ((64, D), BF16),
        ((D, 256), BF16),
        ((256, D), BF16),
        ((LEN, D), BF16),
        ((8, D), F32),
    ]
    scratch = [
        ((ROWS, D), BF16),
        ((ROWS, D), BF16),
        ((2, D), F32),
        ((4, D), F32),
        ((192, D), F32),
        ((64, D), F32),
        ((D, 256), F32),
        ((256, D), F32),
        ((2 * D, D), F32),
        ((LEN, D), BF16),
        ((LEN, D), BF16),
        ((1536, D), BF16),
        ((D, D), BF16),
        ((D, 1024), BF16),
        ((1024, D), BF16),
        ((2, D, D), BF16),
        ((192, LEN), BF16),
        ((LEN, 64), BF16),
        ((LEN, 64), BF16),
        ((LEN, QB), F32),
        ((LEN, QB), BF16),
        ((LEN, QB), BF16),
        ((64, LEN), F32),
        ((64, LEN), BF16),
        ((1, LEN), F32),
        ((D, 256), BF16),
        ((ROWS, D), F32),
        ((ROWS, D), F32),
        ((ROWS, D), F32),
        ((ROWS, D), F32),
        ((ROWS, 128), F32),
        ((256, D), BF16),
        ((256, D), BF16),
        ((ROWS, D), F32),
        ((256, 1024), BF16),
        ((256, 1024), F32),
        ((ROWS, D), F32),
        ((ROWS, D), BF16),
        ((ROWS, D), BF16),
        ((256, D), BF16),
        ((ROWS, D), BF16),
        ((ROWS, D), BF16),
        ((ROWS, D), BF16),
        ((256, 256), BF16),
        ((2, 256, 256), BF16),
        ((256, 1024), BF16),
        ((ROWS, D), F32),
        ((ROWS, D), BF16),
        ((ROWS, D), BF16),
        ((ROWS, D), F32),
        ((D, ROWS), BF16),
        ((64, LEN), BF16),
        ((8, D), F32),
        ((8, D), F32),
        ((8, 8, D), F32),
        ((8, 8, D), F32),
        ((64, LEN), F32),
        ((64, LEN), F32),
        ((64, LEN), F32),
        ((192, LEN), BF16),
        ((1536, ROWS), BF16),
        ((192, D), BF16),
        ((192, 256), BF16),
        ((8, 48, 128), BF16),
        ((8, 48, 128), BF16),
        ((192, D), BF16),
        ((LEN, 256), BF16),
        ((2, 8, 128, 256), BF16),
        ((128, 256), BF16),
        ((D, 256), BF16),
        ((2, 8, 64, 256), BF16),
        ((64, 256), BF16),
        ((64, D), BF16),
        ((D, 256), BF16),
        ((256, D), BF16),
        ((LEN, D), BF16),
    ]
    for rows, cols in ((64, 128), (16, 512)):
        for count in (64, 48, 16, 12, 4, 3):
            scratch.append(((count, rows, cols), BF16))
    return pl.pallas_call(
        layer_kernel,
        out_shape=[jax.ShapeDtypeStruct(s, t) for s, t in shapes]
        + [pltpu.VMEM(s, F32) for s in SHAPES[0:5] for _ in range(3)],
        in_specs=[HBM] * 19,
        out_specs=[VMEM] * 2 + [ANY] * 5 + [VMEM] + [VMEM] * 15,
        scratch_shapes=[pltpu.VMEM(s, t) for s, t in scratch]
        + [pltpu.SemaphoreType.DMA((N_SEMS,)), pltpu.SemaphoreType.DMA((N_LOCAL,))],
        compiler_params=pltpu.CompilerParams(
            collective_id=0, has_side_effects=True, vmem_limit_bytes=40 * 1024 * 1024
        ),
        name="layer",
    )(*args)


SHAPES = ((192, D), (64, D), (D, 256), (256, D), (LEN, D), (2, D), (4, D))
JOBS = [(0, 0, 192), (1, 0, 64), (2, 0, 512), (3, 0, 256)] + [(4, 256 * i, 256) for i in range(4)]


def adamw(weight, first, second, grad, rate):
    first = BETA_ONE * first + (1.0 - BETA_ONE) * grad
    second = BETA_TWO * second + (1.0 - BETA_TWO) * grad * grad
    first_hat = first * (1.0 / (1.0 - BETA_ONE**STEP))
    second_hat = second * (1.0 / (1.0 - BETA_TWO**STEP))
    weight = weight - rate * (first_hat / (jnp.sqrt(second_hat) + ADAM_EPS) + DECAY * weight)
    return (weight, first, second)


def adamw_kernel(*refs):
    states, grads, passed = refs[0:21], refs[21:27], refs[27:29]
    outs, passed_on = refs[29:50], refs[50:52]
    bufs, gbufs = refs[52:57], refs[57:62]
    grad_sems, out_sems, pass_sems = refs[62:65]

    passes = [
        pltpu.make_async_copy(a, b, pass_sems.at[i])
        for i, (a, b) in enumerate(zip(passed, passed_on))
    ]
    for j, (a, r, n) in enumerate(JOBS):
        rows = pl.ds(r, n)
        pltpu.make_async_copy(grads[a].at[rows, :], gbufs[a].at[rows, :], grad_sems.at[j]).start()
    for c in passes:
        c.start()
    for a, lo, hi in ((5, 0, 2), (6, 2, 6)):
        new = adamw(*(states[3 * a + k][...] for k in range(3)), grads[5][lo:hi, :], RATES[a])
        for k in range(3):
            outs[3 * a + k][...] = new[k]
    for j, (a, r, n) in enumerate(JOBS):
        rows = pl.ds(r, n)
        part = gbufs[a].at[rows, :]
        pltpu.make_async_copy(part, part, grad_sems.at[j]).wait()
        step = 16 if SHAPES[a][1] == D else 32

        def update(i, carry):
            at = pl.ds(aligned(r + i * step, step), step)
            new = adamw(*(states[3 * a + k][at, :] for k in range(3)), gbufs[a][at, :].astype(F32), RATES[a])
            for k in range(3):
                bufs[a][k, at, :] = new[k]
            return carry

        lax.fori_loop(0, n // step, update, 0)
        for k in range(3):
            pltpu.make_async_copy(
                bufs[a].at[k, rows, :], outs[3 * a + k].at[rows, :], out_sems.at[j]
            ).start()
    for j, (a, r, n) in enumerate(JOBS):
        whole = bufs[a].at[:, pl.ds(r, n), :]
        pltpu.make_async_copy(whole, whole, out_sems.at[j]).wait()
    for c in passes:
        c.wait()


def run_adamw(states, grads, passed):
    n = len(JOBS)
    state_specs = [VMEM] * 21
    new_specs = [ANY] * 15 + [VMEM] * 6
    return pl.pallas_call(
        adamw_kernel,
        out_shape=[jax.ShapeDtypeStruct(s.shape, F32) for s in (*states, *passed)],
        in_specs=state_specs + [ANY] * 5 + [VMEM] + [ANY] * 2,
        out_specs=new_specs + [ANY] * 2,
        scratch_shapes=[pltpu.VMEM((3, *s), F32) for s in SHAPES[0:5]]
        + [pltpu.VMEM(s, BF16) for s in SHAPES[0:5]]
        + [pltpu.SemaphoreType.DMA((k,)) for k in (n, n, 2)],
        compiler_params=pltpu.CompilerParams(vmem_limit_bytes=20 * 1024 * 1024),
        name="adamw",
    )(*states, *grads, *passed)


def local(inputs, cotangent, *state):
    rows = inputs.shape[1]
    flat = list(state)
    for i in (0, 1, 2):
        flat[i] = jnp.transpose(flat[i], (0, 2, 1)).reshape(192, D)
    for i in (12, 13, 14):
        flat[i] = flat[i].reshape(2 * D, D)
    operands = (inputs.reshape(rows, D), cotangent.reshape(rows, D), flat[15], flat[18])
    operands += tuple(flat[3 * i] for i in range(5))
    operands += tuple(flat[3 * i + k] for i in range(5) for k in (1, 2))
    results = run_layer(*(pltpu.with_memory_space_constraint(a, pltpu.HBM) for a in operands))
    mixed, ingrad, grads, kept = results[0], results[1], results[2:8], results[8:23]
    *new, mixed, ingrad = run_adamw([*kept, *flat[15:21]], grads, (mixed, ingrad))
    for i in (0, 1, 2):
        new[i] = jnp.transpose(new[i].reshape(3, 64, D), (0, 2, 1))
    for i in (12, 13, 14):
        new[i] = new[i].reshape(2, D, D)
    return (mixed.reshape(1, rows, D), ingrad.reshape(1, rows, D), *new)


def solution(mesh):
    batch = P("dp", "head", None)
    qkv = P(None, None, "head")
    first = P("head", None)
    second = P(None, "head")
    state = (qkv,) * 3 + (first,) * 3 + (second,) * 3 + (first,) * 3 + (P(),) * 9
    return jax.shard_map(
        local,
        mesh=mesh,
        in_specs=(batch, batch, *state),
        out_specs=(batch, batch, *state),
        check_vma=False,
    )
```

```python
import jax
import jax.numpy as jnp
from jax import lax
from jax.experimental import pallas as pl
from jax.experimental.pallas import tpu as pltpu
from jax.sharding import PartitionSpec as P

F32 = jnp.float32
BF16 = jnp.bfloat16
STEP = 10
NORM_EPS = 1e-05
BETA_ONE = 0.9
BETA_TWO = 0.999
ADAM_EPS = 1e-08
DECAY = 0.01
RATES = (0.04, 0.1, 0.04, 0.02, 0.04, 0.4, 0.3)
D = 512
ROWS = 128
LEN = 1024
QB = 256
NN = ((1,), (0,))
NT = ((1,), (1,))
TN = ((0,), (0,))


def dot(a, b, dims=NN):
    return lax.dot_general(a, b, (dims, ((), ())), preferred_element_type=F32)


def aligned(value, by):
    return pl.multiple_of(value, by)


class Group:
    def __init__(self, links, total, receives=1, each=None):
        self.send_sem, self.total = links.semaphore(), total
        self.each = total if each is None else each
        self.recv_sems = [links.semaphore() for _ in range(receives)]
        links.groups.append(self)

    def send(self, src, dst, device, k=0):
        pltpu.make_async_remote_copy(
            src_ref=src,
            dst_ref=dst,
            send_sem=self.send_sem,
            recv_sem=self.recv_sems[k],
            device_id=device,
            device_id_type=pl.DeviceIdType.MESH,
        ).start()

    def wait(self, k=0):
        pltpu.make_async_copy(self.each, self.each, self.recv_sems[k]).wait()


class Links:
    def __init__(self, sems):
        self.sems, self.used, self.groups = sems, 0, []

    def semaphore(self):
        self.used += 1
        return self.sems.at[self.used - 1]

    def drain(self):
        for g in self.groups:
            pltpu.make_async_copy(g.total, g.total, g.send_sem).wait()


N_SEMS = 140
N_LOCAL = 19


SHAPES = ((192, D), (64, D), (D, 256), (256, D), (2 * D, D), (2, D), (4, D))


def adamw(weight, first, second, grad, rate):
    first = BETA_ONE * first + (1.0 - BETA_ONE) * grad
    second = BETA_TWO * second + (1.0 - BETA_TWO) * grad * grad
    first_hat = first * (1.0 / (1.0 - BETA_ONE**STEP))
    second_hat = second * (1.0 / (1.0 - BETA_TWO**STEP))
    weight = weight - rate * (first_hat / (jnp.sqrt(second_hat) + ADAM_EPS) + DECAY * weight)
    return (weight, first, second)


SCRATCH = {
    "x_ref": ((ROWS, D), BF16),
    "dy_ref": ((ROWS, D), BF16),
    "gains_ref": ((2, D), F32),
    "biases_ref": ((4, D), F32),
    "x_all": ((LEN, D), BF16),
    "h1_all": ((LEN, D), BF16),
    "w_all": ((1536, D), BF16),
    "out_all": ((D, D), BF16),
    "up_all": ((D, 1024), BF16),
    "down_all": ((1024, D), BF16),
    "gate_low": ((2, D, D), BF16),
    "proj_t": ((192, LEN), BF16),
    "k_nat": ((LEN, 64), BF16),
    "v_nat": ((LEN, 64), BF16),
    "s_buf": ((LEN, QB), F32),
    "p_buf": ((LEN, QB), BF16),
    "ds_buf": ((LEN, QB), BF16),
    "o_t": ((64, LEN), F32),
    "o_low": ((64, LEN), BF16),
    "lse": ((1, LEN), F32),
    "heads_t": ((D, 256), BF16),
    "g1_buf": ((ROWS, D), F32),
    "attn_buf": ((ROWS, D), F32),
    "x1_buf": ((ROWS, D), F32),
    "xhat_buf": ((ROWS, D), F32),
    "rstd_buf": ((ROWS, 128), F32),
    "h2_pair": ((256, D), BF16),
    "g2_buf": ((ROWS, D), F32),
    "act_buf": ((256, 1024), BF16),
    "dgelu_buf": ((256, 1024), F32),
    "ffn_own": ((ROWS, D), F32),
    "ffn_send": ((ROWS, D), BF16),
    "ffn_recv": ((ROWS, D), BF16),
    "dffn_pair": ((256, D), BF16),
    "dz2_full": ((ROWS, D), BF16),
    "dz1_full": ((ROWS, D), BF16),
    "dattn_full": ((ROWS, D), BF16),
    "dz2_half": ((256, 256), BF16),
    "dattn_half": ((256, 256), BF16),
    "dhid_buf": ((256, 1024), BF16),
    "dh2_own": ((ROWS, D), F32),
    "dh2_send": ((ROWS, D), BF16),
    "dh2_recv": ((ROWS, D), BF16),
    "dh2_gate": ((ROWS, D), F32),
    "back_send": ((8, 128, ROWS), BF16),
    "back_t": ((128, LEN), BF16),
    "vec": ((8, D), F32),
    "vec_s": ((8, D), F32),
    "vec_a": ((8, 8, D), F32),
    "vec_b": ((8, 8, D), F32),
    "dq_t": ((64, LEN), F32),
    "dk_t": ((64, LEN), F32),
    "dv_t": ((64, LEN), F32),
    "dproj_low": ((256, LEN), BF16),
    "dproj_all": ((1536, ROWS), BF16),
    "gq_low": ((256, D), BF16),
    "gq_sib": ((256, 256), BF16),
    "gq_send": ((8, 64, 128), BF16),
    "gq_recv": ((8, 64, 128), BF16),
    "gq_all": ((256, D), BF16),
    "g1t_all": ((D, D), BF16),
    "g1_nat": ((D, D), F32),
    "g2_low": ((D, 256), BF16),
    "gy_recv": ((4, 128, 256), BF16),
    "gy_sum": ((128, 256), BF16),
    "gz_recv": ((4, 32, 256), BF16),
    "gz_sum": ((32, 256), BF16),
    "gx_recv": ((4, 32, 256), BF16),
    "g2_all": ((D, D), BF16),
    "gout_low": ((D, 256), BF16),
    "gout_recv": ((2, 8, 64, 256), BF16),
    "gout_sum": ((64, 256), BF16),
    "gout_all": ((64, D), BF16),
    "gup_all": ((D, 256), BF16),
    "gdown_all": ((256, D), BF16),
    "ua_s1": ((64, 32, 128), BF16),
    "ua_r1": ((48, 32, 128), BF16),
    "ua_s2": ((16, 32, 128), BF16),
    "ua_r2": ((12, 32, 128), BF16),
    "ua_s3": ((4, 32, 128), BF16),
    "ua_r3": ((3, 32, 128), BF16),
    "ub_s1": ((64, 32, 128), BF16),
    "ub_r1": ((48, 32, 128), BF16),
    "ub_s2": ((16, 32, 128), BF16),
    "ub_r2": ((12, 32, 128), BF16),
    "ub_s3": ((4, 32, 128), BF16),
    "ub_r3": ((3, 32, 128), BF16),
    "da_s1": ((64, 16, 256), BF16),
    "da_r1": ((48, 16, 256), BF16),
    "da_s2": ((16, 16, 256), BF16),
    "da_r2": ((12, 16, 256), BF16),
    "da_s3": ((4, 16, 256), BF16),
    "da_r3": ((3, 16, 256), BF16),
    "db_s1": ((64, 16, 256), BF16),
    "db_r1": ((48, 16, 256), BF16),
    "db_s2": ((16, 16, 256), BF16),
    "db_r2": ((12, 16, 256), BF16),
    "db_s3": ((4, 16, 256), BF16),
    "db_r3": ((3, 16, 256), BF16),
}


def layer_kernel(*refs):
    x_hbm, dy_hbm, gains_hbm, biases_hbm = refs[0:4]
    states, (mixed_ref, ingrad_ref, vec_ref), kept = refs[4:19], refs[19:22], refs[22:37]
    sems, local_sems = refs[-2:]
    (
        x_ref,
        dy_ref,
        gains_ref,
        biases_ref,
        x_all,
        h1_all,
        w_all,
        out_all,
        up_all,
        down_all,
        gate_low,
        proj_t,
        k_nat,
        v_nat,
        s_buf,
        p_buf,
        ds_buf,
        o_t,
        o_low,
        lse,
        heads_t,
        g1_buf,
        attn_buf,
        x1_buf,
        xhat_buf,
        rstd_buf,
        h2_pair,
        g2_buf,
        act_buf,
        dgelu_buf,
        ffn_own,
        ffn_send,
        ffn_recv,
        dffn_pair,
        dz2_full,
        dz1_full,
        dattn_full,
        dz2_half,
        dattn_half,
        dhid_buf,
        dh2_own,
        dh2_send,
        dh2_recv,
        dh2_gate,
        back_send,
        back_t,
        vec,
        vec_s,
        vec_a,
        vec_b,
        dq_t,
        dk_t,
        dv_t,
        dproj_low,
        dproj_all,
        gq_low,
        gq_sib,
        gq_send,
        gq_recv,
        gq_all,
        g1t_all,
        g1_nat,
        g2_low,
        gy_recv,
        gy_sum,
        gz_recv,
        gz_sum,
        gx_recv,
        g2_all,
        gout_low,
        gout_recv,
        gout_sum,
        gout_all,
        gup_all,
        gdown_all,
        *part_refs,
    ) = refs[37:-2]
    pairs = [(x_hbm, x_ref)] + [(states[i], kept[i]) for i in (0, 3, 6, 9)]
    pairs += [(gains_hbm, gains_ref), (biases_hbm, biases_ref), (states[12], kept[12])]
    pairs += [(dy_hbm, dy_ref)]
    pairs += [(states[i], kept[i]) for i in range(15) if i % 3]
    loads = [
        pltpu.make_async_copy(src, dst, local_sems.at[i]) for i, (src, dst) in enumerate(pairs)
    ]
    for load in loads[0:9]:
        load.start()

    dp, head = lax.axis_index("dp"), lax.axis_index("head")
    x_hi, y, core = dp // 8, (dp // 2) % 4, dp % 2
    z, x_lo = head // 2, head % 2
    xx = x_hi * 2 + x_lo
    sub = x_hi * 4 + y
    links = Links(sems)

    def head_peer(o):
        return (head + o) % 8

    def in_head(o):
        return (dp, (head + o) % 8)

    def head_from(o):
        return (head + 8 - o) % 8

    def sub_peer(o):
        return (sub + o) % 8

    def in_sub(o):
        return (((sub + o) % 8) * 2 + core, head)

    def ring(axis, o):
        nx = (xx + o) % 4 if axis == "x" else xx
        ny = (y + o) % 4 if axis == "y" else y
        nz = (z + o) % 4 if axis == "z" else z
        return ((nx // 2) * 8 + ny * 2 + core, nz * 2 + nx % 2)

    sibling = (sub * 2 + (1 - core), head)

    barrier = pltpu.get_barrier_semaphore()
    greeted = [in_head(o) for o in range(1, 8)] + [in_sub(o) for o in range(1, 8)]
    greeted += [sibling, ((1 - x_hi) * 8 + y * 2 + core, z * 2 + 1 - x_lo)]
    for device in greeted:
        pl.semaphore_signal(
            barrier, inc=1, device_id=device, device_id_type=pl.DeviceIdType.MESH
        )

    own = pl.ds(aligned(head * ROWS, ROWS), ROWS)
    own_core = pl.ds(aligned(core * ROWS, ROWS), ROWS)
    sib_core = pl.ds(aligned((1 - core) * ROWS, ROWS), ROWS)
    half = pl.ds(aligned(core * 256, 256), 256)
    sib_half = pl.ds(aligned((1 - core) * 256, 256), 256)
    own_heads = pl.ds(aligned(head * 64, 64), 64)
    own_w = pl.ds(aligned(head * 192, 64), 192)
    sub_rows = pl.ds(aligned(sub * 128, 128), 128)

    for load in loads[0:5]:
        load.wait()
    x_all[own, :] = x_ref[...]
    w_all[own_w, :] = kept[0][...].astype(BF16)
    out_all[own_heads, :] = kept[3][...].astype(BF16)
    up_all[:, own] = kept[6][:, own_core].astype(BF16)
    down_all[own, :] = kept[9][own_core, :].astype(BF16)

    def rows_of(ref, first, unit):
        def at(s):
            parts = ((0, unit), (0, unit // 2), (unit // 2, unit // 2))
            return [ref.at[pl.ds(aligned(first(s) + a, unit // 2), n), :] for a, n in parts]

        return at

    def up_at(s):
        cols = pl.ds(aligned(s * 128, 128), 128)
        first = (y % 2) * 256
        parts = ((0, 256), (0, 128), (128, 128))
        return [up_all.at[pl.ds(aligned(first + a, 128), n), cols] for a, n in parts]

    class Spread:
        def __init__(self, at, three, four, seven=None, last=None):
            self.at, self.last, self.one = at, last, at(head)[0]
            self.ring_z = Group(links, three, 3, self.one)
            self.over_x = Group(links, four)
            self.over_last = None if last is None else Group(links, seven)

        def begin(self):
            for o in range(1, 4):
                self.ring_z.send(self.one, self.one, ring("z", o), o - 1)

        def forward(self, s):
            _, first, second = self.at(s)
            self.over_x.send(first, first, ring("x", 1))
            self.over_x.send(second, second, ring("x", 3))

        def pass_on(self):
            for o in range(1, 4):
                self.ring_z.wait(o - 1)
                s = ((z + 4 - o) % 4) * 2 + x_lo
                self.forward(s)
                if self.last is not None:
                    self.last(self.over_last, *self.at(s))

        def pass_last(self):
            self.over_x.wait()
            for o in range(4):
                self.last(self.over_last, *self.at(((z + o) % 4) * 2 + 1 - x_lo))

    def to_sibling(group, whole, first, second):
        group.send(whole, whole, sibling)

    def to_both_y(group, whole, first, second):
        group.send(first, first, ring("y", 1))
        group.send(second, second, ring("y", 3))

    spread_out = Spread(
        rows_of(out_all, lambda s: s * 64 + core * 32, 32),
        out_all.at[0:96, :],
        out_all.at[0:128, :],
        out_all.at[0:224, :],
        to_sibling,
    )
    spread_up = Spread(
        up_at,
        up_all.at[0:256, 0:384],
        up_all.at[0:256, 0:512],
        up_all.at[0:256, 0:896],
        to_both_y,
    )
    spread_down = Spread(
        rows_of(down_all, lambda s: s * 128 + (y % 2) * 64, 64),
        down_all.at[0:192, :],
        down_all.at[0:256, :],
        down_all.at[0:448, :],
        to_both_y,
    )
    spread_w = Spread(
        rows_of(w_all, lambda s: s * 192 + core * 96, 96),
        w_all.at[0:288, :],
        w_all.at[0:384, :],
        w_all.at[0:672, :],
        to_sibling,
    )
    x_group = Group(links, x_all.at[0 : 7 * ROWS, :], 7, x_ref)

    pl.semaphore_wait(barrier, len(greeted))
    beside = (dp, z * 2 + 1 - x_lo)
    for o in range(1, 4):
        x_group.send(x_ref, x_all.at[own, :], ring("z", o), o - 1)
    x_group.send(x_ref, x_all.at[own, :], beside, 3)
    spread_out.forward(head)
    spread_up.forward(head)
    spread_down.forward(head)
    for load in loads[9:19]:
        load.start()

    for load in loads[5:9]:
        load.wait()
    for i in range(2):
        gate_low[i] = kept[12][D * i : D * i + D, :].astype(BF16)
    gain_one, shift_one = gains_ref[0:1, :], biases_ref[0:1, :]
    gain_two, shift_two = gains_ref[1:2, :], biases_ref[1:2, :]

    def project(block):
        for s in range(4):
            rows = pl.ds(aligned(block * ROWS + 32 * s, 32), 32)
            v = x_all[rows, :].astype(F32)
            center = v - jnp.mean(v, axis=-1, keepdims=True)
            spread = jnp.mean(center * center, axis=-1, keepdims=True)
            h = center * lax.rsqrt(spread + NORM_EPS) * gain_one + shift_one
            h1_all[rows, :] = h.astype(BF16)
        rows = pl.ds(aligned(block * ROWS, ROWS), ROWS)
        pt = dot(w_all[own_w, :], h1_all[rows, :], NT)
        proj_t[0:64, rows] = (pt[0:64].astype(BF16).astype(F32) * 0.125).astype(BF16)
        proj_t[64:192, rows] = pt[64:192].astype(BF16)
        k_nat[rows, :] = pt[64:128].T.astype(BF16)
        v_nat[rows, :] = pt[128:192].T.astype(BF16)

    def from_z(o):
        return ((z + 4 - o) % 4) * 2

    project(head)
    x_group.wait(3)
    block = x_all.at[pl.ds(aligned((z * 2 + 1 - x_lo) * ROWS, ROWS), ROWS), :]
    x_group.send(block, block, ring("z", 1), 4)
    x_group.send(block, block, ring("z", 3), 5)
    spread_out.begin()
    spread_up.begin()
    spread_down.begin()
    project(z * 2 + 1 - x_lo)
    x_group.wait(0)
    project(from_z(1) + x_lo)
    x_group.wait(2)
    project(from_z(3) + x_lo)
    x_group.wait(1)
    block = x_all.at[pl.ds(aligned((from_z(2) + x_lo) * ROWS, ROWS), ROWS), :]
    x_group.send(block, block, beside, 6)
    project(from_z(2) + x_lo)
    spread_out.pass_on()
    x_group.wait(4)
    project(from_z(1) + 1 - x_lo)
    x_group.wait(5)
    project(from_z(3) + 1 - x_lo)
    x_group.wait(6)
    project(from_z(2) + 1 - x_lo)

    for j in range(LEN // QB):
        cols = slice(QB * j, QB * (j + 1))
        queries = proj_t[0:64, cols]
        ceiling = jnp.full((1, QB), -1e30, F32)
        tiles = QB * (j + 1) // ROWS
        for t in range(tiles):
            s = dot(k_nat[ROWS * t : ROWS * (t + 1), :], queries)
            if ROWS * t >= QB * j:
                keys_at = lax.broadcasted_iota(jnp.int32, (ROWS, QB), 0) + ROWS * t
                queries_at = lax.broadcasted_iota(jnp.int32, (ROWS, QB), 1) + QB * j
                s = jnp.where(keys_at <= queries_at, s, -1e30)
            s_buf[ROWS * t : ROWS * (t + 1), :] = s
            ceiling = jnp.maximum(ceiling, jnp.max(s, axis=0, keepdims=True))
        mass = jnp.zeros((1, QB), F32)
        for t in range(tiles):
            e = jnp.exp(s_buf[ROWS * t : ROWS * (t + 1), :] - ceiling)
            mass = mass + jnp.sum(e, axis=0, keepdims=True)
            p_buf[ROWS * t : ROWS * (t + 1), :] = e.astype(BF16)
        total = dot(proj_t[128:192, 0 : QB * (j + 1)], p_buf[0 : QB * (j + 1), :])
        total = total / mass
        o_t[:, cols] = total
        o_low[:, cols] = total.astype(BF16)
        lse[:, cols] = ceiling + jnp.log(mass)
    heads_group = Group(links, heads_t.at[0:448, 0:ROWS])
    for o in range(1, 8):
        block = o_low.at[:, pl.ds(aligned(head_peer(o) * ROWS, ROWS), ROWS)]
        heads_group.send(block, heads_t.at[own_heads, own_core], in_head(o))
    heads_t[own_heads, own_core] = o_low[:, own]

    g1_buf[...] = dot(h1_all[own, :], gate_low[0]) + biases_ref[2:3, :]
    spread_w.begin()
    spread_w.forward(head)
    spread_out.pass_last()
    spread_up.pass_on()
    spread_down.pass_on()
    spread_up.pass_last()
    heads_group.wait()
    headst_group = Group(links, heads_t.at[:, 0:ROWS])
    headst_group.send(heads_t.at[:, own_core], heads_t.at[:, own_core], sibling)
    spread_out.over_last.wait()
    attn_buf[...] = dot(heads_t[:, own_core], out_all[...], TN)
    for s in range(4):
        rows = slice(32 * s, 32 * s + 32)
        g1 = jax.nn.sigmoid(g1_buf[rows, :])
        g1_buf[rows, :] = g1
        x = x_ref[rows, :].astype(F32)
        x1 = g1 * attn_buf[rows, :] + (1.0 - g1) * x
        x1_buf[rows, :] = x1
        center = x1 - jnp.mean(x1, axis=-1, keepdims=True)
        spread = jnp.mean(center * center, axis=-1, keepdims=True)
        rstd = lax.rsqrt(spread + NORM_EPS)
        xhat = center * rstd
        xhat_buf[rows, :] = xhat
        rstd_buf[rows, :] = jnp.broadcast_to(rstd, (32, 128))
        h2 = xhat * gain_two + shift_two
        h2_pair[pl.ds(aligned(core * ROWS + 32 * s, 32), 32), :] = h2.astype(BF16)
    h2_group = Group(links, h2_pair.at[0:ROWS, :])
    h2_group.send(h2_pair.at[own_core, :], h2_pair.at[own_core, :], sibling)
    g2_buf[...] = dot(h2_pair[own_core, :], gate_low[1]) + biases_ref[3:4, :]
    spread_down.pass_last()
    spread_up.over_last.wait()
    h2_group.wait()
    for n in range(4):
        cols = slice(256 * n, 256 * n + 256)
        u = dot(h2_pair[...], up_all[:, cols])
        c0 = 0.7978845608028654
        inner = jnp.tanh(c0 * (u + 0.044715 * u * u * u))
        act_buf[:, cols] = (0.5 * u * (1.0 + inner)).astype(BF16)
        dgelu_buf[:, cols] = 0.5 * (1.0 + inner) + 0.5 * u * (1.0 - inner * inner) * c0 * (
            1.0 + 3.0 * 0.044715 * u * u
        )
    spread_down.over_last.wait()
    ffn_send[...] = dot(act_buf[sib_core, :], down_all[...]).astype(BF16)
    ffn_group = Group(links, ffn_recv)
    ffn_group.send(ffn_send, ffn_recv, sibling)
    spread_w.pass_on()
    ffn_own[...] = dot(act_buf[own_core, :], down_all[...])
    ffn_group.wait()
    bias_two = jnp.zeros((1, D), F32)
    for s in range(4):
        rows = slice(32 * s, 32 * s + 32)
        ffn = ffn_own[rows, :] + ffn_recv[rows, :].astype(F32)
        g2 = jax.nn.sigmoid(g2_buf[rows, :])
        g2_buf[rows, :] = g2
        x1 = x1_buf[rows, :]
        dy = dy_ref[rows, :].astype(F32)
        mixed_ref[rows, :] = g2 * ffn + (1.0 - g2) * x1
        dffn_pair[pl.ds(aligned(core * ROWS + 32 * s, 32), 32), :] = (g2 * dy).astype(BF16)
        dz = (dy * (ffn - x1) * g2 * (1.0 - g2)).astype(BF16)
        dz2_full[rows, :] = dz
        bias_two = bias_two + jnp.sum(dz.astype(F32), axis=0, keepdims=True)
    dffn_group = Group(links, dffn_pair.at[0:ROWS, :])
    dffn_group.send(dffn_pair.at[own_core, :], dffn_pair.at[own_core, :], sibling)
    dz2_group = Group(links, dz2_half.at[0:ROWS, :])
    dz2_group.send(dz2_full.at[:, sib_half], dz2_half.at[own_core, :], sibling)
    dz2_half[own_core, :] = dz2_full[:, half]
    dh2_gate[...] = dot(dz2_full[...], gate_low[1], NT)

    place = {"x": xx, "y": y, "z": z}

    class Staged:
        def __init__(self, axes, refs):
            self.axes, self.refs, self.step, self.group = axes, refs, 0, None

        def put(self, ch, value):
            a, b, c = (ch[axis] for axis in self.axes)
            self.refs[0][a * 16 + b * 4 + c] = value

        def send(self):
            axis, size = self.axes[self.step], (16, 4, 1)[self.step]
            src, got = self.refs[2 * self.step : 2 * self.step + 2]
            self.group = Group(links, got)
            for o in range(1, 4):
                t = (place[axis] + o) % 4
                block = got.at[pl.ds((o - 1) * size, size)]
                self.group.send(src.at[pl.ds(t * size, size)], block, ring(axis, o))

        def add(self, store=None):
            at, size = place[self.axes[self.step]], (16, 4, 1)[self.step]
            src, got = self.refs[2 * self.step : 2 * self.step + 2]
            self.group.wait()
            self.step += 1
            to = None if store else self.refs[2 * self.step]

            def one(i):
                total = src[at * size + i].astype(F32)
                for o in range(3):
                    total = total + got[o * size + i].astype(F32)
                return total.astype(BF16)

            if store:
                store(one(0))
                return

            def body(i, carry):
                to[i] = one(i)
                return carry

            lax.fori_loop(0, size, body, 0)

        def next(self):
            self.add()
            self.send()

    up_a, up_b, down_a, down_b = (
        Staged(axes, part_refs[6 * i : 6 * i + 6])
        for i, axes in enumerate(("yzx", "xyz", "yxz", "zxy"))
    )

    dz2_group.wait()
    g2_low[...] = dot(h2_pair[...], dz2_half[...], TN).astype(BF16)
    g2_group = Group(links, gy_recv.at[0:3])
    for o in range(1, 4):
        block = g2_low.at[pl.ds(aligned(((y + o) % 4) * 128, 128), 128), :]
        g2_group.send(block, gy_recv.at[y], ring("y", o))
    gy_recv[y] = g2_low[pl.ds(aligned(y * 128, 128), 128), :]

    dffn_group.wait()
    def chip_of(h, g):
        return {"x": (g // 4) * 2 + h % 2, "y": g % 4, "z": h // 2}

    for h in range(8):
        gd = dot(act_buf[:, 128 * h : 128 * h + 128], dffn_pair[...], TN).astype(BF16)
        for g in range(8):
            down_a.put(chip_of(h, g), gd[16 * g : 16 * g + 16, 0:256])
            down_b.put(chip_of(h, g), gd[16 * g : 16 * g + 16, 256:512])
    down_a.send()
    for n in range(4):
        cols = slice(256 * n, 256 * n + 256)
        da = dot(dffn_pair[...], down_all[cols, :], NT)
        dhid_buf[:, cols] = (da * dgelu_buf[:, cols]).astype(BF16)
    dh2_send[...] = dot(dhid_buf[sib_core, :], up_all[...], NT).astype(BF16)
    dh2_group = Group(links, dh2_recv)
    dh2_group.send(dh2_send, dh2_recv, sibling)
    for h in range(8):
        gu = dot(h2_pair[...], dhid_buf[:, 128 * h : 128 * h + 128], TN).astype(BF16)
        for g in range(8):
            up_a.put(chip_of(h, g), gu[64 * g : 64 * g + 32, :])
            up_b.put(chip_of(h, g), gu[64 * g + 32 : 64 * g + 64, :])
    up_a.send()
    dh2_own[...] = dot(dhid_buf[own_core, :], up_all[...], NT)
    dh2_group.wait()
    gain_sum = jnp.zeros((1, D), F32)
    shift_sum = jnp.zeros((1, D), F32)
    bias_one = jnp.zeros((1, D), F32)
    for s in range(4):
        rows = slice(32 * s, 32 * s + 32)
        dh2 = dh2_own[rows, :] + dh2_recv[rows, :].astype(F32) + dh2_gate[rows, :]
        xhat = xhat_buf[rows, :]
        gain_sum = gain_sum + jnp.sum(dh2 * xhat, axis=0, keepdims=True)
        shift_sum = shift_sum + jnp.sum(dh2, axis=0, keepdims=True)
        dxhat = dh2 * gain_two
        mean_a = jnp.mean(dxhat, axis=-1, keepdims=True)
        mean_b = jnp.mean(dxhat * xhat, axis=-1, keepdims=True)
        rstd = rstd_buf[rows, 0:1]
        dx1 = (1.0 - g2_buf[rows, :]) * dy_ref[rows, :].astype(F32) + rstd * (
            dxhat - mean_a - xhat * mean_b
        )
        g1 = g1_buf[rows, :]
        dattn_full[rows, :] = (g1 * dx1).astype(BF16)
        x = x_ref[rows, :].astype(F32)
        dz = (dx1 * (attn_buf[rows, :] - x) * g1 * (1.0 - g1)).astype(BF16)
        dz1_full[rows, :] = dz
        bias_one = bias_one + jnp.sum(dz.astype(F32), axis=0, keepdims=True)
        ingrad_ref[rows, :] = (1.0 - g1) * dx1
    vec[1:2, :] = gain_sum
    vec[3:4, :] = shift_sum
    vec[4:5, :] = bias_one
    vec[5:6, :] = bias_two
    vec[6:8, :] = jnp.zeros((2, D), F32)

    dheads = dot(out_all[...], dattn_full[...], NT).astype(BF16)
    dz1_t = dz1_full[...].astype(F32).T.astype(BF16)
    for h in range(8):
        back_send[h, 0:64, :] = dheads[64 * h : 64 * h + 64, :]
        back_send[h, 64:128, :] = dz1_t[64 * h : 64 * h + 64, :]
    back_group = Group(links, back_t.at[:, 0 : 7 * ROWS])
    for o in range(1, 8):
        back_group.send(back_send.at[head_peer(o)], back_t.at[:, own], in_head(o))
    back_t[:, own] = back_send[head]
    dattn_group = Group(links, dattn_half.at[0:ROWS, :])
    dattn_group.send(dattn_full.at[:, sib_half], dattn_half.at[own_core, :], sibling)
    dattn_half[own_core, :] = dattn_full[:, half]
    down_b.send()
    up_b.send()

    headst_group.wait()
    dattn_group.wait()
    gout_low[...] = dot(heads_t[...], dattn_half[...]).astype(BF16)

    def add_slots(ref, n=8):
        total = ref[0].astype(F32)
        for o in range(1, n):
            total = total + ref[o].astype(F32)
        return total

    g2_group.wait()
    gy_sum[...] = add_slots(gy_recv, 4).astype(BF16)
    g2_group = Group(links, gz_recv.at[0:3])
    for o in range(1, 4):
        block = gy_sum.at[pl.ds(aligned(((z + o) % 4) * 32, 32), 32), :]
        g2_group.send(block, gz_recv.at[z], ring("z", o))
    gz_recv[z] = gy_sum[pl.ds(aligned(z * 32, 32), 32), :]

    back_group.wait()
    dk_t[...] = jnp.zeros_like(dk_t)
    dv_t[...] = jnp.zeros_like(dv_t)
    for j in range(LEN // QB):
        cols = slice(QB * j, QB * (j + 1))
        upto = QB * (j + 1)
        queries = proj_t[0:64, cols]
        grads = back_t[0:64, cols]
        delta = jnp.sum(o_t[:, cols] * grads.astype(F32), axis=0, keepdims=True)
        row_lse = lse[:, cols]
        for t in range(upto // ROWS):
            keys = slice(ROWS * t, ROWS * (t + 1))
            p = jnp.exp(dot(k_nat[keys, :], queries) - row_lse)
            if ROWS * t >= QB * j:
                keys_at = lax.broadcasted_iota(jnp.int32, (ROWS, QB), 0) + ROWS * t
                queries_at = lax.broadcasted_iota(jnp.int32, (ROWS, QB), 1) + QB * j
                p = jnp.where(keys_at <= queries_at, p, 0.0)
            d = dot(v_nat[keys, :], grads)
            p_buf[keys, :] = p.astype(BF16)
            ds_buf[keys, :] = (p * (d - delta)).astype(BF16)
        dq_t[:, cols] = dot(proj_t[64:128, 0:upto], ds_buf[0:upto, :]) * 0.125
        dk_t[:, 0:upto] += dot(queries, ds_buf[0:upto, :], NT)
        dv_t[:, 0:upto] += dot(grads, p_buf[0:upto, :], NT)
    dproj_low[0:64, :] = dq_t[...].astype(BF16)
    dproj_low[64:128, :] = dk_t[...].astype(BF16)
    dproj_low[128:192, :] = dv_t[...].astype(BF16)
    dproj_low[192:256, :] = back_t[64:128, :]
    dproj_group = Group(links, dproj_all.at[0 : 7 * 192, :])
    for o in range(1, 8):
        block = dproj_low.at[0:192, pl.ds(aligned(head_peer(o) * ROWS, ROWS), ROWS)]
        dproj_group.send(block, dproj_all.at[own_w, :], in_head(o))
    dproj_all[own_w, :] = dproj_low[0:192, own]

    gq_low[...] = dot(dproj_low[...], h1_all[...]).astype(BF16)
    gq_pair = Group(links, gq_sib)
    gq_pair.send(gq_low.at[:, sib_half], gq_sib, sibling)

    gout_group = Group(links, gout_recv.at[0, 0:7])
    for o in range(1, 8):
        block = gout_low.at[pl.ds(aligned(head_peer(o) * 64, 64), 64), :]
        gout_group.send(block, gout_recv.at[0, head], in_head(o))
    gout_recv[0, head] = gout_low[own_heads, :]

    down_a.next()
    gq_pair.wait()
    total = gq_low[:, half].astype(F32) + gq_sib[...].astype(F32)
    for i in range(8):
        r, c = 64 * (i // 2), 128 * (i % 2)
        gq_send[i] = total[r : r + 64, c : c + 128].astype(BF16)
    gq_group = Group(links, gq_recv.at[0:7])
    for o in range(1, 8):
        gq_group.send(gq_send.at[sub_peer(o)], gq_recv.at[sub], in_sub(o))
    gq_recv[sub] = gq_send[sub]

    down_b.next()
    up_b.next()

    g2_group.wait()
    gz_sum[...] = add_slots(gz_recv, 4).astype(BF16)
    g2_group = Group(links, gx_recv.at[0:3])
    for o in range(1, 4):
        g2_group.send(gz_sum, gx_recv.at[xx], ring("x", o))
    gx_recv[xx] = gz_sum[...]
    spread_w.pass_last()
    up_a.next()


    gq_group.wait()
    gq_rows = pl.ds(aligned((sub // 2) * 64, 64), 64)
    gq_cols = pl.ds(aligned(core * 256 + (sub % 2) * 128, 128), 128)
    gq_all[gq_rows, gq_cols] = add_slots(gq_recv).astype(BF16)
    gq_group = Group(links, gq_recv.at[0:7])
    for o in range(1, 8):
        block = gq_all.at[gq_rows, gq_cols]
        gq_group.send(block, block, in_sub(o))

    g2_group.wait()
    g2_rows = pl.ds(aligned(y * 128 + z * 32, 32), 32)
    g2_all[g2_rows, half] = add_slots(gx_recv, 4).astype(BF16)
    g2_group = Group(links, gz_recv.at[0:3])
    for o in range(1, 4):
        block = g2_all.at[g2_rows, half]
        g2_group.send(block, block, ring("z", o))

    dproj_group.wait()
    spread_w.over_last.wait()
    dh2_own[...] = dot(dproj_all[...], w_all[...], TN) + dot(dz1_full[...], gate_low[0], NT)
    gain_sum = jnp.zeros((1, D), F32)
    shift_sum = jnp.zeros((1, D), F32)
    for s in range(4):
        rows = slice(32 * s, 32 * s + 32)
        v = x_ref[rows, :].astype(F32)
        center = v - jnp.mean(v, axis=-1, keepdims=True)
        spread = jnp.mean(center * center, axis=-1, keepdims=True)
        rstd = lax.rsqrt(spread + NORM_EPS)
        xhat = center * rstd
        dh = dh2_own[rows, :]
        gain_sum = gain_sum + jnp.sum(dh * xhat, axis=0, keepdims=True)
        shift_sum = shift_sum + jnp.sum(dh, axis=0, keepdims=True)
        dxhat = dh * gain_one
        mean_a = jnp.mean(dxhat, axis=-1, keepdims=True)
        mean_b = jnp.mean(dxhat * xhat, axis=-1, keepdims=True)
        ingrad_ref[rows, :] += rstd * (dxhat - mean_a - xhat * mean_b)
    vec[0:1, :] = gain_sum
    vec[2:3, :] = shift_sum
    vec_group = Group(links, vec_s)
    vec_group.send(vec, vec_s, sibling)

    def update(i, grad):
        rows, cols = SHAPES[i]
        step = 16 if cols == D else 32

        def strip(n, carry):
            at = pl.ds(aligned(n * step, step), step)
            refs = kept[3 * i : 3 * i + 3]
            new = adamw(*(r[at, :] for r in refs), grad[at, :].astype(F32), RATES[i])
            for r, value in zip(refs, new):
                r[at, :] = value
            return carry

        lax.fori_loop(0, rows // step, strip, 0)

    def update_gate(first, grad):
        def strip(n, carry):
            at = pl.ds(aligned(n * 16, 16), 16)
            into = pl.ds(aligned(first + n * 16, 16), 16)
            refs = kept[12:15]
            new = adamw(*(r[into, :] for r in refs), grad[at, :].astype(F32), RATES[4])
            for r, value in zip(refs, new):
                r[into, :] = value
            return carry

        lax.fori_loop(0, D // 16, strip, 0)

    for load in loads[9:19]:
        load.wait()

    down_a.next()
    down_b.next()
    up_b.next()
    gout_group.wait()
    gout_sum[...] = add_slots(gout_recv.at[0]).astype(BF16)
    gout_group = Group(links, gout_recv.at[1, 0:7])
    for o in range(1, 8):
        gout_group.send(gout_sum, gout_recv.at[1, sub], in_sub(o))
    gout_recv[1, sub] = gout_sum[...]

    vec_group.wait()
    vec_a[sub] = vec[...] + vec_s[...]
    vec_group = Group(links, vec_a.at[0:7])
    for o in range(1, 8):
        vec_group.send(vec_a.at[sub], vec_a.at[sub], in_sub(o))

    up_a.next()

    g2_group.wait()
    g2_group = Group(links, gy_recv.at[0:3])
    block = g2_all.at[pl.ds(aligned(y * 128, 128), 128), half]
    for o in range(1, 4):
        g2_group.send(block, block, ring("y", o))

    gq_group.wait()
    gq_pair = Group(links, gq_sib.at[0:192, :])
    gq_pair.send(gq_all.at[0:192, half], gq_all.at[0:192, half], sibling)
    g1_group = Group(links, g1t_all.at[0:448, 0:256])
    for o in range(1, 8):
        g1_group.send(gq_all.at[192:256, half], g1t_all.at[own_heads, half], in_head(o))
    g1t_all[own_heads, half] = gq_all[192:256, half]

    vec_group.wait()
    vec_b[head] = add_slots(vec_a)
    vec_group = Group(links, vec_b.at[0:7])
    for o in range(1, 8):
        vec_group.send(vec_b.at[head], vec_b.at[head], in_head(o))

    up_rows = pl.ds(aligned(sub * 64, 64), 64)
    down_rows = pl.ds(aligned(core * 128 + sub * 16, 16), 16)

    def to_down(cols):
        def store(value):
            gdown_all[down_rows, cols] = value

        return store

    def to_up(first):
        def store(value):
            gup_all[pl.ds(aligned(sub * 64 + first, 32), 32), own_core] = value

        return store

    down_a.add(to_down(slice(0, 256)))
    down_b.add(to_down(slice(256, 512)))
    down_group = Group(links, gdown_all.at[0:112, :])
    for o in range(1, 8):
        block = gdown_all.at[down_rows, :]
        down_group.send(block, block, in_sub(o))
    up_b.add(to_up(32))
    up_a.add(to_up(0))
    up_group = Group(links, gup_all.at[0:448, 0:128])
    for o in range(1, 8):
        block = gup_all.at[up_rows, own_core]
        up_group.send(block, block, in_sub(o))
    gout_group.wait()
    gout_all[:, half] = add_slots(gout_recv.at[1]).astype(BF16)
    gout_pair = Group(links, gout_sum)
    gout_pair.send(gout_all.at[:, half], gout_all.at[:, half], sibling)

    gq_pair.wait()
    update(0, gq_all)
    gout_pair.wait()
    update(1, gout_all)
    g2_group.wait()
    g2_pair = Group(links, g2_low)
    g2_pair.send(g2_all.at[:, half], g2_all.at[:, half], sibling)
    g1_group.wait()
    g1_pair = Group(links, g2_low)
    g1_pair.send(g1t_all.at[:, half], g1t_all.at[:, half], sibling)
    g2_pair.wait()
    update_gate(D, g2_all)
    down_group.wait()
    down_pair = Group(links, gdown_all.at[0:128, :])
    down_pair.send(gdown_all.at[own_core, :], gdown_all.at[own_core, :], sibling)
    up_group.wait()
    up_pair = Group(links, gup_all.at[:, 0:128])
    up_pair.send(gup_all.at[:, own_core], gup_all.at[:, own_core], sibling)
    g1_pair.wait()
    for n in range(4):
        at = slice(128 * n, 128 * n + 128)
        g1_nat[at, :] = g1t_all[:, at].astype(F32).T
    update_gate(0, g1_nat)
    down_pair.wait()
    update(3, gdown_all)
    up_pair.wait()
    update(2, gup_all)
    vec_group.wait()
    vec_ref[...] = add_slots(vec_b)
    links.drain()


VMEM = pl.BlockSpec(memory_space=pltpu.VMEM)
ANY = pl.BlockSpec(memory_space=pl.ANY)
HBM = pl.BlockSpec(memory_space=pltpu.HBM)


def run_layer(*args):
    in_vmem = [pltpu.VMEM(s, F32) for s in SHAPES[0:5] for _ in range(3)]
    shapes = [pltpu.VMEM(s, F32) for s in ((ROWS, D), (ROWS, D), (8, D))]
    return pl.pallas_call(
        layer_kernel,
        out_shape=shapes + in_vmem,
        in_specs=[HBM] * 19,
        out_specs=[VMEM] * 18,
        scratch_shapes=[pltpu.VMEM(s, t) for s, t in SCRATCH.values()]
        + [pltpu.SemaphoreType.DMA((N_SEMS,)), pltpu.SemaphoreType.DMA((N_LOCAL,))],
        compiler_params=pltpu.CompilerParams(
            collective_id=0, has_side_effects=True, vmem_limit_bytes=40 * 1024 * 1024
        ),
        name="layer",
    )(*args)


def finish_kernel(*refs):
    results, small, vec = refs[0:17], refs[17:23], refs[23]
    outs, new_small, sems = refs[24:41], refs[41:47], refs[47]
    copies = [
        pltpu.make_async_copy(a, b, sems.at[i]) for i, (a, b) in enumerate(zip(results, outs))
    ]
    for c in copies:
        c.start()
    for i, (lo, hi) in enumerate(((0, 2), (2, 6))):
        at = slice(3 * i, 3 * i + 3)
        for ref, value in zip(
            new_small[at], adamw(*(r[...] for r in small[at]), vec[lo:hi, :], RATES[5 + i])
        ):
            ref[...] = value
    for c in copies:
        c.wait()


def finish(results, small, vec):
    return pl.pallas_call(
        finish_kernel,
        out_shape=[jax.ShapeDtypeStruct(a.shape, F32) for a in (*results, *small)],
        in_specs=[VMEM] * 24,
        out_specs=[ANY] * 17 + [VMEM] * 6,
        scratch_shapes=[pltpu.SemaphoreType.DMA((17,))],
        compiler_params=pltpu.CompilerParams(vmem_limit_bytes=4 * 1024 * 1024),
        name="finish",
    )(*results, *small, vec)


def local(inputs, cotangent, *state):
    rows = inputs.shape[1]
    flat = list(state)
    for i in (0, 1, 2):
        flat[i] = jnp.transpose(flat[i], (0, 2, 1)).reshape(192, D)
    for i in (12, 13, 14):
        flat[i] = flat[i].reshape(2 * D, D)
    operands = (inputs.reshape(rows, D), cotangent.reshape(rows, D), flat[15], flat[18])
    operands += tuple(flat[0:15])
    mixed, ingrad, vec, *new = run_layer(
        *(pltpu.with_memory_space_constraint(a, pltpu.HBM) for a in operands)
    )
    mixed, ingrad, *new = finish((mixed, ingrad, *new), flat[15:21], vec)
    for i in (0, 1, 2):
        new[i] = jnp.transpose(new[i].reshape(3, 64, D), (0, 2, 1))
    for i in (12, 13, 14):
        new[i] = new[i].reshape(2, D, D)
    return (mixed.reshape(1, rows, D), ingrad.reshape(1, rows, D), *new)


def solution(mesh):
    batch = P("dp", "head", None)
    qkv = P(None, None, "head")
    first = P("head", None)
    second = P(None, "head")
    state = (qkv,) * 3 + (first,) * 3 + (second,) * 3 + (first,) * 3 + (P(),) * 9
    return jax.shard_map(
        local,
        mesh=mesh,
        in_specs=(batch, batch, *state),
        out_specs=(batch, batch, *state),
        check_vma=False,
    )
```

```python
import jax
import jax.numpy as jnp
from jax import lax
from jax.experimental import pallas as pl
from jax.experimental.pallas import tpu as pltpu
from jax.sharding import PartitionSpec as P

F32 = jnp.float32
BF16 = jnp.bfloat16
STEP = 10
NORM_EPS = 1e-05
BETA_ONE = 0.9
BETA_TWO = 0.999
ADAM_EPS = 1e-08
DECAY = 0.01
RATES = (0.04, 0.1, 0.04, 0.02, 0.04, 0.4, 0.3)
D = 512
ROWS = 128
LEN = 1024
QB = 256
NN = ((1,), (0,))
NT = ((1,), (1,))
TN = ((0,), (0,))


def dot(a, b, dims=NN):
    return lax.dot_general(a, b, (dims, ((), ())), preferred_element_type=F32)


def aligned(value, by):
    return pl.multiple_of(value, by)


class Group:
    def __init__(self, links, total, receives=1, each=None):
        self.send_sem, self.total = links.semaphore(), total
        self.each = total if each is None else each
        self.recv_sems = [links.semaphore() for _ in range(receives)]
        links.groups.append(self)

    def send(self, src, dst, device, k=0):
        pltpu.make_async_remote_copy(
            src_ref=src,
            dst_ref=dst,
            send_sem=self.send_sem,
            recv_sem=self.recv_sems[k],
            device_id=device,
            device_id_type=pl.DeviceIdType.MESH,
        ).start()

    def wait(self, k=0):
        pltpu.make_async_copy(self.each, self.each, self.recv_sems[k]).wait()


class Links:
    def __init__(self, sems):
        self.sems, self.used, self.groups = sems, 0, []

    def semaphore(self):
        self.used += 1
        return self.sems.at[self.used - 1]

    def drain(self):
        for g in self.groups:
            pltpu.make_async_copy(g.total, g.total, g.send_sem).wait()


N_SEMS = 138
N_LOCAL = 23


SHAPES = ((192, D), (64, D), (D, 256), (256, D), (2 * D, D), (2, D), (4, D))


def adamw(weight, first, second, grad, rate):
    first = BETA_ONE * first + (1.0 - BETA_ONE) * grad
    second = BETA_TWO * second + (1.0 - BETA_TWO) * grad * grad
    root = (1.0 - BETA_TWO**STEP) ** 0.5
    step = (rate * root / (1.0 - BETA_ONE**STEP)) * first / (jnp.sqrt(second) + ADAM_EPS * root)
    return ((1.0 - rate * DECAY) * weight - step, first, second)


SCRATCH = [
    ((ROWS, D), BF16),
    ((ROWS, D), BF16),
    ((LEN, D), BF16),
    ((LEN, D), BF16),
    ((1536, D), BF16),
    ((D, D), BF16),
    ((D, 1024), BF16),
    ((1024, D), BF16),
    ((2, D, D), BF16),
    ((D, D), BF16),
    ((192, LEN), BF16),
    ((LEN, 64), BF16),
    ((LEN, 64), BF16),
    ((LEN, QB), F32),
    ((LEN, LEN), BF16),
    ((LEN, QB), BF16),
    ((64, LEN), F32),
    ((64, LEN), BF16),
    ((1, LEN), F32),
    ((D, 256), BF16),
    ((ROWS, D), F32),
    ((ROWS, D), F32),
    ((ROWS, D), F32),
    ((ROWS, D), F32),
    ((ROWS, 128), F32),
    ((256, D), BF16),
    ((ROWS, D), F32),
    ((256, 1024), BF16),
    ((256, 1024), F32),
    ((ROWS, D), F32),
    ((ROWS, D), BF16),
    ((ROWS, D), BF16),
    ((256, D), BF16),
    ((ROWS, D), BF16),
    ((ROWS, D), BF16),
    ((ROWS, D), BF16),
    ((256, 256), BF16),
    ((256, 256), BF16),
    ((256, 1024), BF16),
    ((ROWS, D), F32),
    ((ROWS, D), BF16),
    ((ROWS, D), BF16),
    ((ROWS, D), F32),
    ((8, 128, ROWS), BF16),
    ((128, LEN), BF16),
    ((8, D), F32),
    ((8, D), F32),
    ((8, 8, D), F32),
    ((8, 8, D), F32),
    ((64, LEN), F32),
    ((64, LEN), F32),
    ((64, LEN), F32),
    ((192, LEN), BF16),
    ((1536, ROWS), BF16),
    ((192, D), BF16),
    ((192, D), F32),
    ((64, D), F32),
    ((64, D), BF16),
    ((64, 256), BF16),
    ((8, 16, 128), BF16),
    ((8, 16, 128), BF16),
    ((192, 256), BF16),
    ((8, 48, 128), BF16),
    ((8, 48, 128), BF16),
    ((192, D), BF16),
    ((D, D), BF16),
    ((D, D), F32),
    ((D, 256), BF16),
    ((4, 128, 256), BF16),
    ((128, 256), BF16),
    ((4, 32, 256), BF16),
    ((32, 256), BF16),
    ((4, 32, 256), BF16),
    ((D, D), BF16),
    ((D, 256), BF16),
    ((4, 128, 256), BF16),
    ((128, 256), BF16),
    ((4, 32, 256), BF16),
    ((32, 256), BF16),
    ((4, 32, 256), BF16),
    ((64, D), BF16),
    ((D, 256), BF16),
    ((256, D), BF16),
]
for part in ((32, 128), (32, 128), (16, 256), (16, 256)):
    SCRATCH += [((count, *part), BF16) for count in (64, 48, 16, 12, 4, 3)]


def layer_kernel(*refs):
    x_hbm, dy_hbm, states = refs[0], refs[1], refs[2:23]
    mixed_ref, ingrad_ref, kept = refs[23], refs[24], refs[25:46]
    gains_ref, biases_ref = kept[15], kept[18]
    sems, local_sems = refs[-2:]
    (
        x_ref,
        dy_ref,
        x_all,
        h1_all,
        w_all,
        out_all,
        up_all,
        down_all,
        gate_low,
        gate_t,
        proj_t,
        k_nat,
        v_nat,
        s_buf,
        e_buf,
        ds_buf,
        o_t,
        o_low,
        inv_mass,
        heads_t,
        g1_buf,
        attn_buf,
        x1_buf,
        xhat_buf,
        rstd_buf,
        h2_pair,
        g2_buf,
        act_buf,
        dgelu_buf,
        ffn_own,
        ffn_send,
        ffn_recv,
        dffn_pair,
        dz2_full,
        dz1_full,
        dattn_full,
        dz2_half,
        dattn_half,
        dhid_buf,
        dh2_own,
        dh2_send,
        dh2_recv,
        dh2_gate,
        back_send,
        back_t,
        vec,
        vec_s,
        vec_a,
        vec_b,
        dq_t,
        dk_t,
        dv_t,
        dproj_low,
        dproj_all,
        gq_low,
        gq_f32,
        g1_f32,
        g1_low,
        g1_sib,
        g1_send,
        g1_recv,
        gq_sib,
        gq_send,
        gq_recv,
        gq_all,
        g1t_all,
        g1_nat,
        g2_low,
        gy_recv,
        gy_sum,
        gz_recv,
        gz_sum,
        gx_recv,
        g2_all,
        gout_low,
        go_z,
        go_zs,
        go_x,
        go_xs,
        go_y,
        gout_all,
        gup_all,
        gdown_all,
        *part_refs,
    ) = refs[46:-2]
    dp, head = lax.axis_index("dp"), lax.axis_index("head")
    x_hi, y, core = dp // 8, (dp // 2) % 4, dp % 2
    z, x_lo = head // 2, head % 2
    xx = x_hi * 2 + x_lo
    sub = x_hi * 4 + y
    links = Links(sems)

    def head_peer(o):
        return (head + o) % 8

    def in_head(o):
        return (dp, (head + o) % 8)

    def head_from(o):
        return (head + 8 - o) % 8

    def sub_peer(o):
        return (sub + o) % 8

    def in_sub(o):
        return (((sub + o) % 8) * 2 + core, head)

    def ring(axis, o):
        nx = (xx + o) % 4 if axis == "x" else xx
        ny = (y + o) % 4 if axis == "y" else y
        nz = (z + o) % 4 if axis == "z" else z
        return ((nx // 2) * 8 + ny * 2 + core, nz * 2 + nx % 2)

    sibling = (sub * 2 + (1 - core), head)

    barrier = pltpu.get_barrier_semaphore()
    greeted = [in_head(o) for o in range(1, 8)] + [in_sub(o) for o in range(1, 8)]
    greeted += [sibling, ((1 - x_hi) * 8 + y * 2 + core, z * 2 + 1 - x_lo)]
    for device in greeted:
        pl.semaphore_signal(
            barrier, inc=1, device_id=device, device_id_type=pl.DeviceIdType.MESH
        )

    pairs = [(x_hbm, x_ref)] + [(states[i], kept[i]) for i in (0, 3, 6, 9, 15, 18, 12)]
    pairs += [(dy_hbm, dy_ref)] + [(states[i], kept[i]) for i in range(21) if i % 3]
    loads = [
        pltpu.make_async_copy(src, dst, local_sems.at[i]) for i, (src, dst) in enumerate(pairs)
    ]
    for load in loads[0:9]:
        load.start()

    own = pl.ds(aligned(head * ROWS, ROWS), ROWS)
    own_core = pl.ds(aligned(core * ROWS, ROWS), ROWS)
    sib_core = pl.ds(aligned((1 - core) * ROWS, ROWS), ROWS)
    half = pl.ds(aligned(core * 256, 256), 256)
    sib_half = pl.ds(aligned((1 - core) * 256, 256), 256)
    own_heads = pl.ds(aligned(head * 64, 64), 64)
    own_w = pl.ds(aligned(head * 192, 64), 192)
    sub_rows = pl.ds(aligned(sub * 128, 128), 128)

    def rows_of(ref, first, unit):
        def at(s):
            parts = ((0, unit), (0, unit // 2), (unit // 2, unit // 2))
            return [ref.at[pl.ds(aligned(first(s) + a, unit // 2), n), :] for a, n in parts]

        return at

    def up_at(s):
        cols = pl.ds(aligned(s * 128, 128), 128)
        first = (y % 2) * 256
        parts = ((0, 256), (0, 128), (128, 128))
        return [up_all.at[pl.ds(aligned(first + a, 128), n), cols] for a, n in parts]

    class Spread:
        def __init__(self, at, three, four, seven=None, last=None):
            self.at, self.last, self.one = at, last, at(head)[0]
            self.ring_z = Group(links, three, 3, self.one)
            self.over_x = Group(links, four)
            self.over_last = None if last is None else Group(links, seven)

        def begin(self):
            for o in range(1, 4):
                self.ring_z.send(self.one, self.one, ring("z", o), o - 1)

        def begin_x(self):
            self.forward(head)

        def forward(self, s):
            _, first, second = self.at(s)
            self.over_x.send(first, first, ring("x", 1))
            self.over_x.send(second, second, ring("x", 3))

        def pass_on(self):
            for o in range(1, 4):
                self.ring_z.wait(o - 1)
                s = ((z + 4 - o) % 4) * 2 + x_lo
                self.forward(s)
                if self.last is not None:
                    self.last(self.over_last, *self.at(s))

        def pass_last(self):
            self.over_x.wait()
            for o in range(4):
                self.last(self.over_last, *self.at(((z + o) % 4) * 2 + 1 - x_lo))

    def to_sibling(group, whole, first, second):
        group.send(whole, whole, sibling)

    def to_both_y(group, whole, first, second):
        group.send(first, first, ring("y", 1))
        group.send(second, second, ring("y", 3))

    spread_out = Spread(
        rows_of(out_all, lambda s: s * 64 + core * 32, 32),
        out_all.at[0:96, :],
        out_all.at[0:128, :],
        out_all.at[0:224, :],
        to_sibling,
    )
    spread_up = Spread(
        up_at,
        up_all.at[0:256, 0:384],
        up_all.at[0:256, 0:512],
        up_all.at[0:256, 0:896],
        to_both_y,
    )
    spread_down = Spread(
        rows_of(down_all, lambda s: s * 128 + (y % 2) * 64, 64),
        down_all.at[0:192, :],
        down_all.at[0:256, :],
        down_all.at[0:448, :],
        to_both_y,
    )
    spread_w = Spread(
        rows_of(w_all, lambda s: s * 192 + core * 96, 96),
        w_all.at[0:288, :],
        w_all.at[0:384, :],
        w_all.at[0:672, :],
        to_sibling,
    )
    x_group = Group(links, x_all.at[0 : 7 * ROWS, :], 7, x_ref)

    class Groups:
        pass

    g = Groups()

    beside = (dp, z * 2 + 1 - x_lo)
    gain_one, shift_one = pl.ds(0, 1), pl.ds(0, 1)
    gain_two, shift_two = pl.ds(1, 1), pl.ds(1, 1)

    def project(block):
        for s in range(4):
            rows = pl.ds(aligned(block * ROWS + 32 * s, 32), 32)
            v = x_all[rows, :].astype(F32)
            center = v - jnp.mean(v, axis=-1, keepdims=True)
            spread = jnp.mean(center * center, axis=-1, keepdims=True)
            h = center * lax.rsqrt(spread + NORM_EPS) * gains_ref[gain_one, :] + biases_ref[shift_one, :]
            h1_all[rows, :] = h.astype(BF16)
        rows = pl.ds(aligned(block * ROWS, ROWS), ROWS)
        pt = dot(w_all[own_w, :], h1_all[rows, :], NT)
        proj_t[0:64, rows] = (pt[0:64].astype(BF16).astype(F32) * 0.125).astype(BF16)
        proj_t[64:192, rows] = pt[64:192].astype(BF16)
        k_nat[rows, :] = pt[64:128].T.astype(BF16)
        v_nat[rows, :] = pt[128:192].T.astype(BF16)

    def from_z(o):
        return ((z + 4 - o) % 4) * 2

    place = {"x": xx, "y": y, "z": z}

    class Staged:
        def __init__(self, axes, refs):
            self.axes, self.refs, self.step, self.group = axes, refs, 0, None

        def put(self, ch, value):
            a, b, c = (ch[axis] for axis in self.axes)
            self.refs[0][a * 16 + b * 4 + c] = value

        def send(self):
            axis, size = self.axes[self.step], (16, 4, 1)[self.step]
            src, got = self.refs[2 * self.step : 2 * self.step + 2]
            self.group = Group(links, got)
            for o in range(1, 4):
                t = (place[axis] + o) % 4
                block = got.at[pl.ds((o - 1) * size, size)]
                self.group.send(src.at[pl.ds(t * size, size)], block, ring(axis, o))

        def add(self, store=None):
            at, size = place[self.axes[self.step]], (16, 4, 1)[self.step]
            src, got = self.refs[2 * self.step : 2 * self.step + 2]
            self.group.wait()
            self.step += 1
            to = None if store else self.refs[2 * self.step]

            def some(i, n):
                total = src[pl.ds(at * size + i, n)].astype(F32)
                for o in range(3):
                    total = total + got[pl.ds(o * size + i, n)].astype(F32)
                return total.astype(BF16)

            if store:
                store(some(0, 1)[0])
                return

            def body(i, carry):
                to[pl.ds(i * 4, 4)] = some(i * 4, 4)
                return carry

            lax.fori_loop(0, size // 4, body, 0)

        def next(self):
            self.add()
            self.send()

    up_a, up_b, down_a, down_b = (
        Staged(axes, part_refs[6 * i : 6 * i + 6])
        for i, axes in enumerate(("yzx", "xyz", "yxz", "zxy"))
    )

    def chip_of(h, n):
        return {"x": (n // 4) * 2 + h % 2, "y": n % 4, "z": h // 2}

    def add_slots(ref, n=8):
        total = ref[0].astype(F32)
        for o in range(1, n):
            total = total + ref[o].astype(F32)
        return total

    def block_of(ref, at, rows, cols=slice(None)):
        return ref.at[pl.ds(aligned(at * rows, rows), rows), cols]

    def to_all(group, peers, ref):
        for o in range(1, 4 if peers not in (in_head, in_sub) else 8):
            group.send(ref, ref, peers(o))

    def in_ring(axis):
        return lambda o: ring(axis, o)

    def update(i, grad, first=0, rows=None):
        rows = SHAPES[i][0] if rows is None else rows
        step = 32 if SHAPES[i][1] == D else 64

        def strip(n, carry):
            at = pl.ds(aligned(n * step, step), step)
            into = pl.ds(aligned(first + n * step, step), step)
            refs = kept[3 * i : 3 * i + 3]
            values = adamw(*(r[into, :] for r in refs), grad[at, :].astype(F32), RATES[i])
            for r, value in zip(refs, values):
                r[into, :] = value
            return carry

        lax.fori_loop(0, rows // step, strip, 0, unroll=2)


    def x_out():
        for o in range(1, 4):
            x_group.send(x_ref, x_all.at[own, :], ring("z", o), o - 1)
        x_group.send(x_ref, x_all.at[own, :], beside, 3)

    def cast_weights():
        for load in loads[1:5]:
            load.wait()
        w_all[own_w, :] = kept[0][...].astype(BF16)
        out_all[own_heads, :] = kept[3][...].astype(BF16)
        up_all[:, own] = kept[6][:, own_core].astype(BF16)
        down_all[own, :] = kept[9][own_core, :].astype(BF16)

    def load_rest():
        for load in loads[9:]:
            load.start()
        for load in loads[5:9]:
            load.wait()
        for i in range(2):
            gate_low[i] = kept[12][D * i : D * i + D, :].astype(BF16)
        for n in range(4):
            cols = slice(128 * n, 128 * n + 128)
            gate_t[cols, :] = kept[12][0:D, cols].T.astype(BF16)

    def project_own():
        project(head)

    def x_pass_z():
        x_group.wait(3)
        block = block_of(x_all, z * 2 + 1 - x_lo, ROWS)
        x_group.send(block, block, ring("z", 1), 4)
        x_group.send(block, block, ring("z", 3), 5)

    def project_beside():
        project(z * 2 + 1 - x_lo)

    def from_z(o):
        return ((z + 4 - o) % 4) * 2

    def project_near():
        x_group.wait(0)
        project(from_z(1) + x_lo)
        x_group.wait(2)
        project(from_z(3) + x_lo)

    def x_pass_x():
        x_group.wait(1)
        block = block_of(x_all, from_z(2) + x_lo, ROWS)
        x_group.send(block, block, beside, 6)

    def project_far():
        project(from_z(2) + x_lo)

    def project_passed():
        x_group.wait(4)
        project(from_z(1) + 1 - x_lo)
        x_group.wait(5)
        project(from_z(3) + 1 - x_lo)

    def project_last():
        x_group.wait(6)
        project(from_z(2) + 1 - x_lo)


    def attention():
        for j in range(LEN // QB):
            cols = slice(QB * j, QB * (j + 1))
            queries = proj_t[0:64, cols]
            ceiling = jnp.full((1, QB), -1e30, F32)
            tiles = QB * (j + 1) // ROWS
            for t in range(tiles):
                s = dot(k_nat[ROWS * t : ROWS * (t + 1), :], queries)
                if ROWS * t >= QB * j:
                    keys_at = lax.broadcasted_iota(jnp.int32, (ROWS, QB), 0) + ROWS * t
                    queries_at = lax.broadcasted_iota(jnp.int32, (ROWS, QB), 1) + QB * j
                    s = jnp.where(keys_at <= queries_at, s, -1e30)
                s_buf[ROWS * t : ROWS * (t + 1), :] = s
                ceiling = jnp.maximum(ceiling, jnp.max(s, axis=0, keepdims=True))
            mass = jnp.zeros((1, QB), F32)
            for t in range(tiles):
                e = jnp.exp(s_buf[ROWS * t : ROWS * (t + 1), :] - ceiling)
                mass = mass + jnp.sum(e, axis=0, keepdims=True)
                e_buf[ROWS * t : ROWS * (t + 1), cols] = e.astype(BF16)
            total = dot(proj_t[128:192, 0 : QB * (j + 1)], e_buf[0 : QB * (j + 1), cols])
            total = total / mass
            o_t[:, cols] = total
            o_low[:, cols] = total.astype(BF16)
            inv_mass[:, cols] = 1.0 / mass
        group = g.heads = Group(links, heads_t.at[0:448, 0:ROWS])
        for o in range(1, 8):
            block = o_low.at[:, pl.ds(aligned(head_peer(o) * ROWS, ROWS), ROWS)]
            group.send(block, heads_t.at[own_heads, own_core], in_head(o))
        heads_t[own_heads, own_core] = o_low[:, own]


    def gate_one():
        g1_buf[...] = dot(h1_all[own, :], gate_low[0]) + biases_ref[2:3, :]

    def middle():
        g.heads.wait()
        group = g.heads_pair = Group(links, heads_t.at[:, 0:ROWS])
        group.send(heads_t.at[:, own_core], heads_t.at[:, own_core], sibling)
        spread_out.over_last.wait()
        attn_buf[...] = dot(heads_t[:, own_core], out_all[...], TN)
        for s in range(4):
            rows = slice(32 * s, 32 * s + 32)
            g1 = jax.nn.sigmoid(g1_buf[rows, :])
            g1_buf[rows, :] = g1
            x = x_ref[rows, :].astype(F32)
            x1 = g1 * attn_buf[rows, :] + (1.0 - g1) * x
            x1_buf[rows, :] = x1
            center = x1 - jnp.mean(x1, axis=-1, keepdims=True)
            spread = jnp.mean(center * center, axis=-1, keepdims=True)
            rstd = lax.rsqrt(spread + NORM_EPS)
            xhat = center * rstd
            xhat_buf[rows, :] = xhat
            rstd_buf[rows, :] = jnp.broadcast_to(rstd, (32, 128))
            h2 = xhat * gains_ref[gain_two, :] + biases_ref[shift_two, :]
            h2_pair[pl.ds(aligned(core * ROWS + 32 * s, 32), 32), :] = h2.astype(BF16)
        group = g.h2 = Group(links, h2_pair.at[0:ROWS, :])
        group.send(h2_pair.at[own_core, :], h2_pair.at[own_core, :], sibling)

    def gate_two():
        g2_buf[...] = dot(h2_pair[own_core, :], gate_low[1]) + biases_ref[3:4, :]

    def hidden():
        g.h2.wait()
        spread_up.over_last.wait()
        for n in range(4):
            cols = slice(256 * n, 256 * n + 256)
            u = dot(h2_pair[...], up_all[:, cols])
            c0 = 0.7978845608028654
            inner = jnp.tanh(c0 * (u + 0.044715 * u * u * u))
            act_buf[:, cols] = (0.5 * u * (1.0 + inner)).astype(BF16)
            dgelu_buf[:, cols] = 0.5 * (1.0 + inner) + 0.5 * u * (1.0 - inner * inner) * c0 * (
                1.0 + 3.0 * 0.044715 * u * u
            )

    def ffn():
        spread_down.over_last.wait()
        ffn_send[...] = dot(act_buf[sib_core, :], down_all[...]).astype(BF16)
        g.ffn = Group(links, ffn_recv)
        g.ffn.send(ffn_send, ffn_recv, sibling)
        ffn_own[...] = dot(act_buf[own_core, :], down_all[...])

    def mix():
        g.ffn.wait()
        bias_two = jnp.zeros((1, D), F32)
        for s in range(4):
            rows = slice(32 * s, 32 * s + 32)
            total = ffn_own[rows, :] + ffn_recv[rows, :].astype(F32)
            g2 = jax.nn.sigmoid(g2_buf[rows, :])
            g2_buf[rows, :] = g2
            x1 = x1_buf[rows, :]
            dy = dy_ref[rows, :].astype(F32)
            mixed_ref[rows, :] = g2 * total + (1.0 - g2) * x1
            dffn_pair[pl.ds(aligned(core * ROWS + 32 * s, 32), 32), :] = (g2 * dy).astype(BF16)
            dz = (dy * (total - x1) * g2 * (1.0 - g2)).astype(BF16)
            dz2_full[rows, :] = dz
            bias_two = bias_two + jnp.sum(dz.astype(F32), axis=0, keepdims=True)
        group = g.dffn = Group(links, dffn_pair.at[0:ROWS, :])
        group.send(dffn_pair.at[own_core, :], dffn_pair.at[own_core, :], sibling)
        group = g.dz2 = Group(links, dz2_half.at[0:ROWS, :])
        group.send(dz2_full.at[:, sib_half], dz2_half.at[own_core, :], sibling)
        dz2_half[own_core, :] = dz2_full[:, half]
        vec[5:6, :] = bias_two
        vec[6:8, :] = jnp.zeros((2, D), F32)


    def back_gate_two():
        dh2_gate[...] = dot(dz2_full[...], gate_low[1], NT)

    def back_hidden():
        g.dffn.wait()
        for n in range(4):
            cols = slice(256 * n, 256 * n + 256)
            da = dot(dffn_pair[...], down_all[cols, :], NT)
            dhid_buf[:, cols] = (da * dgelu_buf[:, cols]).astype(BF16)
        dh2_send[...] = dot(dhid_buf[sib_core, :], up_all[...], NT).astype(BF16)
        g.dh2 = Group(links, dh2_recv)
        g.dh2.send(dh2_send, dh2_recv, sibling)
        dh2_own[...] = dot(dhid_buf[own_core, :], up_all[...], NT)

    def back_middle():
        g.dh2.wait()
        gain_sum = jnp.zeros((1, D), F32)
        shift_sum = jnp.zeros((1, D), F32)
        bias_one = jnp.zeros((1, D), F32)
        for s in range(4):
            rows = slice(32 * s, 32 * s + 32)
            dh2 = dh2_own[rows, :] + dh2_recv[rows, :].astype(F32) + dh2_gate[rows, :]
            xhat = xhat_buf[rows, :]
            gain_sum = gain_sum + jnp.sum(dh2 * xhat, axis=0, keepdims=True)
            shift_sum = shift_sum + jnp.sum(dh2, axis=0, keepdims=True)
            dxhat = dh2 * gains_ref[gain_two, :]
            mean_a = jnp.mean(dxhat, axis=-1, keepdims=True)
            mean_b = jnp.mean(dxhat * xhat, axis=-1, keepdims=True)
            rstd = rstd_buf[rows, 0:1]
            dx1 = (1.0 - g2_buf[rows, :]) * dy_ref[rows, :].astype(F32) + rstd * (
                dxhat - mean_a - xhat * mean_b
            )
            g1 = g1_buf[rows, :]
            dattn_full[rows, :] = (g1 * dx1).astype(BF16)
            x = x_ref[rows, :].astype(F32)
            dz = (dx1 * (attn_buf[rows, :] - x) * g1 * (1.0 - g1)).astype(BF16)
            dz1_full[rows, :] = dz
            bias_one = bias_one + jnp.sum(dz.astype(F32), axis=0, keepdims=True)
            ingrad_ref[rows, :] = (1.0 - g1) * dx1
        dheads = dot(out_all[...], dattn_full[...], NT).astype(BF16)
        dz1_t = dz1_full[...].astype(F32).T.astype(BF16)
        for h in range(8):
            back_send[h, 0:64, :] = dheads[64 * h : 64 * h + 64, :]
            back_send[h, 64:128, :] = dz1_t[64 * h : 64 * h + 64, :]
        group = g.back = Group(links, back_t.at[:, 0 : 7 * ROWS])
        for o in range(1, 8):
            group.send(back_send.at[head_peer(o)], back_t.at[:, own], in_head(o))
        back_t[:, own] = back_send[head]
        group = g.dattn = Group(links, dattn_half.at[0:ROWS, :])
        group.send(dattn_full.at[:, sib_half], dattn_half.at[own_core, :], sibling)
        dattn_half[own_core, :] = dattn_full[:, half]
        vec[1:2, :] = gain_sum
        vec[3:4, :] = shift_sum
        vec[4:5, :] = bias_one

    def back_attention():
        dk_t[...] = jnp.zeros_like(dk_t)
        dv_t[...] = jnp.zeros_like(dv_t)
        for j in range(LEN // QB):
            cols = slice(QB * j, QB * (j + 1))
            upto = QB * (j + 1)
            queries = proj_t[0:64, cols]
            grads = back_t[0:64, cols]
            inverse = inv_mass[:, cols]
            delta = jnp.sum(o_t[:, cols] * grads.astype(F32), axis=0, keepdims=True)
            for t in range(upto // ROWS):
                keys = slice(ROWS * t, ROWS * (t + 1))
                p = e_buf[keys, cols].astype(F32) * inverse
                ds_buf[keys, :] = (p * (dot(v_nat[keys, :], grads) - delta)).astype(BF16)
            dq_t[:, cols] = dot(proj_t[64:128, 0:upto], ds_buf[0:upto, :]) * 0.125
            dk_t[:, 0:upto] += dot(queries, ds_buf[0:upto, :], NT)
            scaled = (grads.astype(F32) * inverse).astype(BF16)
            dv_t[:, 0:upto] += dot(scaled, e_buf[0:upto, cols], NT)
        dproj_low[0:64, :] = dq_t[...].astype(BF16)
        dproj_low[64:128, :] = dk_t[...].astype(BF16)
        dproj_low[128:192, :] = dv_t[...].astype(BF16)
        group = g.dproj = Group(links, dproj_all.at[0 : 7 * 192, :])
        for o in range(1, 8):
            block = dproj_low.at[:, pl.ds(aligned(head_peer(o) * ROWS, ROWS), ROWS)]
            group.send(block, dproj_all.at[own_w, :], in_head(o))
        dproj_all[own_w, :] = dproj_low[:, own]

    def input_grad():
        g.dproj.wait()
        spread_w.over_last.wait()
        dh2_own[...] = dot(dproj_all[...], w_all[...], TN) + dot(
            dz1_full[...], gate_low[0], NT
        )
        for s in range(4):
            rows = slice(32 * s, 32 * s + 32)
            v = x_ref[rows, :].astype(F32)
            center = v - jnp.mean(v, axis=-1, keepdims=True)
            spread = jnp.mean(center * center, axis=-1, keepdims=True)
            rstd = lax.rsqrt(spread + NORM_EPS)
            xhat = center * rstd
            dxhat = dh2_own[rows, :] * gains_ref[gain_one, :]
            mean_a = jnp.mean(dxhat, axis=-1, keepdims=True)
            mean_b = jnp.mean(dxhat * xhat, axis=-1, keepdims=True)
            ingrad_ref[rows, :] += rstd * (dxhat - mean_a - xhat * mean_b)

    def vec_pair():
        gain = jnp.zeros((1, D), F32)
        shift = jnp.zeros((1, D), F32)
        gate_rows = gate_t[own_heads, :]
        for n in range(4):
            rows = slice(64 * n, 64 * n + 64)
            grads = (dproj_low[rows, :] if n < 3 else back_t[64:128, :]).astype(F32)
            sums = jnp.sum(grads, axis=1, keepdims=True)
            weights = w_all[pl.ds(aligned(head * 192 + 64 * n, 64), 64), :] if n < 3 else gate_rows
            weights = weights.astype(F32)
            products = gq_f32[rows, :] if n < 3 else g1_f32[...]
            moved = products - biases_ref[shift_one, :] * sums
            gain = gain + jnp.sum(weights * moved, axis=0, keepdims=True)
            shift = shift + jnp.sum(weights * sums, axis=0, keepdims=True)
        vec[0:1, :] = gain / gains_ref[gain_one, :]
        vec[2:3, :] = shift
        g.vec_pair = Group(links, vec_s)
        g.vec_pair.send(vec, vec_s, sibling)

    def vec_sub():
        g.vec_pair.wait()
        vec_a[sub] = vec[...] + vec_s[...]
        g.vec_sub = Group(links, vec_a.at[0:7])
        to_all(g.vec_sub, in_sub, vec_a.at[sub])

    def vec_head():
        g.vec_sub.wait()
        vec_b[head] = add_slots(vec_a)
        g.vec_head = Group(links, vec_b.at[0:7])
        to_all(g.vec_head, in_head, vec_b.at[head])

    def vec_done():
        g.vec_head.wait()
        total = add_slots(vec_b)
        for i, grad in ((5, total[0:2]), (6, total[2:6])):
            refs = kept[3 * i : 3 * i + 3]
            for r, value in zip(refs, adamw(*(r[...] for r in refs), grad, RATES[i])):
                r[...] = value


    def grad_down():
        for h in range(8):
            gd = dot(act_buf[:, 128 * h : 128 * h + 128], dffn_pair[...], TN).astype(BF16)
            for n in range(8):
                down_a.put(chip_of(h, n), gd[16 * n : 16 * n + 16, 0:256])
                down_b.put(chip_of(h, n), gd[16 * n : 16 * n + 16, 256:512])

    def grad_up():
        for h in range(8):
            gu = dot(h2_pair[...], dhid_buf[:, 128 * h : 128 * h + 128], TN).astype(BF16)
            for n in range(8):
                up_a.put(chip_of(h, n), gu[64 * n : 64 * n + 32, :])
                up_b.put(chip_of(h, n), gu[64 * n + 32 : 64 * n + 64, :])

    def down_sub():
        rows = pl.ds(aligned(core * 128 + sub * 16, 16), 16)
        for part, cols in ((down_a, slice(0, 256)), (down_b, slice(256, 512))):

            def store(value, cols=cols):
                gdown_all[rows, cols] = value

            part.add(store)
        g.down_sub = Group(links, gdown_all.at[0:112, :])
        to_all(g.down_sub, in_sub, gdown_all.at[rows, :])

    def down_pair():
        g.down_sub.wait()
        group = g.down_pair = Group(links, gdown_all.at[0:128, :])
        group.send(gdown_all.at[own_core, :], gdown_all.at[own_core, :], sibling)

    def down_done():
        g.down_pair.wait()
        update(3, gdown_all)

    def up_sub():
        for part, first in ((up_a, 0), (up_b, 32)):

            def store(value, first=first):
                gup_all[pl.ds(aligned(sub * 64 + first, 32), 32), own_core] = value

            part.add(store)
        block = block_of(gup_all, sub, 64, own_core)
        g.up_sub = Group(links, gup_all.at[0:448, 0:128])
        to_all(g.up_sub, in_sub, block)

    def up_pair():
        g.up_sub.wait()
        group = g.up_pair = Group(links, gup_all.at[:, 0:128])
        group.send(gup_all.at[:, own_core], gup_all.at[:, own_core], sibling)

    def up_done():
        g.up_pair.wait()
        update(2, gup_all)


    def second_y():
        g.dz2.wait()
        g2_low[...] = dot(h2_pair[...], dz2_half[...], TN).astype(BF16)
        group = g.second_y = Group(links, gy_recv.at[0:3])
        for o in range(1, 4):
            group.send(block_of(g2_low, (y + o) % 4, 128), gy_recv.at[y], ring("y", o))
        gy_recv[y] = g2_low[pl.ds(aligned(y * 128, 128), 128), :]

    def second_z():
        g.second_y.wait()
        gy_sum[...] = add_slots(gy_recv, 4).astype(BF16)
        group = g.second_z = Group(links, gz_recv.at[0:3])
        for o in range(1, 4):
            group.send(block_of(gy_sum, (z + o) % 4, 32), gz_recv.at[z], ring("z", o))
        gz_recv[z] = gy_sum[pl.ds(aligned(z * 32, 32), 32), :]

    def second_x():
        g.second_z.wait()
        gz_sum[...] = add_slots(gz_recv, 4).astype(BF16)
        group = g.second_x = Group(links, gx_recv.at[0:3])
        for o in range(1, 4):
            group.send(gz_sum, gx_recv.at[xx], ring("x", o))
        gx_recv[xx] = gz_sum[...]

    def second_back_z():
        g.second_x.wait()
        rows = pl.ds(aligned(y * 128 + z * 32, 32), 32)
        g2_all[rows, half] = add_slots(gx_recv, 4).astype(BF16)
        g.second_back_z = Group(links, gz_recv.at[0:3])
        to_all(g.second_back_z, in_ring("z"), g2_all.at[rows, half])

    def second_back_y():
        g.second_back_z.wait()
        block = block_of(g2_all, y, 128, half)
        g.second_back_y = Group(links, gy_recv.at[0:3])
        to_all(g.second_back_y, in_ring("y"), block)

    def second_pair():
        g.second_back_y.wait()
        group = g.second_pair = Group(links, g2_low)
        group.send(g2_all.at[:, half], g2_all.at[:, half], sibling)

    def second_done():
        g.second_pair.wait()
        update(4, g2_all, D, D)


    def grad_out_z():
        g.heads_pair.wait()
        g.dattn.wait()
        gout_low[...] = dot(heads_t[...], dattn_half[...]).astype(BF16)
        group = g.grad_out_z = Group(links, go_z.at[0:3])
        for o in range(1, 4):
            group.send(block_of(gout_low, (z + o) % 4, 128), go_z.at[z], ring("z", o))
        go_z[z] = gout_low[pl.ds(aligned(z * 128, 128), 128), :]

    def grad_out_x():
        g.grad_out_z.wait()
        go_zs[...] = add_slots(go_z, 4).astype(BF16)
        group = g.grad_out_x = Group(links, go_x.at[0:3])
        for o in range(1, 4):
            to = (xx + o) % 4
            block = block_of(go_zs, (to % 2) * 2 + to // 2, 32)
            group.send(block, go_x.at[xx], ring("x", o))
        go_x[xx] = go_zs[pl.ds(aligned((x_lo * 2 + x_hi) * 32, 32), 32), :]

    def grad_out_y():
        g.grad_out_x.wait()
        go_xs[...] = add_slots(go_x, 4).astype(BF16)
        group = g.grad_out_y = Group(links, go_y.at[0:3])
        for o in range(1, 4):
            group.send(go_xs, go_y.at[y], ring("y", o))
        go_y[y] = go_xs[...]

    def grad_out_far():
        g.grad_out_y.wait()
        rows = pl.ds(aligned(x_hi * 32, 32), 32)
        gout_all[rows, half] = add_slots(go_y, 4).astype(BF16)
        group = g.grad_out_far = Group(links, go_xs)
        group.send(gout_all.at[rows, half], gout_all.at[rows, half], ring("x", 2))

    def grad_out_pair():
        g.grad_out_far.wait()
        group = g.grad_out_pair = Group(links, go_zs.at[0:64, :])
        group.send(gout_all.at[:, half], gout_all.at[:, half], sibling)

    def grad_out_done():
        g.grad_out_pair.wait()
        update(1, gout_all)


    def qkv_pair():
        gq_f32[...] = dot(dproj_low[...], h1_all[...])
        gq_low[...] = gq_f32[...].astype(BF16)
        g.qkv_pair = Group(links, gq_sib)
        g.qkv_pair.send(gq_low.at[:, sib_half], gq_sib, sibling)

    def qkv_sub():
        g.qkv_pair.wait()
        total = gq_low[:, half].astype(F32) + gq_sib[...].astype(F32)
        for i in range(8):
            r, c = 48 * (i // 2), 128 * (i % 2)
            gq_send[i] = total[r : r + 48, c : c + 128].astype(BF16)
        group = g.qkv_sub = Group(links, gq_recv.at[0:7])
        for o in range(1, 8):
            group.send(gq_send.at[sub_peer(o)], gq_recv.at[sub], in_sub(o))
        gq_recv[sub] = gq_send[sub]

    def qkv_back():
        g.qkv_sub.wait()
        rows = pl.ds(aligned((sub // 2) * 48, 48), 48)
        cols = pl.ds(aligned(core * 256 + (sub % 2) * 128, 128), 128)
        gq_all[rows, cols] = add_slots(gq_recv).astype(BF16)
        g.qkv_back = Group(links, gq_recv.at[0:7])
        to_all(g.qkv_back, in_sub, gq_all.at[rows, cols])


    def first_start():
        g.back.wait()
        g1_f32[...] = dot(back_t[64:128, :], h1_all[...])
        g1_low[...] = g1_f32[...].astype(BF16)
        g.first_start = Group(links, g1_sib)
        g.first_start.send(g1_low.at[:, sib_half], g1_sib, sibling)

    def first_sub():
        g.first_start.wait()
        total = g1_low[:, half].astype(F32) + g1_sib[...].astype(F32)
        for i in range(8):
            r, c = 16 * (i // 2), 128 * (i % 2)
            g1_send[i] = total[r : r + 16, c : c + 128].astype(BF16)
        group = g.first_sub = Group(links, g1_recv.at[0:7])
        for o in range(1, 8):
            group.send(g1_send.at[sub_peer(o)], g1_recv.at[sub], in_sub(o))
        g1_recv[sub] = g1_send[sub]

    def first_back():
        g.first_sub.wait()
        rows = pl.ds(aligned(head * 64 + (sub // 2) * 16, 16), 16)
        cols = pl.ds(aligned(core * 256 + (sub % 2) * 128, 128), 128)
        g1t_all[rows, cols] = add_slots(g1_recv).astype(BF16)
        g.first_back = Group(links, g1_recv.at[0:7])
        to_all(g.first_back, in_sub, g1t_all.at[rows, cols])

    def first_head():
        g.first_back.wait()
        g.first_head = Group(links, g1t_all.at[0:448, 0:256])
        to_all(g.first_head, in_head, g1t_all.at[own_heads, half])

    def qkv_back_pair():
        g.qkv_back.wait()
        g.qkv_back_pair = Group(links, gq_sib)
        g.qkv_back_pair.send(gq_all.at[:, half], gq_all.at[:, half], sibling)

    def qkv_done():
        g.qkv_back_pair.wait()
        update(0, gq_all)

    def first_pair():
        g.first_head.wait()
        group = g.first_pair = Group(links, g2_low)
        group.send(g1t_all.at[:, half], g1t_all.at[:, half], sibling)

    def first_done():
        g.first_pair.wait()
        for n in range(4):
            at = slice(128 * n, 128 * n + 128)
            g1_nat[at, :] = g1t_all[:, at].astype(F32).T
        update(4, g1_nat, 0, D)

    def moments():
        for load in loads[9:]:
            load.wait()

    loads[0].wait()
    x_all[own, :] = x_ref[...]
    pl.semaphore_wait(barrier, len(greeted))
    for run in (
        x_out,
        cast_weights,
        spread_up.begin_x,
        x_pass_z,
        spread_up.begin,
        load_rest,
        spread_down.begin,
        x_pass_x,
        project_beside,
        project_own,
        spread_out.begin_x,
        project_far,
        spread_out.begin,
        spread_down.begin_x,
        project_passed,
        project_near,
        project_last,
        spread_up.pass_on,
        attention,
        spread_down.pass_on,
        spread_out.pass_on,
        spread_up.pass_last,
        spread_w.begin,
        spread_down.pass_last,
        spread_w.begin_x,
        spread_out.pass_last,
        gate_one,
        middle,
        hidden,
        ffn,
        spread_w.pass_on,
        gate_two,
        mix,
        back_gate_two,
        back_hidden,
        second_y,
        back_middle,
        grad_down,
        down_a.send,
        grad_up,
        up_a.send,
        up_b.send,
        grad_out_z,
        second_z,
        first_start,
        down_b.send,
        down_a.next,
        first_sub,
        grad_out_x,
        second_x,
        back_attention,
        up_a.next,
        qkv_pair,
        first_back,
        grad_out_y,
        down_b.next,
        up_b.next,
        qkv_sub,
        vec_pair,
        spread_w.pass_last,
        second_back_z,
        grad_out_far,
        vec_sub,
        up_b.next,
        down_a.next,
        up_a.next,
        down_b.next,
        first_head,
        second_back_y,
        input_grad,
        qkv_back,
        up_sub,
        grad_out_pair,
        down_sub,
        moments,
        grad_out_done,
        second_pair,
        vec_head,
        first_pair,
        second_done,
        qkv_back_pair,
        first_done,
        up_pair,
        down_pair,
        qkv_done,
        vec_done,
        up_done,
        down_done,
    ):
        run()
    links.drain()


VMEM = pl.BlockSpec(memory_space=pltpu.VMEM)
ANY = pl.BlockSpec(memory_space=pl.ANY)
HBM = pl.BlockSpec(memory_space=pltpu.HBM)


def run_layer(*args):
    in_vmem = [pltpu.VMEM(s, F32) for s in SHAPES for _ in range(3)]
    shapes = [pltpu.VMEM((ROWS, D), F32)] * 2
    return pl.pallas_call(
        layer_kernel,
        out_shape=shapes + in_vmem,
        in_specs=[HBM] * 23,
        out_specs=[VMEM] * 23,
        scratch_shapes=[pltpu.VMEM(s, t) for s, t in SCRATCH]
        + [pltpu.SemaphoreType.DMA((N_SEMS,)), pltpu.SemaphoreType.DMA((N_LOCAL,))],
        compiler_params=pltpu.CompilerParams(
            collective_id=0, has_side_effects=True, vmem_limit_bytes=40 * 1024 * 1024
        ),
        name="layer",
    )(*args)


def finish_kernel(*refs):
    sems = refs[46]
    copies = [
        pltpu.make_async_copy(refs[i], refs[23 + i], sems.at[i]) for i in range(23)
    ]
    for c in copies:
        c.start()
    for c in copies:
        c.wait()


def finish(results):
    return pl.pallas_call(
        finish_kernel,
        out_shape=[jax.ShapeDtypeStruct(a.shape, F32) for a in results],
        in_specs=[ANY] * 23,
        out_specs=[ANY] * 23,
        scratch_shapes=[pltpu.SemaphoreType.DMA((23,))],
        compiler_params=pltpu.CompilerParams(vmem_limit_bytes=1024 * 1024),
        name="finish",
    )(*results)


def local(inputs, cotangent, *state):
    rows = inputs.shape[1]
    flat = list(state)
    for i in (0, 1, 2):
        flat[i] = jnp.transpose(flat[i], (0, 2, 1)).reshape(192, D)
    for i in (12, 13, 14):
        flat[i] = flat[i].reshape(2 * D, D)
    operands = (inputs.reshape(rows, D), cotangent.reshape(rows, D), *flat)
    results = run_layer(*(pltpu.with_memory_space_constraint(a, pltpu.HBM) for a in operands))
    mixed, ingrad, *new = finish(results)
    for i in (0, 1, 2):
        new[i] = jnp.transpose(new[i].reshape(3, 64, D), (0, 2, 1))
    for i in (12, 13, 14):
        new[i] = new[i].reshape(2, D, D)
    return (mixed.reshape(1, rows, D), ingrad.reshape(1, rows, D), *new)


def solution(mesh):
    batch = P("dp", "head", None)
    qkv = P(None, None, "head")
    first = P("head", None)
    second = P(None, "head")
    state = (qkv,) * 3 + (first,) * 3 + (second,) * 3 + (first,) * 3 + (P(),) * 9
    return jax.shard_map(
        local,
        mesh=mesh,
        in_specs=(batch, batch, *state),
        out_specs=(batch, batch, *state),
        check_vma=False,
    )
```

```python
import math

import jax
import jax.numpy as jnp
from jax import lax
from jax.experimental import pallas as pl
from jax.experimental.pallas import tpu as pltpu
from jax.sharding import PartitionSpec as P

F32 = jnp.float32
BF16 = jnp.bfloat16
STEP = 10
NORM_EPS = 1e-05
BETA_ONE = 0.9
BETA_TWO = 0.999
ADAM_EPS = 1e-08
DECAY = 0.01
RATES = (0.04, 0.1, 0.04, 0.02, 0.04, 0.4, 0.3)
D = 512
ROWS = 128
LEN = 1024
QB = 256
NN = ((1,), (0,))
NT = ((1,), (1,))
TN = ((0,), (0,))


def dot(a, b, dims=NN):
    return lax.dot_general(a, b, (dims, ((), ())), preferred_element_type=F32)


def aligned(value, by):
    return pl.multiple_of(value, by)


class Group:
    def __init__(self, links, total, receives=1, each=None):
        self.send_sem, self.total = links.send_sem, total
        self.each = total if each is None else each
        self.recv_sems = [links.semaphore() for _ in range(receives)]
        links.groups.append(self)

    def send(self, src, dst, device, k=0):
        pltpu.make_async_remote_copy(
            src_ref=src,
            dst_ref=dst,
            send_sem=self.send_sem,
            recv_sem=self.recv_sems[k],
            device_id=device,
            device_id_type=pl.DeviceIdType.MESH,
        ).start()

    def wait(self, k=0):
        pltpu.make_async_copy(self.each, self.each, self.recv_sems[k]).wait()


class Links:
    def __init__(self, sems):
        self.sems, self.send_sem, self.used, self.groups = sems, sems.at[0], 1, []

    def semaphore(self):
        self.used += 1
        return self.sems.at[self.used - 1]

    def drain(self, sent):
        words = [t.dtype.itemsize * math.prod(t.shape) for t in (g.total for g in self.groups)]
        if sum(words) != 2 * math.prod(sent.shape):
            raise ValueError(sum(words))
        pltpu.make_async_copy(sent, sent, self.send_sem).wait()


N_SEMS = 78
N_LOCAL = 23


SHAPES = ((192, D), (64, D), (D, 256), (256, D), (2 * D, D), (2, D), (4, D))


def adamw(weight, first, second, grad, rate):
    first = BETA_ONE * first + (1.0 - BETA_ONE) * grad
    second = BETA_TWO * second + (1.0 - BETA_TWO) * grad * grad
    root = (1.0 - BETA_TWO**STEP) ** 0.5
    step = (rate * root / (1.0 - BETA_ONE**STEP)) * first / (second * lax.rsqrt(second) + ADAM_EPS * root)
    return ((1.0 - rate * DECAY) * weight - step, first, second)


SENT_ROWS = 42816
SCRATCH = [
    ((ROWS, D), BF16),
    ((ROWS, D), BF16),
    ((LEN, D), BF16),
    ((LEN, D), BF16),
    ((1536, D), BF16),
    ((D, D), BF16),
    ((D, 1024), BF16),
    ((1024, D), BF16),
    ((2, D, D), BF16),
    ((D, D), BF16),
    ((192, LEN), BF16),
    ((LEN, 64), BF16),
    ((LEN, 64), BF16),
    ((LEN, QB), F32),
    ((LEN, LEN), BF16),
    ((LEN, QB), BF16),
    ((64, LEN), F32),
    ((64, LEN), BF16),
    ((1, LEN), F32),
    ((D, 256), BF16),
    ((ROWS, D), F32),
    ((ROWS, D), F32),
    ((ROWS, D), F32),
    ((ROWS, D), F32),
    ((ROWS, 128), F32),
    ((256, D), BF16),
    ((ROWS, D), F32),
    ((256, 1024), BF16),
    ((256, 1024), F32),
    ((256, 1024), F32),
    ((ROWS, D), F32),
    ((ROWS, D), BF16),
    ((ROWS, D), BF16),
    ((256, D), BF16),
    ((ROWS, D), BF16),
    ((ROWS, D), BF16),
    ((ROWS, D), BF16),
    ((256, 256), BF16),
    ((256, 256), BF16),
    ((256, 1024), BF16),
    ((ROWS, D), F32),
    ((ROWS, D), BF16),
    ((ROWS, D), BF16),
    ((ROWS, D), F32),
    ((D, ROWS), BF16),
    ((D, ROWS), BF16),
    ((64, LEN), BF16),
    ((64, LEN), BF16),
    ((8, D), F32),
    ((8, D), F32),
    ((8, 8, D), F32),
    ((8, 8, D), F32),
    ((64, LEN), F32),
    ((64, LEN), F32),
    ((64, LEN), F32),
    ((192, LEN), BF16),
    ((1536, ROWS), BF16),
    ((192, D), BF16),
    ((192, D), F32),
    ((64, D), F32),
    ((64, D), BF16),
    ((64, 256), BF16),
    ((8, 16, 128), BF16),
    ((8, 16, 128), BF16),
    ((192, 256), BF16),
    ((8, 48, 128), BF16),
    ((8, 48, 128), BF16),
    ((192, D), BF16),
    ((D, D), BF16),
    ((D, D), F32),
    ((D, 256), BF16),
    ((4, 128, 256), BF16),
    ((128, 256), BF16),
    ((4, 32, 256), BF16),
    ((32, 256), BF16),
    ((4, 32, 256), BF16),
    ((D, D), BF16),
    ((D, 256), BF16),
    ((4, 128, 256), BF16),
    ((128, 256), BF16),
    ((4, 32, 256), BF16),
    ((32, 256), BF16),
    ((4, 32, 256), BF16),
    ((64, D), BF16),
    ((D, 256), BF16),
    ((256, D), BF16),
    ((SENT_ROWS, 128), BF16),
]
for part in ((32, 128), (32, 128), (16, 256), (16, 256)):
    SCRATCH += [((count, *part), BF16) for count in (64, 48, 16, 12, 4, 3)]


def layer_kernel(*refs):
    x_hbm, dy_hbm, states = refs[0], refs[1], refs[2:23]
    mixed_ref, ingrad_ref, kept = refs[23], refs[24], refs[25:46]
    gains_ref, biases_ref = kept[15], kept[18]
    sems, local_sems = refs[-2:]
    (
        x_ref,
        dy_ref,
        x_all,
        h1_all,
        w_all,
        out_all,
        up_all,
        down_all,
        gate_low,
        gate_t,
        proj_t,
        k_nat,
        v_nat,
        s_buf,
        e_buf,
        ds_buf,
        o_t,
        o_low,
        inv_mass,
        heads_t,
        g1_buf,
        attn_buf,
        x1_buf,
        xhat_buf,
        rstd_buf,
        h2_pair,
        g2_buf,
        act_buf,
        dgelu_buf,
        tanh_buf,
        ffn_own,
        ffn_send,
        ffn_recv,
        dffn_pair,
        dz2_full,
        dz1_full,
        dattn_full,
        dz2_half,
        dattn_half,
        dhid_buf,
        dh2_own,
        dh2_send,
        dh2_recv,
        dh2_gate,
        dheads_t,
        dz1_t,
        do_t,
        dz_t,
        vec,
        vec_s,
        vec_a,
        vec_b,
        dq_t,
        dk_t,
        dv_t,
        dproj_low,
        dproj_all,
        gq_low,
        gq_f32,
        g1_f32,
        g1_low,
        g1_sib,
        g1_send,
        g1_recv,
        gq_sib,
        gq_send,
        gq_recv,
        gq_all,
        g1t_all,
        g1_nat,
        g2_low,
        gy_recv,
        gy_sum,
        gz_recv,
        gz_sum,
        gx_recv,
        g2_all,
        gout_low,
        go_z,
        go_zs,
        go_x,
        go_xs,
        go_y,
        gout_all,
        gup_all,
        gdown_all,
        sent,
        *part_refs,
    ) = refs[46:-2]
    dp, head = lax.axis_index("dp"), lax.axis_index("head")
    x_hi, y, core = dp // 8, (dp // 2) % 4, dp % 2
    z, x_lo = head // 2, head % 2
    xx = x_hi * 2 + x_lo
    sub = x_hi * 4 + y
    links = Links(sems)

    def head_peer(o):
        return (head + o) % 8

    def in_head(o):
        return (dp, (head + o) % 8)

    def head_from(o):
        return (head + 8 - o) % 8

    def sub_peer(o):
        return (sub + o) % 8

    def in_sub(o):
        return (((sub + o) % 8) * 2 + core, head)

    def ring(axis, o):
        nx = (xx + o) % 4 if axis == "x" else xx
        ny = (y + o) % 4 if axis == "y" else y
        nz = (z + o) % 4 if axis == "z" else z
        return ((nx // 2) * 8 + ny * 2 + core, nz * 2 + nx % 2)

    sibling = (sub * 2 + (1 - core), head)

    barrier = pltpu.get_barrier_semaphore()
    greeted = [in_sub(o) for o in range(7, 0, -1)] + [in_head(o) for o in range(7, 0, -1)]
    greeted += [((1 - x_hi) * 8 + y * 2 + core, z * 2 + 1 - x_lo), sibling]
    for device in greeted:
        pl.semaphore_signal(
            barrier, inc=1, device_id=device, device_id_type=pl.DeviceIdType.MESH
        )

    pairs = [(x_hbm, x_ref)] + [(states[i], kept[i]) for i in (0, 3, 6, 9, 15, 18, 12)]
    pairs += [(dy_hbm, dy_ref)] + [(states[i], kept[i]) for i in range(21) if i % 3]
    loads = [
        pltpu.make_async_copy(src, dst, local_sems.at[i]) for i, (src, dst) in enumerate(pairs)
    ]
    for load in loads[0:9]:
        load.start()

    own = pl.ds(aligned(head * ROWS, ROWS), ROWS)
    own_core = pl.ds(aligned(core * ROWS, ROWS), ROWS)
    sib_core = pl.ds(aligned((1 - core) * ROWS, ROWS), ROWS)
    half = pl.ds(aligned(core * 256, 256), 256)
    sib_half = pl.ds(aligned((1 - core) * 256, 256), 256)
    own_heads = pl.ds(aligned(head * 64, 64), 64)
    own_w = pl.ds(aligned(head * 192, 64), 192)
    sub_rows = pl.ds(aligned(sub * 128, 128), 128)

    def rows_of(ref, first, unit):
        def at(s):
            parts = ((0, unit), (0, unit // 2), (unit // 2, unit // 2))
            return [ref.at[pl.ds(aligned(first(s) + a, unit // 2), n), :] for a, n in parts]

        return at

    def up_at(s):
        cols = pl.ds(aligned(s * 128, 128), 128)
        first = (y % 2) * 256
        parts = ((0, 256), (0, 128), (128, 128))
        return [up_all.at[pl.ds(aligned(first + a, 128), n), cols] for a, n in parts]

    class Spread:
        def __init__(self, at, three, four, seven=None, last=None):
            self.at, self.last, self.one = at, last, at(head)[0]
            self.ring_z = Group(links, three, 3, self.one)
            self.over_x = Group(links, four)
            self.over_last = None if last is None else Group(links, seven)

        def begin(self):
            for o in range(1, 4):
                self.ring_z.send(self.one, self.one, ring("z", o), o - 1)

        def begin_x(self):
            self.forward(head)

        def forward(self, s):
            _, first, second = self.at(s)
            self.over_x.send(first, first, ring("x", 1))
            self.over_x.send(second, second, ring("x", 3))

        def pass_on(self):
            for o in range(1, 4):
                self.ring_z.wait(o - 1)
                s = ((z + 4 - o) % 4) * 2 + x_lo
                self.forward(s)
                if self.last is not None:
                    self.last(self.over_last, *self.at(s))

        def pass_last(self):
            self.over_x.wait()
            for o in range(4):
                self.last(self.over_last, *self.at(((z + o) % 4) * 2 + 1 - x_lo))

    def to_sibling(group, whole, first, second):
        group.send(whole, whole, sibling)

    def to_both_y(group, whole, first, second):
        group.send(first, first, ring("y", 1))
        group.send(second, second, ring("y", 3))

    spread_out = Spread(
        rows_of(out_all, lambda s: s * 64 + core * 32, 32),
        out_all.at[0:96, :],
        out_all.at[0:128, :],
        out_all.at[0:224, :],
        to_sibling,
    )
    spread_up = Spread(
        up_at,
        up_all.at[0:256, 0:384],
        up_all.at[0:256, 0:512],
        up_all.at[0:256, 0:896],
        to_both_y,
    )
    spread_down = Spread(
        rows_of(down_all, lambda s: s * 128 + (y % 2) * 64, 64),
        down_all.at[0:192, :],
        down_all.at[0:256, :],
        down_all.at[0:448, :],
        to_both_y,
    )
    spread_w = Spread(
        rows_of(w_all, lambda s: s * 192 + core * 96, 96),
        w_all.at[0:288, :],
        w_all.at[0:384, :],
        w_all.at[0:672, :],
        to_sibling,
    )
    x_group = Group(links, x_all.at[0 : 7 * ROWS, :], 7, x_ref)

    class Groups:
        pass

    g = Groups()

    beside = (dp, z * 2 + 1 - x_lo)
    gain_one, shift_one = pl.ds(0, 1), pl.ds(0, 1)
    gain_two, shift_two = pl.ds(1, 1), pl.ds(1, 1)

    def project(block):
        for s in range(4):
            rows = pl.ds(aligned(block * ROWS + 32 * s, 32), 32)
            v = x_all[rows, :].astype(F32)
            center = v - jnp.mean(v, axis=-1, keepdims=True)
            spread = jnp.mean(center * center, axis=-1, keepdims=True)
            h = center * lax.rsqrt(spread + NORM_EPS) * gains_ref[gain_one, :] + biases_ref[shift_one, :]
            h1_all[rows, :] = h.astype(BF16)
        rows = pl.ds(aligned(block * ROWS, ROWS), ROWS)
        pt = dot(w_all[own_w, :], h1_all[rows, :], NT)
        proj_t[0:64, rows] = (pt[0:64].astype(BF16).astype(F32) * 0.125).astype(BF16)
        proj_t[64:192, rows] = pt[64:192].astype(BF16)
        k_nat[rows, :] = pt[64:128].T.astype(BF16)
        v_nat[rows, :] = pt[128:192].T.astype(BF16)

    def from_z(o):
        return ((z + 4 - o) % 4) * 2

    place = {"x": xx, "y": y, "z": z}

    class Staged:
        def __init__(self, axes, refs):
            self.axes, self.refs, self.step, self.group = axes, refs, 0, None

        def put(self, ch, value):
            a, b, c = (ch[axis] for axis in self.axes)
            self.refs[0][a * 16 + b * 4 + c] = value

        def send(self):
            axis, size = self.axes[self.step], (16, 4, 1)[self.step]
            src, got = self.refs[2 * self.step : 2 * self.step + 2]
            self.group = Group(links, got)
            for o in range(1, 4):
                t = (place[axis] + o) % 4
                block = got.at[pl.ds((o - 1) * size, size)]
                self.group.send(src.at[pl.ds(t * size, size)], block, ring(axis, o))

        def add(self, store=None):
            at, size = place[self.axes[self.step]], (16, 4, 1)[self.step]
            src, got = self.refs[2 * self.step : 2 * self.step + 2]
            self.group.wait()
            self.step += 1
            to = None if store else self.refs[2 * self.step]

            def some(i, n):
                total = src[pl.ds(at * size + i, n)].astype(F32)
                for o in range(3):
                    total = total + got[pl.ds(o * size + i, n)].astype(F32)
                return total.astype(BF16)

            if store:
                store(some(0, 1)[0])
                return

            def body(i, carry):
                to[pl.ds(i * 4, 4)] = some(i * 4, 4)
                return carry

            lax.fori_loop(0, size // 4, body, 0)

        def next(self):
            self.add()
            self.send()

    up_a, up_b, down_a, down_b = (
        Staged(axes, part_refs[6 * i : 6 * i + 6])
        for i, axes in enumerate(("yzx", "xyz", "yxz", "zxy"))
    )

    def chip_of(h, n):
        return {"x": (n // 4) * 2 + h % 2, "y": n % 4, "z": h // 2}

    def add_slots(ref, n=8):
        total = ref[0].astype(F32)
        for o in range(1, n):
            total = total + ref[o].astype(F32)
        return total

    def block_of(ref, at, rows, cols=slice(None)):
        return ref.at[pl.ds(aligned(at * rows, rows), rows), cols]

    def to_all(group, peers, ref):
        for o in range(1, 4 if peers not in (in_head, in_sub) else 8):
            group.send(ref, ref, peers(o))

    def in_ring(axis):
        return lambda o: ring(axis, o)

    def update(i, grad, first=0, rows=None):
        rows = SHAPES[i][0] if rows is None else rows
        step = 32 if SHAPES[i][1] == D else 64

        def strip(n, carry):
            at = pl.ds(aligned(n * step, step), step)
            into = pl.ds(aligned(first + n * step, step), step)
            refs = kept[3 * i : 3 * i + 3]
            values = adamw(*(r[into, :] for r in refs), grad[at, :].astype(F32), RATES[i])
            for r, value in zip(refs, values):
                r[into, :] = value
            return carry

        lax.fori_loop(0, rows // step, strip, 0, unroll=2)


    def x_out():
        for o in range(1, 4):
            x_group.send(x_ref, x_all.at[own, :], ring("z", o), o - 1)
        x_group.send(x_ref, x_all.at[own, :], beside, 3)

    def cast_weights():
        for load in loads[1:5]:
            load.wait()
        w_all[own_w, :] = kept[0][...].astype(BF16)
        out_all[own_heads, :] = kept[3][...].astype(BF16)
        up_all[:, own] = kept[6][:, own_core].astype(BF16)
        down_all[own, :] = kept[9][own_core, :].astype(BF16)

    def load_rest():
        for load in loads[9:]:
            load.start()
        for load in loads[5:9]:
            load.wait()
        for i in range(2):
            gate_low[i] = kept[12][D * i : D * i + D, :].astype(BF16)
        for n in range(4):
            cols = slice(128 * n, 128 * n + 128)
            gate_t[cols, :] = kept[12][0:D, cols].T.astype(BF16)

    def project_own():
        project(head)

    def x_pass_z():
        x_group.wait(3)
        block = block_of(x_all, z * 2 + 1 - x_lo, ROWS)
        x_group.send(block, block, ring("z", 1), 4)
        x_group.send(block, block, ring("z", 3), 5)

    def project_beside():
        project(z * 2 + 1 - x_lo)

    def from_z(o):
        return ((z + 4 - o) % 4) * 2

    def project_near():
        x_group.wait(0)
        project(from_z(1) + x_lo)
        x_group.wait(2)
        project(from_z(3) + x_lo)

    def x_pass_x():
        x_group.wait(1)
        block = block_of(x_all, from_z(2) + x_lo, ROWS)
        x_group.send(block, block, beside, 6)

    def project_far():
        project(from_z(2) + x_lo)

    def project_passed():
        x_group.wait(4)
        project(from_z(1) + 1 - x_lo)
        x_group.wait(5)
        project(from_z(3) + 1 - x_lo)

    def project_last():
        x_group.wait(6)
        project(from_z(2) + 1 - x_lo)


    def attention():
        for j in range(LEN // QB):
            cols = slice(QB * j, QB * (j + 1))
            queries = proj_t[0:64, cols]
            ceiling = jnp.full((1, QB), -1e30, F32)
            tiles = QB * (j + 1) // ROWS
            for t in range(tiles):
                s = dot(k_nat[ROWS * t : ROWS * (t + 1), :], queries)
                if ROWS * t >= QB * j:
                    keys_at = lax.broadcasted_iota(jnp.int32, (ROWS, QB), 0) + ROWS * t
                    queries_at = lax.broadcasted_iota(jnp.int32, (ROWS, QB), 1) + QB * j
                    s = jnp.where(keys_at <= queries_at, s, -1e30)
                s_buf[ROWS * t : ROWS * (t + 1), :] = s
                ceiling = jnp.maximum(ceiling, jnp.max(s, axis=0, keepdims=True))
            mass = jnp.zeros((1, QB), F32)
            for t in range(tiles):
                e = jnp.exp(s_buf[ROWS * t : ROWS * (t + 1), :] - ceiling)
                mass = mass + jnp.sum(e, axis=0, keepdims=True)
                e_buf[ROWS * t : ROWS * (t + 1), cols] = e.astype(BF16)
            total = dot(proj_t[128:192, 0 : QB * (j + 1)], e_buf[0 : QB * (j + 1), cols])
            total = total / mass
            o_t[:, cols] = total
            o_low[:, cols] = total.astype(BF16)
            inv_mass[:, cols] = 1.0 / mass
        group = g.heads = Group(links, heads_t.at[0:448, 0:ROWS])
        for o in range(1, 8):
            block = o_low.at[:, pl.ds(aligned(head_peer(o) * ROWS, ROWS), ROWS)]
            group.send(block, heads_t.at[own_heads, own_core], in_head(o))
        heads_t[own_heads, own_core] = o_low[:, own]


    def gate_one():
        g1_buf[...] = dot(h1_all[own, :], gate_low[0]) + biases_ref[2:3, :]

    def middle():
        g.heads.wait()
        group = g.heads_pair = Group(links, heads_t.at[:, 0:ROWS])
        group.send(heads_t.at[:, own_core], heads_t.at[:, own_core], sibling)
        spread_out.over_last.wait()
        attn_buf[...] = dot(heads_t[:, own_core], out_all[...], TN)
        for s in range(4):
            rows = slice(32 * s, 32 * s + 32)
            g1 = jax.nn.sigmoid(g1_buf[rows, :])
            g1_buf[rows, :] = g1
            x = x_ref[rows, :].astype(F32)
            x1 = g1 * attn_buf[rows, :] + (1.0 - g1) * x
            x1_buf[rows, :] = x1
            center = x1 - jnp.mean(x1, axis=-1, keepdims=True)
            spread = jnp.mean(center * center, axis=-1, keepdims=True)
            rstd = lax.rsqrt(spread + NORM_EPS)
            xhat = center * rstd
            xhat_buf[rows, :] = xhat
            rstd_buf[rows, :] = jnp.broadcast_to(rstd, (32, 128))
            h2 = xhat * gains_ref[gain_two, :] + biases_ref[shift_two, :]
            h2_pair[pl.ds(aligned(core * ROWS + 32 * s, 32), 32), :] = h2.astype(BF16)
        group = g.h2 = Group(links, h2_pair.at[0:ROWS, :])
        group.send(h2_pair.at[own_core, :], h2_pair.at[own_core, :], sibling)

    def gate_two():
        g2_buf[...] = dot(h2_pair[own_core, :], gate_low[1]) + biases_ref[3:4, :]

    def hidden():
        g.h2.wait()
        spread_up.over_last.wait()
        for n in range(4):
            cols = slice(256 * n, 256 * n + 256)
            u = dot(h2_pair[...], up_all[:, cols])
            c0 = 0.7978845608028654
            inner = jnp.tanh(c0 * (u + 0.044715 * u * u * u))
            act_buf[:, cols] = (0.5 * u * (1.0 + inner)).astype(BF16)
            dgelu_buf[:, cols] = u
            tanh_buf[:, cols] = inner

    def gelu_slope():
        c0 = 0.7978845608028654

        def strip(n, carry):
            rows = pl.ds(aligned(n * 16, 16), 16)
            u, inner = dgelu_buf[rows, :], tanh_buf[rows, :]
            slope = (1.0 - inner * inner) * (c0 + 3.0 * 0.044715 * c0 * u * u)
            dgelu_buf[rows, :] = 0.5 * (1.0 + inner) + 0.5 * u * slope
            return carry

        lax.fori_loop(0, 16, strip, 0)

    def ffn():
        spread_down.over_last.wait()
        ffn_send[...] = dot(act_buf[sib_core, :], down_all[...]).astype(BF16)
        g.ffn = Group(links, ffn_recv)
        g.ffn.send(ffn_send, ffn_recv, sibling)
        ffn_own[...] = dot(act_buf[own_core, :], down_all[...])

    def mix():
        g.ffn.wait()
        bias_two = jnp.zeros((1, D), F32)
        for s in range(4):
            rows = slice(32 * s, 32 * s + 32)
            total = ffn_own[rows, :] + ffn_recv[rows, :].astype(F32)
            g2 = jax.nn.sigmoid(g2_buf[rows, :])
            g2_buf[rows, :] = g2
            x1 = x1_buf[rows, :]
            dy = dy_ref[rows, :].astype(F32)
            mixed_ref[rows, :] = g2 * total + (1.0 - g2) * x1
            dffn_pair[pl.ds(aligned(core * ROWS + 32 * s, 32), 32), :] = (g2 * dy).astype(BF16)
            dz = (dy * (total - x1) * g2 * (1.0 - g2)).astype(BF16)
            dz2_full[rows, :] = dz
            bias_two = bias_two + jnp.sum(dz.astype(F32), axis=0, keepdims=True)
        group = g.dffn = Group(links, dffn_pair.at[0:ROWS, :])
        group.send(dffn_pair.at[own_core, :], dffn_pair.at[own_core, :], sibling)
        group = g.dz2 = Group(links, dz2_half.at[0:ROWS, :])
        group.send(dz2_full.at[:, sib_half], dz2_half.at[own_core, :], sibling)
        dz2_half[own_core, :] = dz2_full[:, half]
        vec[5:6, :] = bias_two
        vec[6:8, :] = jnp.zeros((2, D), F32)


    def back_gate_two():
        dh2_gate[...] = dot(dz2_full[...], gate_low[1], NT)

    def back_hidden():
        g.dffn.wait()
        for n in range(4):
            cols = slice(256 * n, 256 * n + 256)
            da = dot(dffn_pair[...], down_all[cols, :], NT)
            dhid_buf[:, cols] = (da * dgelu_buf[:, cols]).astype(BF16)
        dh2_send[...] = dot(dhid_buf[sib_core, :], up_all[...], NT).astype(BF16)
        g.dh2 = Group(links, dh2_recv)
        g.dh2.send(dh2_send, dh2_recv, sibling)
        dh2_own[...] = dot(dhid_buf[own_core, :], up_all[...], NT)

    def back_middle():
        g.dh2.wait()
        gain_sum = jnp.zeros((1, D), F32)
        shift_sum = jnp.zeros((1, D), F32)
        bias_one = jnp.zeros((1, D), F32)
        for s in range(4):
            rows = slice(32 * s, 32 * s + 32)
            dh2 = dh2_own[rows, :] + dh2_recv[rows, :].astype(F32) + dh2_gate[rows, :]
            xhat = xhat_buf[rows, :]
            gain_sum = gain_sum + jnp.sum(dh2 * xhat, axis=0, keepdims=True)
            shift_sum = shift_sum + jnp.sum(dh2, axis=0, keepdims=True)
            dxhat = dh2 * gains_ref[gain_two, :]
            mean_a = jnp.mean(dxhat, axis=-1, keepdims=True)
            mean_b = jnp.mean(dxhat * xhat, axis=-1, keepdims=True)
            rstd = rstd_buf[rows, 0:1]
            dx1 = (1.0 - g2_buf[rows, :]) * dy_ref[rows, :].astype(F32) + rstd * (
                dxhat - mean_a - xhat * mean_b
            )
            g1 = g1_buf[rows, :]
            dattn_full[rows, :] = (g1 * dx1).astype(BF16)
            x = x_ref[rows, :].astype(F32)
            dz = (dx1 * (attn_buf[rows, :] - x) * g1 * (1.0 - g1)).astype(BF16)
            dz1_full[rows, :] = dz
            bias_one = bias_one + jnp.sum(dz.astype(F32), axis=0, keepdims=True)
            ingrad_ref[rows, :] = (1.0 - g1) * dx1
        dheads_t[...] = dot(out_all[...], dattn_full[...], NT).astype(BF16)
        group = g.back = Group(links, do_t.at[:, 0 : 7 * ROWS])
        for o in range(1, 8):
            group.send(block_of(dheads_t, head_peer(o), 64), do_t.at[:, own], in_head(o))
        do_t[:, own] = dheads_t[own_heads, :]
        group = g.dattn = Group(links, dattn_half.at[0:ROWS, :])
        group.send(dattn_full.at[:, sib_half], dattn_half.at[own_core, :], sibling)
        dattn_half[own_core, :] = dattn_full[:, half]
        vec[1:2, :] = gain_sum
        vec[3:4, :] = shift_sum
        vec[4:5, :] = bias_one

    def back_first():
        dz1_t[...] = dz1_full[...].astype(F32).T.astype(BF16)
        group = g.back_first = Group(links, dz_t.at[:, 0 : 7 * ROWS])
        for o in range(1, 8):
            group.send(block_of(dz1_t, head_peer(o), 64), dz_t.at[:, own], in_head(o))
        dz_t[:, own] = dz1_t[own_heads, :]

    def back_attention():
        g.back.wait()
        dk_t[...] = jnp.zeros_like(dk_t)
        dv_t[...] = jnp.zeros_like(dv_t)
        for j in range(LEN // QB):
            cols = slice(QB * j, QB * (j + 1))
            upto = QB * (j + 1)
            queries = proj_t[0:64, cols]
            grads = do_t[:, cols]
            inverse = inv_mass[:, cols]
            delta = jnp.sum(o_t[:, cols] * grads.astype(F32), axis=0, keepdims=True)
            for t in range(upto // ROWS):
                keys = slice(ROWS * t, ROWS * (t + 1))
                p = e_buf[keys, cols].astype(F32) * inverse
                ds_buf[keys, :] = (p * (dot(v_nat[keys, :], grads) - delta)).astype(BF16)
            dq_t[:, cols] = dot(proj_t[64:128, 0:upto], ds_buf[0:upto, :]) * 0.125
            dk_t[:, 0:upto] += dot(queries, ds_buf[0:upto, :], NT)
            scaled = (grads.astype(F32) * inverse).astype(BF16)
            dv_t[:, 0:upto] += dot(scaled, e_buf[0:upto, cols], NT)
        dproj_low[0:64, :] = dq_t[...].astype(BF16)
        dproj_low[64:128, :] = dk_t[...].astype(BF16)
        dproj_low[128:192, :] = dv_t[...].astype(BF16)
        group = g.dproj = Group(links, dproj_all.at[0 : 7 * 192, :])
        for o in range(1, 8):
            block = dproj_low.at[:, pl.ds(aligned(head_peer(o) * ROWS, ROWS), ROWS)]
            group.send(block, dproj_all.at[own_w, :], in_head(o))
        dproj_all[own_w, :] = dproj_low[:, own]

    def input_grad():
        g.dproj.wait()
        spread_w.over_last.wait()
        dh2_own[...] = dot(dproj_all[...], w_all[...], TN) + dot(
            dz1_full[...], gate_low[0], NT
        )
        for s in range(4):
            rows = slice(32 * s, 32 * s + 32)
            v = x_ref[rows, :].astype(F32)
            center = v - jnp.mean(v, axis=-1, keepdims=True)
            spread = jnp.mean(center * center, axis=-1, keepdims=True)
            rstd = lax.rsqrt(spread + NORM_EPS)
            xhat = center * rstd
            dxhat = dh2_own[rows, :] * gains_ref[gain_one, :]
            mean_a = jnp.mean(dxhat, axis=-1, keepdims=True)
            mean_b = jnp.mean(dxhat * xhat, axis=-1, keepdims=True)
            ingrad_ref[rows, :] += rstd * (dxhat - mean_a - xhat * mean_b)

    def vec_pair():
        gain = jnp.zeros((1, D), F32)
        shift = jnp.zeros((1, D), F32)
        gate_rows = gate_t[own_heads, :]
        for n in range(4):
            rows = slice(64 * n, 64 * n + 64)
            grads = (dproj_low[rows, :] if n < 3 else dz_t[...]).astype(F32)
            sums = jnp.sum(grads, axis=1, keepdims=True)
            weights = w_all[pl.ds(aligned(head * 192 + 64 * n, 64), 64), :] if n < 3 else gate_rows
            weights = weights.astype(F32)
            products = gq_f32[rows, :] if n < 3 else g1_f32[...]
            moved = products - biases_ref[shift_one, :] * sums
            gain = gain + jnp.sum(weights * moved, axis=0, keepdims=True)
            shift = shift + jnp.sum(weights * sums, axis=0, keepdims=True)
        vec[0:1, :] = gain / gains_ref[gain_one, :]
        vec[2:3, :] = shift
        g.vec_pair = Group(links, vec_s)
        g.vec_pair.send(vec, vec_s, sibling)

    def vec_sub():
        g.vec_pair.wait()
        vec_a[sub] = vec[...] + vec_s[...]
        g.vec_sub = Group(links, vec_a.at[0:7])
        to_all(g.vec_sub, in_sub, vec_a.at[sub])

    def vec_head():
        g.vec_sub.wait()
        vec_b[head] = add_slots(vec_a)
        g.vec_head = Group(links, vec_b.at[0:7])
        to_all(g.vec_head, in_head, vec_b.at[head])

    def vec_done():
        g.vec_head.wait()
        total = add_slots(vec_b)
        for i, grad in ((5, total[0:2]), (6, total[2:6])):
            refs = kept[3 * i : 3 * i + 3]
            for r, value in zip(refs, adamw(*(r[...] for r in refs), grad, RATES[i])):
                r[...] = value


    def grad_down():
        for h in range(8):
            gd = dot(act_buf[:, 128 * h : 128 * h + 128], dffn_pair[...], TN).astype(BF16)
            for n in range(8):
                down_a.put(chip_of(h, n), gd[16 * n : 16 * n + 16, 0:256])
                down_b.put(chip_of(h, n), gd[16 * n : 16 * n + 16, 256:512])

    def grad_up():
        for h in range(8):
            gu = dot(h2_pair[...], dhid_buf[:, 128 * h : 128 * h + 128], TN).astype(BF16)
            for n in range(8):
                up_a.put(chip_of(h, n), gu[64 * n : 64 * n + 32, :])
                up_b.put(chip_of(h, n), gu[64 * n + 32 : 64 * n + 64, :])

    def down_sub():
        rows = pl.ds(aligned(core * 128 + sub * 16, 16), 16)
        for part, cols in ((down_a, slice(0, 256)), (down_b, slice(256, 512))):

            def store(value, cols=cols):
                gdown_all[rows, cols] = value

            part.add(store)
        g.down_sub = Group(links, gdown_all.at[0:112, :])
        to_all(g.down_sub, in_sub, gdown_all.at[rows, :])

    def down_pair():
        g.down_sub.wait()
        group = g.down_pair = Group(links, gdown_all.at[0:128, :])
        group.send(gdown_all.at[own_core, :], gdown_all.at[own_core, :], sibling)

    def down_done():
        g.down_pair.wait()
        update(3, gdown_all)

    def up_sub():
        for part, first in ((up_a, 0), (up_b, 32)):

            def store(value, first=first):
                gup_all[pl.ds(aligned(sub * 64 + first, 32), 32), own_core] = value

            part.add(store)
        block = block_of(gup_all, sub, 64, own_core)
        g.up_sub = Group(links, gup_all.at[0:448, 0:128])
        to_all(g.up_sub, in_sub, block)

    def up_pair():
        g.up_sub.wait()
        group = g.up_pair = Group(links, gup_all.at[:, 0:128])
        group.send(gup_all.at[:, own_core], gup_all.at[:, own_core], sibling)

    def up_done():
        g.up_pair.wait()
        update(2, gup_all)


    def second_y():
        g.dz2.wait()
        g2_low[...] = dot(h2_pair[...], dz2_half[...], TN).astype(BF16)
        group = g.second_y = Group(links, gy_recv.at[0:3])
        for o in range(1, 4):
            group.send(block_of(g2_low, (y + o) % 4, 128), gy_recv.at[y], ring("y", o))
        gy_recv[y] = g2_low[pl.ds(aligned(y * 128, 128), 128), :]

    def second_z():
        g.second_y.wait()
        gy_sum[...] = add_slots(gy_recv, 4).astype(BF16)
        group = g.second_z = Group(links, gz_recv.at[0:3])
        for o in range(1, 4):
            group.send(block_of(gy_sum, (z + o) % 4, 32), gz_recv.at[z], ring("z", o))
        gz_recv[z] = gy_sum[pl.ds(aligned(z * 32, 32), 32), :]

    def second_x():
        g.second_z.wait()
        gz_sum[...] = add_slots(gz_recv, 4).astype(BF16)
        group = g.second_x = Group(links, gx_recv.at[0:3])
        for o in range(1, 4):
            group.send(gz_sum, gx_recv.at[xx], ring("x", o))
        gx_recv[xx] = gz_sum[...]

    def second_back_z():
        g.second_x.wait()
        rows = pl.ds(aligned(y * 128 + z * 32, 32), 32)
        g2_all[rows, half] = add_slots(gx_recv, 4).astype(BF16)
        g.second_back_z = Group(links, gz_recv.at[0:3])
        to_all(g.second_back_z, in_ring("z"), g2_all.at[rows, half])

    def second_back_y():
        g.second_back_z.wait()
        block = block_of(g2_all, y, 128, half)
        g.second_back_y = Group(links, gy_recv.at[0:3])
        to_all(g.second_back_y, in_ring("y"), block)

    def second_pair():
        g.second_back_y.wait()
        group = g.second_pair = Group(links, g2_low)
        group.send(g2_all.at[:, half], g2_all.at[:, half], sibling)

    def second_done():
        g.second_pair.wait()
        update(4, g2_all, D, D)


    def grad_out_z():
        g.heads_pair.wait()
        g.dattn.wait()
        gout_low[...] = dot(heads_t[...], dattn_half[...]).astype(BF16)
        group = g.grad_out_z = Group(links, go_z.at[0:3])
        for o in range(1, 4):
            group.send(block_of(gout_low, (z + o) % 4, 128), go_z.at[z], ring("z", o))
        go_z[z] = gout_low[pl.ds(aligned(z * 128, 128), 128), :]

    def grad_out_x():
        g.grad_out_z.wait()
        go_zs[...] = add_slots(go_z, 4).astype(BF16)
        group = g.grad_out_x = Group(links, go_x.at[0:3])
        for o in range(1, 4):
            to = (xx + o) % 4
            block = block_of(go_zs, (to % 2) * 2 + to // 2, 32)
            group.send(block, go_x.at[xx], ring("x", o))
        go_x[xx] = go_zs[pl.ds(aligned((x_lo * 2 + x_hi) * 32, 32), 32), :]

    def grad_out_y():
        g.grad_out_x.wait()
        go_xs[...] = add_slots(go_x, 4).astype(BF16)
        group = g.grad_out_y = Group(links, go_y.at[0:3])
        for o in range(1, 4):
            group.send(go_xs, go_y.at[y], ring("y", o))
        go_y[y] = go_xs[...]

    def grad_out_far():
        g.grad_out_y.wait()
        rows = pl.ds(aligned(x_hi * 32, 32), 32)
        gout_all[rows, half] = add_slots(go_y, 4).astype(BF16)
        group = g.grad_out_far = Group(links, go_xs)
        group.send(gout_all.at[rows, half], gout_all.at[rows, half], ring("x", 2))

    def grad_out_pair():
        g.grad_out_far.wait()
        group = g.grad_out_pair = Group(links, go_zs.at[0:64, :])
        group.send(gout_all.at[:, half], gout_all.at[:, half], sibling)

    def grad_out_done():
        g.grad_out_pair.wait()
        update(1, gout_all)


    def qkv_pair():
        gq_f32[...] = dot(dproj_low[...], h1_all[...])
        gq_low[...] = gq_f32[...].astype(BF16)
        g.qkv_pair = Group(links, gq_sib)
        g.qkv_pair.send(gq_low.at[:, sib_half], gq_sib, sibling)

    def qkv_sub():
        g.qkv_pair.wait()
        total = gq_low[:, half].astype(F32) + gq_sib[...].astype(F32)
        for i in range(8):
            r, c = 48 * (i // 2), 128 * (i % 2)
            gq_send[i] = total[r : r + 48, c : c + 128].astype(BF16)
        group = g.qkv_sub = Group(links, gq_recv.at[0:7])
        for o in range(1, 8):
            group.send(gq_send.at[sub_peer(o)], gq_recv.at[sub], in_sub(o))
        gq_recv[sub] = gq_send[sub]

    def qkv_back():
        g.qkv_sub.wait()
        rows = pl.ds(aligned((sub // 2) * 48, 48), 48)
        cols = pl.ds(aligned(core * 256 + (sub % 2) * 128, 128), 128)
        gq_all[rows, cols] = add_slots(gq_recv).astype(BF16)
        g.qkv_back = Group(links, gq_recv.at[0:7])
        to_all(g.qkv_back, in_sub, gq_all.at[rows, cols])


    def first_start():
        g.back_first.wait()
        g1_f32[...] = dot(dz_t[...], h1_all[...])
        g1_low[...] = g1_f32[...].astype(BF16)
        g.first_start = Group(links, g1_sib)
        g.first_start.send(g1_low.at[:, sib_half], g1_sib, sibling)

    def first_sub():
        g.first_start.wait()
        total = g1_low[:, half].astype(F32) + g1_sib[...].astype(F32)
        for i in range(8):
            r, c = 16 * (i // 2), 128 * (i % 2)
            g1_send[i] = total[r : r + 16, c : c + 128].astype(BF16)
        group = g.first_sub = Group(links, g1_recv.at[0:7])
        for o in range(1, 8):
            group.send(g1_send.at[sub_peer(o)], g1_recv.at[sub], in_sub(o))
        g1_recv[sub] = g1_send[sub]

    def first_back():
        g.first_sub.wait()
        rows = pl.ds(aligned(head * 64 + (sub // 2) * 16, 16), 16)
        cols = pl.ds(aligned(core * 256 + (sub % 2) * 128, 128), 128)
        g1t_all[rows, cols] = add_slots(g1_recv).astype(BF16)
        g.first_back = Group(links, g1_recv.at[0:7])
        to_all(g.first_back, in_sub, g1t_all.at[rows, cols])

    def first_head():
        g.first_back.wait()
        g.first_head = Group(links, g1t_all.at[0:448, 0:256])
        to_all(g.first_head, in_head, g1t_all.at[own_heads, half])

    def qkv_back_pair():
        g.qkv_back.wait()
        g.qkv_back_pair = Group(links, gq_sib)
        g.qkv_back_pair.send(gq_all.at[:, half], gq_all.at[:, half], sibling)

    def qkv_done():
        g.qkv_back_pair.wait()
        update(0, gq_all)

    def first_pair():
        g.first_head.wait()
        group = g.first_pair = Group(links, g2_low)
        group.send(g1t_all.at[:, half], g1t_all.at[:, half], sibling)

    def first_done():
        g.first_pair.wait()
        for n in range(4):
            at = slice(128 * n, 128 * n + 128)
            g1_nat[at, :] = g1t_all[:, at].astype(F32).T
        update(4, g1_nat, 0, D)

    def moments():
        for load in loads[9:]:
            load.wait()

    loads[0].wait()
    x_all[own, :] = x_ref[...]
    pl.semaphore_wait(barrier, len(greeted))
    for run in (
        x_out,
        cast_weights,
        spread_up.begin_x,
        x_pass_z,
        spread_up.begin,
        load_rest,
        spread_down.begin,
        x_pass_x,
        project_beside,
        project_own,
        spread_out.begin_x,
        project_far,
        spread_out.begin,
        spread_down.begin_x,
        project_passed,
        project_near,
        project_last,
        spread_up.pass_on,
        attention,
        spread_down.pass_on,
        spread_out.pass_on,
        spread_up.pass_last,
        spread_w.begin,
        spread_down.pass_last,
        spread_w.begin_x,
        spread_out.pass_last,
        gate_one,
        middle,
        hidden,
        ffn,
        gelu_slope,
        spread_w.pass_on,
        gate_two,
        mix,
        back_gate_two,
        back_hidden,
        second_y,
        back_middle,
        back_first,
        grad_down,
        down_a.send,
        grad_up,
        up_a.send,
        up_b.send,
        grad_out_z,
        second_z,
        first_start,
        down_b.send,
        first_sub,
        down_a.next,
        grad_out_x,
        second_x,
        back_attention,
        up_a.next,
        qkv_pair,
        first_back,
        grad_out_y,
        down_b.next,
        up_b.next,
        qkv_sub,
        vec_pair,
        spread_w.pass_last,
        second_back_z,
        grad_out_far,
        vec_sub,
        up_b.next,
        down_a.next,
        up_a.next,
        down_b.next,
        first_head,
        second_back_y,
        input_grad,
        qkv_back,
        up_sub,
        grad_out_pair,
        down_sub,
        moments,
        grad_out_done,
        vec_head,
        second_pair,
        first_pair,
        second_done,
        qkv_back_pair,
        first_done,
        up_pair,
        down_pair,
        qkv_done,
        vec_done,
        up_done,
        down_done,
    ):
        run()
    links.drain(sent)


VMEM = pl.BlockSpec(memory_space=pltpu.VMEM)
ANY = pl.BlockSpec(memory_space=pl.ANY)
HBM = pl.BlockSpec(memory_space=pltpu.HBM)


def run_layer(*args):
    in_vmem = [pltpu.VMEM(s, F32) for s in SHAPES for _ in range(3)]
    shapes = [pltpu.VMEM((ROWS, D), F32)] * 2
    return pl.pallas_call(
        layer_kernel,
        out_shape=shapes + in_vmem,
        in_specs=[HBM] * 23,
        out_specs=[VMEM] * 23,
        scratch_shapes=[pltpu.VMEM(s, t) for s, t in SCRATCH]
        + [pltpu.SemaphoreType.DMA((N_SEMS,)), pltpu.SemaphoreType.DMA((N_LOCAL,))],
        compiler_params=pltpu.CompilerParams(
            collective_id=0, has_side_effects=True, vmem_limit_bytes=44 * 1024 * 1024
        ),
        name="layer",
    )(*args)


def finish_kernel(*refs):
    sems = refs[46]
    copies = [
        pltpu.make_async_copy(refs[i], refs[23 + i], sems.at[i]) for i in range(23)
    ]
    for c in copies:
        c.start()
    for c in copies:
        c.wait()


def finish(results):
    return pl.pallas_call(
        finish_kernel,
        out_shape=[jax.ShapeDtypeStruct(a.shape, F32) for a in results],
        in_specs=[ANY] * 23,
        out_specs=[ANY] * 23,
        scratch_shapes=[pltpu.SemaphoreType.DMA((23,))],
        compiler_params=pltpu.CompilerParams(vmem_limit_bytes=1024 * 1024),
        name="finish",
    )(*results)


def local(inputs, cotangent, *state):
    rows = inputs.shape[1]
    flat = list(state)
    for i in (0, 1, 2):
        flat[i] = jnp.transpose(flat[i], (0, 2, 1)).reshape(192, D)
    for i in (12, 13, 14):
        flat[i] = flat[i].reshape(2 * D, D)
    operands = (inputs.reshape(rows, D), cotangent.reshape(rows, D), *flat)
    results = run_layer(*(pltpu.with_memory_space_constraint(a, pltpu.HBM) for a in operands))
    mixed, ingrad, *new = finish(results)
    for i in (0, 1, 2):
        new[i] = jnp.transpose(new[i].reshape(3, 64, D), (0, 2, 1))
    for i in (12, 13, 14):
        new[i] = new[i].reshape(2, D, D)
    return (mixed.reshape(1, rows, D), ingrad.reshape(1, rows, D), *new)


def solution(mesh):
    batch = P("dp", "head", None)
    qkv = P(None, None, "head")
    first = P("head", None)
    second = P(None, "head")
    state = (qkv,) * 3 + (first,) * 3 + (second,) * 3 + (first,) * 3 + (P(),) * 9
    return jax.shard_map(
        local,
        mesh=mesh,
        in_specs=(batch, batch, *state),
        out_specs=(batch, batch, *state),
        check_vma=False,
    )
```

```python
import math

import jax
import jax.numpy as jnp
from jax import lax
from jax.experimental import pallas as pl
from jax.experimental.pallas import tpu as pltpu
from jax.sharding import PartitionSpec as P

F32 = jnp.float32
BF16 = jnp.bfloat16
STEP = 10
NORM_EPS = 1e-05
BETA_ONE = 0.9
BETA_TWO = 0.999
ADAM_EPS = 1e-08
DECAY = 0.01
RATES = (0.04, 0.1, 0.04, 0.02, 0.04, 0.4, 0.3)
D = 512
ROWS = 128
LEN = 1024
QB = 256
NN = ((1,), (0,))
NT = ((1,), (1,))
TN = ((0,), (0,))


def dot(a, b, dims=NN):
    return lax.dot_general(a, b, (dims, ((), ())), preferred_element_type=F32)


def aligned(value, by):
    return pl.multiple_of(value, by)


class Group:
    def __init__(self, links, total, receives=1, each=None):
        self.send_sem, self.total = links.send_sem, total
        self.each = total if each is None else each
        self.recv_sems = [links.semaphore() for _ in range(receives)]
        links.groups.append(self)

    def send(self, src, dst, device, k=0):
        pltpu.make_async_remote_copy(
            src_ref=src,
            dst_ref=dst,
            send_sem=self.send_sem,
            recv_sem=self.recv_sems[k],
            device_id=device,
            device_id_type=pl.DeviceIdType.MESH,
        ).start()

    def wait(self, k=0):
        pltpu.make_async_copy(self.each, self.each, self.recv_sems[k]).wait()


class Links:
    def __init__(self, sems):
        self.sems, self.send_sem, self.used, self.groups = sems, sems.at[0], 1, []

    def semaphore(self):
        self.used += 1
        return self.sems.at[self.used - 1]

    def drain(self, sent):
        words = [t.dtype.itemsize * math.prod(t.shape) for t in (g.total for g in self.groups)]
        if sum(words) != 2 * math.prod(sent.shape):
            raise ValueError(sum(words))
        pltpu.make_async_copy(sent, sent, self.send_sem).wait()


N_SEMS = 78
N_LOCAL = 23


SHAPES = ((192, D), (64, D), (D, 256), (256, D), (2 * D, D), (2, D), (4, D))


def adamw(weight, first, second, grad, rate):
    first = BETA_ONE * first + (1.0 - BETA_ONE) * grad
    second = BETA_TWO * second + (1.0 - BETA_TWO) * grad * grad
    root = (1.0 - BETA_TWO**STEP) ** 0.5
    step = (rate * root / (1.0 - BETA_ONE**STEP)) * first / (second * lax.rsqrt(second) + ADAM_EPS * root)
    return ((1.0 - rate * DECAY) * weight - step, first, second)


SENT_ROWS = 42816
SCRATCH = [
    ((ROWS, D), BF16),
    ((ROWS, D), BF16),
    ((LEN, D), BF16),
    ((LEN, D), BF16),
    ((1536, D), BF16),
    ((D, D), BF16),
    ((D, 1024), BF16),
    ((1024, D), BF16),
    ((2, D, D), BF16),
    ((D, D), BF16),
    ((192, LEN), BF16),
    ((LEN, 64), BF16),
    ((LEN, 64), BF16),
    ((LEN, QB), F32),
    ((LEN, LEN), BF16),
    ((LEN, QB), BF16),
    ((64, LEN), F32),
    ((64, LEN), BF16),
    ((1, LEN), F32),
    ((D, 256), BF16),
    ((ROWS, D), F32),
    ((ROWS, D), F32),
    ((ROWS, D), F32),
    ((ROWS, D), F32),
    ((ROWS, 128), F32),
    ((256, D), BF16),
    ((ROWS, D), F32),
    ((256, 1024), BF16),
    ((256, 1024), F32),
    ((256, 1024), F32),
    ((ROWS, D), F32),
    ((ROWS, D), BF16),
    ((ROWS, D), BF16),
    ((256, D), BF16),
    ((ROWS, D), BF16),
    ((ROWS, D), BF16),
    ((ROWS, D), BF16),
    ((256, 256), BF16),
    ((256, 256), BF16),
    ((256, 1024), BF16),
    ((ROWS, D), F32),
    ((ROWS, D), BF16),
    ((ROWS, D), BF16),
    ((ROWS, D), F32),
    ((D, ROWS), BF16),
    ((D, ROWS), BF16),
    ((64, LEN), BF16),
    ((64, LEN), BF16),
    ((8, D), F32),
    ((8, D), F32),
    ((8, 8, D), F32),
    ((8, 8, D), F32),
    ((64, LEN), F32),
    ((64, LEN), F32),
    ((64, LEN), F32),
    ((192, LEN), BF16),
    ((1536, ROWS), BF16),
    ((192, D), BF16),
    ((192, D), F32),
    ((64, D), F32),
    ((64, D), BF16),
    ((64, 256), BF16),
    ((8, 16, 128), BF16),
    ((8, 16, 128), BF16),
    ((192, 256), BF16),
    ((8, 48, 128), BF16),
    ((8, 48, 128), BF16),
    ((192, D), BF16),
    ((D, D), BF16),
    ((D, D), F32),
    ((D, 256), BF16),
    ((4, 128, 256), BF16),
    ((128, 256), BF16),
    ((4, 32, 256), BF16),
    ((32, 256), BF16),
    ((4, 32, 256), BF16),
    ((D, D), BF16),
    ((D, 256), BF16),
    ((4, 128, 256), BF16),
    ((128, 256), BF16),
    ((4, 32, 256), BF16),
    ((32, 256), BF16),
    ((4, 32, 256), BF16),
    ((64, D), BF16),
    ((D, 256), BF16),
    ((256, D), BF16),
    ((SENT_ROWS, 128), BF16),
]
for part in ((32, 128), (32, 128), (16, 256), (16, 256)):
    SCRATCH += [((count, *part), BF16) for count in (64, 48, 16, 12, 4, 3)]


def layer_kernel(*refs):
    x_hbm, dy_hbm, states = refs[0], refs[1], refs[2:23]
    mixed_ref, ingrad_ref, kept = refs[23], refs[24], refs[25:46]
    gains_ref, biases_ref = kept[15], kept[18]
    sems, local_sems = refs[-2:]
    (
        x_ref,
        dy_ref,
        x_all,
        h1_all,
        w_all,
        out_all,
        up_all,
        down_all,
        gate_low,
        gate_t,
        proj_t,
        k_nat,
        v_nat,
        s_buf,
        e_buf,
        ds_buf,
        o_t,
        o_low,
        inv_mass,
        heads_t,
        g1_buf,
        attn_buf,
        x1_buf,
        xhat_buf,
        rstd_buf,
        h2_pair,
        g2_buf,
        act_buf,
        dgelu_buf,
        tanh_buf,
        ffn_own,
        ffn_send,
        ffn_recv,
        dffn_pair,
        dz2_full,
        dz1_full,
        dattn_full,
        dz2_half,
        dattn_half,
        dhid_buf,
        dh2_own,
        dh2_send,
        dh2_recv,
        dh2_gate,
        dheads_t,
        dz1_t,
        do_t,
        dz_t,
        vec,
        vec_s,
        vec_a,
        vec_b,
        dq_t,
        dk_t,
        dv_t,
        dproj_low,
        dproj_all,
        gq_low,
        gq_f32,
        g1_f32,
        g1_low,
        g1_sib,
        g1_send,
        g1_recv,
        gq_sib,
        gq_send,
        gq_recv,
        gq_all,
        g1t_all,
        g1_nat,
        g2_low,
        gy_recv,
        gy_sum,
        gz_recv,
        gz_sum,
        gx_recv,
        g2_all,
        gout_low,
        go_z,
        go_zs,
        go_x,
        go_xs,
        go_y,
        gout_all,
        gup_all,
        gdown_all,
        sent,
        *part_refs,
    ) = refs[46:-2]
    dp, head = lax.axis_index("dp"), lax.axis_index("head")
    x_hi, y, core = dp // 8, (dp // 2) % 4, dp % 2
    z, x_lo = head // 2, head % 2
    xx = x_hi * 2 + x_lo
    sub = x_hi * 4 + y
    links = Links(sems)

    def head_peer(o):
        return (head + o) % 8

    def in_head(o):
        return (dp, (head + o) % 8)

    def head_from(o):
        return (head + 8 - o) % 8

    def sub_peer(o):
        return (sub + o) % 8

    def in_sub(o):
        return (((sub + o) % 8) * 2 + core, head)

    def ring(axis, o):
        nx = (xx + o) % 4 if axis == "x" else xx
        ny = (y + o) % 4 if axis == "y" else y
        nz = (z + o) % 4 if axis == "z" else z
        return ((nx // 2) * 8 + ny * 2 + core, nz * 2 + nx % 2)

    sibling = (sub * 2 + (1 - core), head)

    barrier = pltpu.get_barrier_semaphore()
    greeted = [in_sub(o) for o in range(7, 0, -1)] + [in_head(o) for o in range(7, 0, -1)]
    greeted += [((1 - x_hi) * 8 + y * 2 + core, z * 2 + 1 - x_lo), sibling]
    for device in greeted:
        pl.semaphore_signal(
            barrier, inc=1, device_id=device, device_id_type=pl.DeviceIdType.MESH
        )

    pairs = [(x_hbm, x_ref)] + [(states[i], kept[i]) for i in (0, 3, 6, 9, 15, 18, 12)]
    pairs += [(dy_hbm, dy_ref)] + [(states[i], kept[i]) for i in range(21) if i % 3]
    loads = [
        pltpu.make_async_copy(src, dst, local_sems.at[i]) for i, (src, dst) in enumerate(pairs)
    ]
    for load in loads[0:9]:
        load.start()

    own = pl.ds(aligned(head * ROWS, ROWS), ROWS)
    own_core = pl.ds(aligned(core * ROWS, ROWS), ROWS)
    sib_core = pl.ds(aligned((1 - core) * ROWS, ROWS), ROWS)
    half = pl.ds(aligned(core * 256, 256), 256)
    sib_half = pl.ds(aligned((1 - core) * 256, 256), 256)
    own_heads = pl.ds(aligned(head * 64, 64), 64)
    own_w = pl.ds(aligned(head * 192, 64), 192)
    sub_rows = pl.ds(aligned(sub * 128, 128), 128)

    def rows_of(ref, first, unit):
        def at(s):
            parts = ((0, unit), (0, unit // 2), (unit // 2, unit // 2))
            return [ref.at[pl.ds(aligned(first(s) + a, unit // 2), n), :] for a, n in parts]

        return at

    def up_at(s):
        cols = pl.ds(aligned(s * 128, 128), 128)
        first = (y % 2) * 256
        parts = ((0, 256), (0, 128), (128, 128))
        return [up_all.at[pl.ds(aligned(first + a, 128), n), cols] for a, n in parts]

    class Spread:
        def __init__(self, at, three, four, seven=None, last=None):
            self.at, self.last, self.one = at, last, at(head)[0]
            self.ring_z = Group(links, three, 3, self.one)
            self.over_x = Group(links, four)
            self.over_last = None if last is None else Group(links, seven)

        def begin(self):
            for o in range(1, 4):
                self.ring_z.send(self.one, self.one, ring("z", o), o - 1)

        def begin_x(self):
            self.forward(head)

        def forward(self, s):
            _, first, second = self.at(s)
            self.over_x.send(first, first, ring("x", 1))
            self.over_x.send(second, second, ring("x", 3))

        def pass_on(self):
            for o in range(1, 4):
                self.ring_z.wait(o - 1)
                s = ((z + 4 - o) % 4) * 2 + x_lo
                self.forward(s)
                if self.last is not None:
                    self.last(self.over_last, *self.at(s))

        def pass_last(self):
            self.over_x.wait()
            for o in range(4):
                self.last(self.over_last, *self.at(((z + o) % 4) * 2 + 1 - x_lo))

    def to_sibling(group, whole, first, second):
        group.send(whole, whole, sibling)

    def to_both_y(group, whole, first, second):
        group.send(first, first, ring("y", 1))
        group.send(second, second, ring("y", 3))

    spread_out = Spread(
        rows_of(out_all, lambda s: s * 64 + core * 32, 32),
        out_all.at[0:96, :],
        out_all.at[0:128, :],
        out_all.at[0:224, :],
        to_sibling,
    )
    spread_up = Spread(
        up_at,
        up_all.at[0:256, 0:384],
        up_all.at[0:256, 0:512],
        up_all.at[0:256, 0:896],
        to_both_y,
    )
    spread_down = Spread(
        rows_of(down_all, lambda s: s * 128 + (y % 2) * 64, 64),
        down_all.at[0:192, :],
        down_all.at[0:256, :],
        down_all.at[0:448, :],
        to_both_y,
    )
    spread_w = Spread(
        rows_of(w_all, lambda s: s * 192 + core * 96, 96),
        w_all.at[0:288, :],
        w_all.at[0:384, :],
        w_all.at[0:672, :],
        to_sibling,
    )
    x_group = Group(links, x_all.at[0 : 7 * ROWS, :], 7, x_ref)

    class Groups:
        pass

    g = Groups()

    beside = (dp, z * 2 + 1 - x_lo)
    gain_one, shift_one = pl.ds(0, 1), pl.ds(0, 1)
    gain_two, shift_two = pl.ds(1, 1), pl.ds(1, 1)

    def project(block):
        for s in range(4):
            rows = pl.ds(aligned(block * ROWS + 32 * s, 32), 32)
            v = x_all[rows, :].astype(F32)
            center = v - jnp.mean(v, axis=-1, keepdims=True)
            spread = jnp.mean(center * center, axis=-1, keepdims=True)
            h = center * lax.rsqrt(spread + NORM_EPS) * gains_ref[gain_one, :] + biases_ref[shift_one, :]
            h1_all[rows, :] = h.astype(BF16)
        rows = pl.ds(aligned(block * ROWS, ROWS), ROWS)
        pt = dot(w_all[own_w, :], h1_all[rows, :], NT)
        proj_t[0:64, rows] = (pt[0:64].astype(BF16).astype(F32) * 0.125).astype(BF16)
        proj_t[64:192, rows] = pt[64:192].astype(BF16)
        k_nat[rows, :] = pt[64:128].T.astype(BF16)
        v_nat[rows, :] = pt[128:192].T.astype(BF16)

    def from_z(o):
        return ((z + 4 - o) % 4) * 2

    place = {"x": xx, "y": y, "z": z}

    class Staged:
        def __init__(self, axes, refs):
            self.axes, self.refs, self.step, self.group = axes, refs, 0, None

        def put(self, ch, value):
            a, b, c = (ch[axis] for axis in self.axes)
            self.refs[0][a * 16 + b * 4 + c] = value

        def send(self):
            axis, size = self.axes[self.step], (16, 4, 1)[self.step]
            src, got = self.refs[2 * self.step : 2 * self.step + 2]
            self.group = Group(links, got)
            for o in range(1, 4):
                t = (place[axis] + o) % 4
                block = got.at[pl.ds((o - 1) * size, size)]
                self.group.send(src.at[pl.ds(t * size, size)], block, ring(axis, o))

        def add(self, store=None):
            at, size = place[self.axes[self.step]], (16, 4, 1)[self.step]
            src, got = self.refs[2 * self.step : 2 * self.step + 2]
            self.group.wait()
            self.step += 1
            to = None if store else self.refs[2 * self.step]

            def some(i, n):
                total = src[pl.ds(at * size + i, n)].astype(F32)
                for o in range(3):
                    total = total + got[pl.ds(o * size + i, n)].astype(F32)
                return total.astype(BF16)

            if store:
                store(some(0, 1)[0])
                return

            def body(i, carry):
                to[pl.ds(i * 4, 4)] = some(i * 4, 4)
                return carry

            lax.fori_loop(0, size // 4, body, 0)

        def next(self):
            self.add()
            self.send()

    up_a, up_b, down_a, down_b = (
        Staged(axes, part_refs[6 * i : 6 * i + 6])
        for i, axes in enumerate(("yzx", "xyz", "yxz", "zxy"))
    )

    def chip_of(h, n):
        return {"x": (n // 4) * 2 + h % 2, "y": n % 4, "z": h // 2}

    def add_slots(ref, n=8):
        total = ref[0].astype(F32)
        for o in range(1, n):
            total = total + ref[o].astype(F32)
        return total

    def block_of(ref, at, rows, cols=slice(None)):
        return ref.at[pl.ds(aligned(at * rows, rows), rows), cols]

    def to_all(group, peers, ref):
        for o in range(1, 4 if peers not in (in_head, in_sub) else 8):
            group.send(ref, ref, peers(o))

    def in_ring(axis):
        return lambda o: ring(axis, o)

    def update(i, grad, first=0, rows=None):
        rows = SHAPES[i][0] if rows is None else rows
        step = 32 if SHAPES[i][1] == D else 64

        def strip(n, carry):
            at = pl.ds(aligned(n * step, step), step)
            into = pl.ds(aligned(first + n * step, step), step)
            refs = kept[3 * i : 3 * i + 3]
            values = adamw(*(r[into, :] for r in refs), grad[at, :].astype(F32), RATES[i])
            for r, value in zip(refs, values):
                r[into, :] = value
            return carry

        lax.fori_loop(0, rows // step, strip, 0, unroll=2)


    def x_out():
        for o in range(1, 4):
            x_group.send(x_ref, x_all.at[own, :], ring("z", o), o - 1)
        x_group.send(x_ref, x_all.at[own, :], beside, 3)

    def cast_weights():
        for load in loads[1:5]:
            load.wait()
        w_all[own_w, :] = kept[0][...].astype(BF16)
        out_all[own_heads, :] = kept[3][...].astype(BF16)
        up_all[:, own] = kept[6][:, own_core].astype(BF16)
        down_all[own, :] = kept[9][own_core, :].astype(BF16)

    def load_rest():
        for load in loads[9:]:
            load.start()
        for load in loads[5:9]:
            load.wait()
        for i in range(2):
            gate_low[i] = kept[12][D * i : D * i + D, :].astype(BF16)
        for n in range(4):
            cols = slice(128 * n, 128 * n + 128)
            gate_t[cols, :] = kept[12][0:D, cols].T.astype(BF16)

    def project_own():
        project(head)

    def x_pass_z():
        x_group.wait(3)
        block = block_of(x_all, z * 2 + 1 - x_lo, ROWS)
        x_group.send(block, block, ring("z", 1), 4)
        x_group.send(block, block, ring("z", 3), 5)

    def project_beside():
        project(z * 2 + 1 - x_lo)

    def from_z(o):
        return ((z + 4 - o) % 4) * 2

    def project_near():
        x_group.wait(0)
        project(from_z(1) + x_lo)
        x_group.wait(2)
        project(from_z(3) + x_lo)

    def x_pass_x():
        x_group.wait(1)
        block = block_of(x_all, from_z(2) + x_lo, ROWS)
        x_group.send(block, block, beside, 6)

    def project_far():
        project(from_z(2) + x_lo)

    def project_passed():
        x_group.wait(4)
        project(from_z(1) + 1 - x_lo)
        x_group.wait(5)
        project(from_z(3) + 1 - x_lo)

    def project_last():
        x_group.wait(6)
        project(from_z(2) + 1 - x_lo)


    def attention():
        for j in range(LEN // QB):
            cols = slice(QB * j, QB * (j + 1))
            queries = proj_t[0:64, cols]
            ceiling = jnp.full((1, QB), -1e30, F32)
            tiles = QB * (j + 1) // ROWS
            for t in range(tiles):
                s = dot(k_nat[ROWS * t : ROWS * (t + 1), :], queries)
                if ROWS * t >= QB * j:
                    keys_at = lax.broadcasted_iota(jnp.int32, (ROWS, QB), 0) + ROWS * t
                    queries_at = lax.broadcasted_iota(jnp.int32, (ROWS, QB), 1) + QB * j
                    s = jnp.where(keys_at <= queries_at, s, -1e30)
                s_buf[ROWS * t : ROWS * (t + 1), :] = s
                ceiling = jnp.maximum(ceiling, jnp.max(s, axis=0, keepdims=True))
            mass = jnp.zeros((1, QB), F32)
            for t in range(tiles):
                e = jnp.exp(s_buf[ROWS * t : ROWS * (t + 1), :] - ceiling)
                mass = mass + jnp.sum(e, axis=0, keepdims=True)
                e_buf[ROWS * t : ROWS * (t + 1), cols] = e.astype(BF16)
            total = dot(proj_t[128:192, 0 : QB * (j + 1)], e_buf[0 : QB * (j + 1), cols])
            total = total / mass
            o_t[:, cols] = total
            o_low[:, cols] = total.astype(BF16)
            inv_mass[:, cols] = 1.0 / mass
        group = g.heads = Group(links, heads_t.at[0:448, 0:ROWS])
        for o in range(1, 8):
            block = o_low.at[:, pl.ds(aligned(head_peer(o) * ROWS, ROWS), ROWS)]
            group.send(block, heads_t.at[own_heads, own_core], in_head(o))
        heads_t[own_heads, own_core] = o_low[:, own]


    def gate_one():
        g1_buf[...] = dot(h1_all[own, :], gate_low[0]) + biases_ref[2:3, :]

    def middle():
        g.heads.wait()
        group = g.heads_pair = Group(links, heads_t.at[:, 0:ROWS])
        group.send(heads_t.at[:, own_core], heads_t.at[:, own_core], sibling)
        spread_out.over_last.wait()
        attn_buf[...] = dot(heads_t[:, own_core], out_all[...], TN)
        for s in range(4):
            rows = slice(32 * s, 32 * s + 32)
            g1 = jax.nn.sigmoid(g1_buf[rows, :])
            g1_buf[rows, :] = g1
            x = x_ref[rows, :].astype(F32)
            x1 = g1 * attn_buf[rows, :] + (1.0 - g1) * x
            x1_buf[rows, :] = x1
            center = x1 - jnp.mean(x1, axis=-1, keepdims=True)
            spread = jnp.mean(center * center, axis=-1, keepdims=True)
            rstd = lax.rsqrt(spread + NORM_EPS)
            xhat = center * rstd
            xhat_buf[rows, :] = xhat
            rstd_buf[rows, :] = jnp.broadcast_to(rstd, (32, 128))
            h2 = xhat * gains_ref[gain_two, :] + biases_ref[shift_two, :]
            h2_pair[pl.ds(aligned(core * ROWS + 32 * s, 32), 32), :] = h2.astype(BF16)
        group = g.h2 = Group(links, h2_pair.at[0:ROWS, :])
        group.send(h2_pair.at[own_core, :], h2_pair.at[own_core, :], sibling)

    def gate_two():
        g2_buf[...] = dot(h2_pair[own_core, :], gate_low[1]) + biases_ref[3:4, :]

    def hidden():
        g.h2.wait()
        spread_up.over_last.wait()
        for n in range(4):
            cols = slice(256 * n, 256 * n + 256)
            u = dot(h2_pair[...], up_all[:, cols])
            c0 = 0.7978845608028654
            inner = jnp.tanh(c0 * (u + 0.044715 * u * u * u))
            act_buf[:, cols] = (0.5 * u * (1.0 + inner)).astype(BF16)
            dgelu_buf[:, cols] = u
            tanh_buf[:, cols] = inner

    def gelu_slope():
        c0 = 0.7978845608028654

        def strip(n, carry):
            rows = pl.ds(aligned(n * 16, 16), 16)
            u, inner = dgelu_buf[rows, :], tanh_buf[rows, :]
            slope = (1.0 - inner * inner) * (c0 + 3.0 * 0.044715 * c0 * u * u)
            dgelu_buf[rows, :] = 0.5 * (1.0 + inner) + 0.5 * u * slope
            return carry

        lax.fori_loop(0, 16, strip, 0)

    def ffn():
        spread_down.over_last.wait()
        ffn_send[...] = dot(act_buf[sib_core, :], down_all[...]).astype(BF16)
        g.ffn = Group(links, ffn_recv)
        g.ffn.send(ffn_send, ffn_recv, sibling)
        ffn_own[...] = dot(act_buf[own_core, :], down_all[...])

    def mix():
        g.ffn.wait()
        bias_two = jnp.zeros((1, D), F32)
        for s in range(4):
            rows = slice(32 * s, 32 * s + 32)
            total = ffn_own[rows, :] + ffn_recv[rows, :].astype(F32)
            g2 = jax.nn.sigmoid(g2_buf[rows, :])
            g2_buf[rows, :] = g2
            x1 = x1_buf[rows, :]
            dy = dy_ref[rows, :].astype(F32)
            mixed_ref[rows, :] = g2 * total + (1.0 - g2) * x1
            dffn_pair[pl.ds(aligned(core * ROWS + 32 * s, 32), 32), :] = (g2 * dy).astype(BF16)
            dz = (dy * (total - x1) * g2 * (1.0 - g2)).astype(BF16)
            dz2_full[rows, :] = dz
            bias_two = bias_two + jnp.sum(dz.astype(F32), axis=0, keepdims=True)
        group = g.dffn = Group(links, dffn_pair.at[0:ROWS, :])
        group.send(dffn_pair.at[own_core, :], dffn_pair.at[own_core, :], sibling)
        group = g.dz2 = Group(links, dz2_half.at[0:ROWS, :])
        group.send(dz2_full.at[:, sib_half], dz2_half.at[own_core, :], sibling)
        dz2_half[own_core, :] = dz2_full[:, half]
        vec[5:6, :] = bias_two
        vec[6:8, :] = jnp.zeros((2, D), F32)


    def back_gate_two():
        dh2_gate[...] = dot(dz2_full[...], gate_low[1], NT)

    def back_hidden():
        g.dffn.wait()
        for n in range(4):
            cols = slice(256 * n, 256 * n + 256)
            da = dot(dffn_pair[...], down_all[cols, :], NT)
            dhid_buf[:, cols] = (da * dgelu_buf[:, cols]).astype(BF16)
        dh2_send[...] = dot(dhid_buf[sib_core, :], up_all[...], NT).astype(BF16)
        g.dh2 = Group(links, dh2_recv)
        g.dh2.send(dh2_send, dh2_recv, sibling)
        dh2_own[...] = dot(dhid_buf[own_core, :], up_all[...], NT)

    def back_middle():
        g.dh2.wait()
        gain_sum = jnp.zeros((1, D), F32)
        shift_sum = jnp.zeros((1, D), F32)
        bias_one = jnp.zeros((1, D), F32)
        for s in range(4):
            rows = slice(32 * s, 32 * s + 32)
            dh2 = dh2_own[rows, :] + dh2_recv[rows, :].astype(F32) + dh2_gate[rows, :]
            xhat = xhat_buf[rows, :]
            gain_sum = gain_sum + jnp.sum(dh2 * xhat, axis=0, keepdims=True)
            shift_sum = shift_sum + jnp.sum(dh2, axis=0, keepdims=True)
            dxhat = dh2 * gains_ref[gain_two, :]
            mean_a = jnp.mean(dxhat, axis=-1, keepdims=True)
            mean_b = jnp.mean(dxhat * xhat, axis=-1, keepdims=True)
            rstd = rstd_buf[rows, 0:1]
            dx1 = (1.0 - g2_buf[rows, :]) * dy_ref[rows, :].astype(F32) + rstd * (
                dxhat - mean_a - xhat * mean_b
            )
            g1 = g1_buf[rows, :]
            dattn_full[rows, :] = (g1 * dx1).astype(BF16)
            x = x_ref[rows, :].astype(F32)
            dz = (dx1 * (attn_buf[rows, :] - x) * g1 * (1.0 - g1)).astype(BF16)
            dz1_full[rows, :] = dz
            bias_one = bias_one + jnp.sum(dz.astype(F32), axis=0, keepdims=True)
            ingrad_ref[rows, :] = (1.0 - g1) * dx1
        dheads_t[...] = dot(out_all[...], dattn_full[...], NT).astype(BF16)
        group = g.back = Group(links, do_t.at[:, 0 : 7 * ROWS])
        for o in range(1, 8):
            group.send(block_of(dheads_t, head_peer(o), 64), do_t.at[:, own], in_head(o))
        do_t[:, own] = dheads_t[own_heads, :]
        group = g.dattn = Group(links, dattn_half.at[0:ROWS, :])
        group.send(dattn_full.at[:, sib_half], dattn_half.at[own_core, :], sibling)
        dattn_half[own_core, :] = dattn_full[:, half]
        vec[1:2, :] = gain_sum
        vec[3:4, :] = shift_sum
        vec[4:5, :] = bias_one

    def back_first():
        dz1_t[...] = dz1_full[...].astype(F32).T.astype(BF16)
        group = g.back_first = Group(links, dz_t.at[:, 0 : 7 * ROWS])
        for o in range(1, 8):
            group.send(block_of(dz1_t, head_peer(o), 64), dz_t.at[:, own], in_head(o))
        dz_t[:, own] = dz1_t[own_heads, :]

    def back_attention():
        g.back.wait()
        dk_t[...] = jnp.zeros_like(dk_t)
        dv_t[...] = jnp.zeros_like(dv_t)
        for j in range(LEN // QB):
            cols = slice(QB * j, QB * (j + 1))
            upto = QB * (j + 1)
            queries = proj_t[0:64, cols]
            grads = do_t[:, cols]
            inverse = inv_mass[:, cols]
            delta = jnp.sum(o_t[:, cols] * grads.astype(F32), axis=0, keepdims=True)
            for t in range(upto // ROWS):
                keys = slice(ROWS * t, ROWS * (t + 1))
                p = e_buf[keys, cols].astype(F32) * inverse
                ds_buf[keys, :] = (p * (dot(v_nat[keys, :], grads) - delta)).astype(BF16)
            dq_t[:, cols] = dot(proj_t[64:128, 0:upto], ds_buf[0:upto, :]) * 0.125
            dk_t[:, 0:upto] += dot(queries, ds_buf[0:upto, :], NT)
            scaled = (grads.astype(F32) * inverse).astype(BF16)
            dv_t[:, 0:upto] += dot(scaled, e_buf[0:upto, cols], NT)
        dproj_low[0:64, :] = dq_t[...].astype(BF16)
        dproj_low[64:128, :] = dk_t[...].astype(BF16)
        dproj_low[128:192, :] = dv_t[...].astype(BF16)
        group = g.dproj = Group(links, dproj_all.at[0 : 7 * 192, :])
        for o in range(1, 8):
            block = dproj_low.at[:, pl.ds(aligned(head_peer(o) * ROWS, ROWS), ROWS)]
            group.send(block, dproj_all.at[own_w, :], in_head(o))
        dproj_all[own_w, :] = dproj_low[:, own]

    def input_grad():
        g.dproj.wait()
        spread_w.over_last.wait()
        dh2_own[...] = dot(dproj_all[...], w_all[...], TN) + dot(
            dz1_full[...], gate_low[0], NT
        )
        for s in range(4):
            rows = slice(32 * s, 32 * s + 32)
            v = x_ref[rows, :].astype(F32)
            center = v - jnp.mean(v, axis=-1, keepdims=True)
            spread = jnp.mean(center * center, axis=-1, keepdims=True)
            rstd = lax.rsqrt(spread + NORM_EPS)
            xhat = center * rstd
            dxhat = dh2_own[rows, :] * gains_ref[gain_one, :]
            mean_a = jnp.mean(dxhat, axis=-1, keepdims=True)
            mean_b = jnp.mean(dxhat * xhat, axis=-1, keepdims=True)
            ingrad_ref[rows, :] += rstd * (dxhat - mean_a - xhat * mean_b)

    def vec_pair():
        gain = jnp.zeros((1, D), F32)
        shift = jnp.zeros((1, D), F32)
        gate_rows = gate_t[own_heads, :]
        for n in range(4):
            rows = slice(64 * n, 64 * n + 64)
            grads = (dproj_low[rows, :] if n < 3 else dz_t[...]).astype(F32)
            sums = jnp.sum(grads, axis=1, keepdims=True)
            weights = w_all[pl.ds(aligned(head * 192 + 64 * n, 64), 64), :] if n < 3 else gate_rows
            weights = weights.astype(F32)
            products = gq_f32[rows, :] if n < 3 else g1_f32[...]
            moved = products - biases_ref[shift_one, :] * sums
            gain = gain + jnp.sum(weights * moved, axis=0, keepdims=True)
            shift = shift + jnp.sum(weights * sums, axis=0, keepdims=True)
        vec[0:1, :] = gain / gains_ref[gain_one, :]
        vec[2:3, :] = shift
        g.vec_pair = Group(links, vec_s)
        g.vec_pair.send(vec, vec_s, sibling)

    def vec_sub():
        g.vec_pair.wait()
        vec_a[sub] = vec[...] + vec_s[...]
        g.vec_sub = Group(links, vec_a.at[0:7])
        to_all(g.vec_sub, in_sub, vec_a.at[sub])

    def vec_head():
        g.vec_sub.wait()
        vec_b[head] = add_slots(vec_a)
        g.vec_head = Group(links, vec_b.at[0:7])
        to_all(g.vec_head, in_head, vec_b.at[head])

    def vec_done():
        g.vec_head.wait()
        total = add_slots(vec_b)
        for i, grad in ((5, total[0:2]), (6, total[2:6])):
            refs = kept[3 * i : 3 * i + 3]
            for r, value in zip(refs, adamw(*(r[...] for r in refs), grad, RATES[i])):
                r[...] = value


    def grad_down():
        for h in range(8):
            gd = dot(act_buf[:, 128 * h : 128 * h + 128], dffn_pair[...], TN).astype(BF16)
            for n in range(8):
                down_a.put(chip_of(h, n), gd[16 * n : 16 * n + 16, 0:256])
                down_b.put(chip_of(h, n), gd[16 * n : 16 * n + 16, 256:512])

    def grad_up():
        for h in range(8):
            gu = dot(h2_pair[...], dhid_buf[:, 128 * h : 128 * h + 128], TN).astype(BF16)
            for n in range(8):
                up_a.put(chip_of(h, n), gu[64 * n : 64 * n + 32, :])
                up_b.put(chip_of(h, n), gu[64 * n + 32 : 64 * n + 64, :])

    def down_sub():
        rows = pl.ds(aligned(core * 128 + sub * 16, 16), 16)
        for part, cols in ((down_a, slice(0, 256)), (down_b, slice(256, 512))):

            def store(value, cols=cols):
                gdown_all[rows, cols] = value

            part.add(store)
        g.down_sub = Group(links, gdown_all.at[0:112, :])
        to_all(g.down_sub, in_sub, gdown_all.at[rows, :])

    def down_pair():
        g.down_sub.wait()
        group = g.down_pair = Group(links, gdown_all.at[0:128, :])
        group.send(gdown_all.at[own_core, :], gdown_all.at[own_core, :], sibling)

    def down_done():
        g.down_pair.wait()
        update(3, gdown_all)

    def up_sub():
        for part, first in ((up_a, 0), (up_b, 32)):

            def store(value, first=first):
                gup_all[pl.ds(aligned(sub * 64 + first, 32), 32), own_core] = value

            part.add(store)
        block = block_of(gup_all, sub, 64, own_core)
        g.up_sub = Group(links, gup_all.at[0:448, 0:128])
        to_all(g.up_sub, in_sub, block)

    def up_pair():
        g.up_sub.wait()
        group = g.up_pair = Group(links, gup_all.at[:, 0:128])
        group.send(gup_all.at[:, own_core], gup_all.at[:, own_core], sibling)

    def up_done():
        g.up_pair.wait()
        update(2, gup_all)


    def second_y():
        g.dz2.wait()
        g2_low[...] = dot(h2_pair[...], dz2_half[...], TN).astype(BF16)
        group = g.second_y = Group(links, gy_recv.at[0:3])
        for o in range(1, 4):
            group.send(block_of(g2_low, (y + o) % 4, 128), gy_recv.at[y], ring("y", o))
        gy_recv[y] = g2_low[pl.ds(aligned(y * 128, 128), 128), :]

    def second_z():
        g.second_y.wait()
        gy_sum[...] = add_slots(gy_recv, 4).astype(BF16)
        group = g.second_z = Group(links, gz_recv.at[0:3])
        for o in range(1, 4):
            group.send(block_of(gy_sum, (z + o) % 4, 32), gz_recv.at[z], ring("z", o))
        gz_recv[z] = gy_sum[pl.ds(aligned(z * 32, 32), 32), :]

    def second_x():
        g.second_z.wait()
        gz_sum[...] = add_slots(gz_recv, 4).astype(BF16)
        group = g.second_x = Group(links, gx_recv.at[0:3])
        for o in range(1, 4):
            group.send(gz_sum, gx_recv.at[xx], ring("x", o))
        gx_recv[xx] = gz_sum[...]

    def second_back_z():
        g.second_x.wait()
        rows = pl.ds(aligned(y * 128 + z * 32, 32), 32)
        g2_all[rows, half] = add_slots(gx_recv, 4).astype(BF16)
        g.second_back_z = Group(links, gz_recv.at[0:3])
        to_all(g.second_back_z, in_ring("z"), g2_all.at[rows, half])

    def second_back_y():
        g.second_back_z.wait()
        block = block_of(g2_all, y, 128, half)
        g.second_back_y = Group(links, gy_recv.at[0:3])
        to_all(g.second_back_y, in_ring("y"), block)

    def second_pair():
        g.second_back_y.wait()
        group = g.second_pair = Group(links, g2_low)
        group.send(g2_all.at[:, half], g2_all.at[:, half], sibling)

    def second_done():
        g.second_pair.wait()
        update(4, g2_all, D, D)


    def grad_out_z():
        g.heads_pair.wait()
        g.dattn.wait()
        gout_low[...] = dot(heads_t[...], dattn_half[...]).astype(BF16)
        group = g.grad_out_z = Group(links, go_z.at[0:3])
        for o in range(1, 4):
            group.send(block_of(gout_low, (z + o) % 4, 128), go_z.at[z], ring("z", o))
        go_z[z] = gout_low[pl.ds(aligned(z * 128, 128), 128), :]

    def grad_out_x():
        g.grad_out_z.wait()
        go_zs[...] = add_slots(go_z, 4).astype(BF16)
        group = g.grad_out_x = Group(links, go_x.at[0:3])
        for o in range(1, 4):
            to = (xx + o) % 4
            block = block_of(go_zs, (to % 2) * 2 + to // 2, 32)
            group.send(block, go_x.at[xx], ring("x", o))
        go_x[xx] = go_zs[pl.ds(aligned((x_lo * 2 + x_hi) * 32, 32), 32), :]

    def grad_out_y():
        g.grad_out_x.wait()
        go_xs[...] = add_slots(go_x, 4).astype(BF16)
        group = g.grad_out_y = Group(links, go_y.at[0:3])
        for o in range(1, 4):
            group.send(go_xs, go_y.at[y], ring("y", o))
        go_y[y] = go_xs[...]

    def grad_out_far():
        g.grad_out_y.wait()
        rows = pl.ds(aligned(x_hi * 32, 32), 32)
        gout_all[rows, half] = add_slots(go_y, 4).astype(BF16)
        group = g.grad_out_far = Group(links, go_xs)
        group.send(gout_all.at[rows, half], gout_all.at[rows, half], ring("x", 2))

    def grad_out_pair():
        g.grad_out_far.wait()
        group = g.grad_out_pair = Group(links, go_zs.at[0:64, :])
        group.send(gout_all.at[:, half], gout_all.at[:, half], sibling)

    def grad_out_done():
        g.grad_out_pair.wait()
        update(1, gout_all)


    def qkv_pair():
        gq_f32[...] = dot(dproj_low[...], h1_all[...])
        gq_low[...] = gq_f32[...].astype(BF16)
        g.qkv_pair = Group(links, gq_sib)
        g.qkv_pair.send(gq_low.at[:, sib_half], gq_sib, sibling)

    def qkv_sub():
        g.qkv_pair.wait()
        total = gq_low[:, half].astype(F32) + gq_sib[...].astype(F32)
        for i in range(8):
            r, c = 48 * (i // 2), 128 * (i % 2)
            gq_send[i] = total[r : r + 48, c : c + 128].astype(BF16)
        group = g.qkv_sub = Group(links, gq_recv.at[0:7])
        for o in range(1, 8):
            group.send(gq_send.at[sub_peer(o)], gq_recv.at[sub], in_sub(o))
        gq_recv[sub] = gq_send[sub]

    def qkv_back():
        g.qkv_sub.wait()
        rows = pl.ds(aligned((sub // 2) * 48, 48), 48)
        cols = pl.ds(aligned(core * 256 + (sub % 2) * 128, 128), 128)
        gq_all[rows, cols] = add_slots(gq_recv).astype(BF16)
        g.qkv_back = Group(links, gq_recv.at[0:7])
        to_all(g.qkv_back, in_sub, gq_all.at[rows, cols])


    def first_start():
        g.back_first.wait()
        g1_f32[...] = dot(dz_t[...], h1_all[...])
        g1_low[...] = g1_f32[...].astype(BF16)
        g.first_start = Group(links, g1_sib)
        g.first_start.send(g1_low.at[:, sib_half], g1_sib, sibling)

    def first_sub():
        g.first_start.wait()
        total = g1_low[:, half].astype(F32) + g1_sib[...].astype(F32)
        for i in range(8):
            r, c = 16 * (i // 2), 128 * (i % 2)
            g1_send[i] = total[r : r + 16, c : c + 128].astype(BF16)
        group = g.first_sub = Group(links, g1_recv.at[0:7])
        for o in range(1, 8):
            group.send(g1_send.at[sub_peer(o)], g1_recv.at[sub], in_sub(o))
        g1_recv[sub] = g1_send[sub]

    def first_back():
        g.first_sub.wait()
        rows = pl.ds(aligned(head * 64 + (sub // 2) * 16, 16), 16)
        cols = pl.ds(aligned(core * 256 + (sub % 2) * 128, 128), 128)
        g1t_all[rows, cols] = add_slots(g1_recv).astype(BF16)
        g.first_back = Group(links, g1_recv.at[0:7])
        to_all(g.first_back, in_sub, g1t_all.at[rows, cols])

    def first_head():
        g.first_back.wait()
        g.first_head = Group(links, g1t_all.at[0:448, 0:256])
        to_all(g.first_head, in_head, g1t_all.at[own_heads, half])

    def qkv_back_pair():
        g.qkv_back.wait()
        g.qkv_back_pair = Group(links, gq_sib)
        g.qkv_back_pair.send(gq_all.at[:, half], gq_all.at[:, half], sibling)

    def qkv_done():
        g.qkv_back_pair.wait()
        update(0, gq_all)

    def first_pair():
        g.first_head.wait()
        group = g.first_pair = Group(links, g2_low)
        group.send(g1t_all.at[:, half], g1t_all.at[:, half], sibling)
        g1_nat[half, :] = g1t_all[:, half].astype(F32).T
        update(4, g1_nat.at[half, :], core * 256, 256)

    def first_done():
        g.first_pair.wait()
        g1_nat[sib_half, :] = g1t_all[:, sib_half].astype(F32).T
        update(4, g1_nat.at[sib_half, :], (1 - core) * 256, 256)

    def moments():
        for load in loads[9:]:
            load.wait()

    loads[0].wait()
    x_all[own, :] = x_ref[...]
    pl.semaphore_wait(barrier, len(greeted))
    for run in (
        x_out,
        cast_weights,
        spread_up.begin_x,
        x_pass_z,
        spread_up.begin,
        load_rest,
        spread_down.begin,
        x_pass_x,
        project_beside,
        project_own,
        spread_out.begin_x,
        project_far,
        spread_out.begin,
        spread_down.begin_x,
        project_passed,
        project_near,
        project_last,
        spread_up.pass_on,
        attention,
        spread_down.pass_on,
        spread_out.pass_on,
        spread_up.pass_last,
        spread_w.begin,
        spread_down.pass_last,
        spread_w.begin_x,
        spread_out.pass_last,
        gate_one,
        middle,
        hidden,
        ffn,
        gelu_slope,
        spread_w.pass_on,
        gate_two,
        mix,
        back_gate_two,
        back_hidden,
        second_y,
        back_middle,
        back_first,
        grad_down,
        down_a.send,
        grad_up,
        up_a.send,
        up_b.send,
        grad_out_z,
        second_z,
        first_start,
        down_b.send,
        first_sub,
        down_a.next,
        grad_out_x,
        second_x,
        back_attention,
        up_a.next,
        qkv_pair,
        first_back,
        grad_out_y,
        down_b.next,
        up_b.next,
        qkv_sub,
        vec_pair,
        spread_w.pass_last,
        second_back_z,
        grad_out_far,
        vec_sub,
        up_b.next,
        down_a.next,
        up_a.next,
        down_b.next,
        first_head,
        second_back_y,
        input_grad,
        qkv_back,
        up_sub,
        grad_out_pair,
        down_sub,
        moments,
        grad_out_done,
        vec_head,
        second_pair,
        first_pair,
        second_done,
        qkv_back_pair,
        first_done,
        up_pair,
        down_pair,
        qkv_done,
        vec_done,
        up_done,
        down_done,
    ):
        run()
    links.drain(sent)


VMEM = pl.BlockSpec(memory_space=pltpu.VMEM)
ANY = pl.BlockSpec(memory_space=pl.ANY)
HBM = pl.BlockSpec(memory_space=pltpu.HBM)


def run_layer(*args):
    in_vmem = [pltpu.VMEM(s, F32) for s in SHAPES for _ in range(3)]
    shapes = [pltpu.VMEM((ROWS, D), F32)] * 2
    return pl.pallas_call(
        layer_kernel,
        out_shape=shapes + in_vmem,
        in_specs=[HBM] * 23,
        out_specs=[VMEM] * 23,
        scratch_shapes=[pltpu.VMEM(s, t) for s, t in SCRATCH]
        + [pltpu.SemaphoreType.DMA((N_SEMS,)), pltpu.SemaphoreType.DMA((N_LOCAL,))],
        compiler_params=pltpu.CompilerParams(
            collective_id=0, has_side_effects=True, vmem_limit_bytes=44 * 1024 * 1024
        ),
        name="layer",
    )(*args)


def finish_kernel(*refs):
    sems = refs[46]
    copies = [
        pltpu.make_async_copy(refs[i], refs[23 + i], sems.at[i]) for i in range(23)
    ]
    for c in copies:
        c.start()
    for c in copies:
        c.wait()


def finish(results):
    return pl.pallas_call(
        finish_kernel,
        out_shape=[jax.ShapeDtypeStruct(a.shape, F32) for a in results],
        in_specs=[ANY] * 23,
        out_specs=[ANY] * 23,
        scratch_shapes=[pltpu.SemaphoreType.DMA((23,))],
        compiler_params=pltpu.CompilerParams(vmem_limit_bytes=1024 * 1024),
        name="finish",
    )(*results)


def local(inputs, cotangent, *state):
    rows = inputs.shape[1]
    flat = list(state)
    for i in (0, 1, 2):
        flat[i] = jnp.transpose(flat[i], (0, 2, 1)).reshape(192, D)
    for i in (12, 13, 14):
        flat[i] = flat[i].reshape(2 * D, D)
    operands = (inputs.reshape(rows, D), cotangent.reshape(rows, D), *flat)
    results = run_layer(*(pltpu.with_memory_space_constraint(a, pltpu.HBM) for a in operands))
    mixed, ingrad, *new = finish(results)
    for i in (0, 1, 2):
        new[i] = jnp.transpose(new[i].reshape(3, 64, D), (0, 2, 1))
    for i in (12, 13, 14):
        new[i] = new[i].reshape(2, D, D)
    return (mixed.reshape(1, rows, D), ingrad.reshape(1, rows, D), *new)


def solution(mesh):
    batch = P("dp", "head", None)
    qkv = P(None, None, "head")
    first = P("head", None)
    second = P(None, "head")
    state = (qkv,) * 3 + (first,) * 3 + (second,) * 3 + (first,) * 3 + (P(),) * 9
    return jax.shard_map(
        local,
        mesh=mesh,
        in_specs=(batch, batch, *state),
        out_specs=(batch, batch, *state),
        check_vma=False,
    )
```
